32 devices in a mesh: dp: 16 (over z, x, core), tensor: 2 (over y).
Axes of the slice: x: 2, y: 2, z: 4, core: 2. Of those that a mesh axis runs over, the one named last changes fastest.
Arguments:
- residual: float32 [4096, 1024], P(('dp', 'tensor')), may hold values from -6 to 6
- out_grad: float32 [4096, 1024], P(('dp', 'tensor')), may hold values from -6 to 6
- doc_lengths: int32 [16, 4], P('dp'), may hold values from 0 to 256, as said below
- mixer_weight: float32 [1024, 3840], P('dp', 'tensor'), may hold values from -0.1875 to 0.1875
- mixer_first: float32 [1024, 3840], P('dp', 'tensor'), may hold values from -40 to 40
- mixer_second: float32 [1024, 3840], P('dp', 'tensor'), may hold values from 102.4 to 1638.4
- scan_weight: float32 [1024, 280], P('dp'), may hold values from -0.1875 to 0.1875
- scan_first: float32 [1024, 280], P('dp'), may hold values from -40 to 40
- scan_second: float32 [1024, 280], P('dp'), may hold values from 102.4 to 1638.4
- merge_weight: float32 [2048, 1024], P('tensor', 'dp'), may hold values from -0.25 to 0.25
- merge_first: float32 [2048, 1024], P('tensor', 'dp'), may hold values from -40 to 40
- merge_second: float32 [2048, 1024], P('tensor', 'dp'), may hold values from 102.4 to 1638.4
- hidden_weight: float32 [1024, 4096], P('dp', 'tensor'), may hold values from -0.1875 to 0.1875
- hidden_first: float32 [1024, 4096], P('dp', 'tensor'), may hold values from -40 to 40
- hidden_second: float32 [1024, 4096], P('dp', 'tensor'), may hold values from 102.4 to 1638.4
- down_weight: float32 [2048, 1024], P('tensor', 'dp'), may hold values from -0.125 to 0.125
- down_first: float32 [2048, 1024], P('tensor', 'dp'), may hold values from -40 to 40
- down_second: float32 [2048, 1024], P('tensor', 'dp'), may hold values from 102.4 to 1638.4
- head_params: float32 [24, 323], P('tensor'), may hold values from -4 to 1.5, as said below
- head_first: float32 [24, 323], P('tensor'), may hold values from -40 to 40
- head_second: float32 [24, 323], P('tensor'), may hold values from 102.4 to 1638.4
- shared_params: float32 [3328], replicated, may hold values from -1.5 to 1.5, as said below
- shared_first: float32 [3328], replicated, may hold values from -40 to 40
- shared_second: float32 [3328], replicated, may hold values from 102.4 to 1638.4
Outputs:
- block_out: float32 [4096, 1024], P(('dp', 'tensor'))
- input_grad: float32 [4096, 1024], P(('dp', 'tensor'))
- mixer_momentum: float32 [1024, 3840], P('dp', 'tensor')
- mixer_squares: float32 [1024, 3840], P('dp', 'tensor')
- mixer_updated: float32 [1024, 3840], P('dp', 'tensor')
- scan_momentum: float32 [1024, 280], P('dp')
- scan_squares: float32 [1024, 280], P('dp')
- scan_updated: float32 [1024, 280], P('dp')
- merge_momentum: float32 [2048, 1024], P('tensor', 'dp')
- merge_squares: float32 [2048, 1024], P('tensor', 'dp')
- merge_updated: float32 [2048, 1024], P('tensor', 'dp')
- hidden_momentum: float32 [1024, 4096], P('dp', 'tensor')
- hidden_squares: float32 [1024, 4096], P('dp', 'tensor')
- hidden_updated: float32 [1024, 4096], P('dp', 'tensor')
- down_momentum: float32 [2048, 1024], P('tensor', 'dp')
- down_squares: float32 [2048, 1024], P('tensor', 'dp')
- down_updated: float32 [2048, 1024], P('tensor', 'dp')
- head_momentum: float32 [24, 323], P('tensor')
- head_squares: float32 [24, 323], P('tensor')
- head_updated: float32 [24, 323], P('tensor')
- shared_momentum: float32 [3328], replicated
- shared_squares: float32 [3328], replicated
- shared_updated: float32 [3328], replicated
The draws below stay inside these ranges and needn't reach their ends.
Inputs may be any that keep to these rules, and one draw needn't show every extreme that they name: `doc_lengths`: each row lists the lengths of the documents of one group in order and sums to 256; zeros are empty slots. The first document of each row is longer than half of 256; one row holds a single document of 256 tokens. `head_params`: columns below 256: convolution taps; next 64: biases; then a_log, skip, dt_bias. `shared_params`: gains first, then taps, then biases.
All inputs are finite; a program needn't handle non-finite values.
Results may differ from the reference program's by a relative error of at most 0.012.
The reference program's roundings to bfloat16 on the way count: a program that leaves them out, or rounds other values in their place, can miss the bound.
Values may be sent and summed in bfloat16 or wider, within the bound.
No kernel may reach another device: no remote copies, remote signals or barrier semaphores. Data moves between devices by JAX's collectives and lax.ppermute only.
A program may use at most 128 MiB of HBM per device.

```python
import math
import jax
import jax.numpy as jnp
from jax import lax

D = 1024
FF = 2048
HEADS_M = 24
HEAD_M = 64
STATE = 128
CONV = 4
HEADS_Q = 8
HEADS_KV = 2
HEAD_A = 64
MAXDOCS = 4
STEP = 10
GRP_TOK = 256
TOKENS = 4096
IN_TP = 1920
OUT_TP = 1024
SEQ_W = 280
HEAD_COLS = 323
SMALL_REP = 3328
N_DP = 16
N_TENSOR = 2


def draw_doc_lengths(key, part):
    key = jax.random.fold_in(key, 1)
    key_first, key_cuts, key_whole = jax.random.split(key, 3)
    first = GRP_TOK // 2 + GRP_TOK // 8 + jax.random.randint(key_first, (N_DP,), 0, GRP_TOK // 4 + 1)
    rest = GRP_TOK - first
    cuts = jax.random.randint(key_cuts, (N_DP, MAXDOCS - 2), 0, 1 << 20) % (rest[:, None] + 1)
    cuts = jnp.sort(cuts, axis=1)
    edges = jnp.concatenate([jnp.zeros((N_DP, 1), jnp.int32), cuts.astype(jnp.int32), rest[:, None].astype(jnp.int32)], axis=1)
    pieces = edges[:, 1:] - edges[:, :-1]
    lengths = jnp.concatenate([first[:, None].astype(jnp.int32), pieces], axis=1)
    whole_row = jax.random.randint(key_whole, (), 0, N_DP)
    single = jnp.where(jnp.arange(MAXDOCS) == 0, GRP_TOK, 0).astype(jnp.int32)
    chosen = jnp.arange(N_DP)[:, None] == whole_row
    return jnp.where(chosen, single[None, :], lengths).astype(jnp.int32)


def draw_head_params(key, part):
    key = jax.random.fold_in(key, 2)
    keys = jax.random.split(key, 5)
    shape = (HEADS_M, (CONV + 1) * HEAD_M + 3)
    column = jnp.arange(shape[1])[None, :] + jnp.zeros(shape, jnp.int32)
    taps = jnp.clip(0.5 * jax.random.normal(keys[0], shape), -1.5, 1.5)
    bias = jnp.clip(0.2 * jax.random.normal(keys[1], shape), -0.6, 0.6)
    a_log = jax.random.uniform(keys[2], shape, minval=-3.9, maxval=0.7)
    skip = jax.random.uniform(keys[3], shape, minval=0.5, maxval=1.5)
    dt_bias = jax.random.uniform(keys[4], shape, minval=-4.0, maxval=-2.0)
    base = (CONV + 1) * HEAD_M
    values = jnp.where(column < CONV * HEAD_M, taps, bias)
    values = jnp.where(column == base, a_log, values)
    values = jnp.where(column == base + 1, skip, values)
    values = jnp.where(column == base + 2, dt_bias, values)
    return values.astype(jnp.float32)


def draw_shared_params(key, part):
    key = jax.random.fold_in(key, 3)
    keys = jax.random.split(key, 3)
    total = 2 * D + (CONV + 1) * 2 * STATE
    index = jnp.arange(total)
    gains = 1.0 + jax.random.uniform(keys[0], (total,), minval=-0.15, maxval=0.15)
    taps = jnp.clip(0.5 * jax.random.normal(keys[1], (total,)), -1.5, 1.5)
    bias = jnp.clip(0.2 * jax.random.normal(keys[2], (total,)), -0.6, 0.6)
    values = jnp.where(index < 2 * D, gains, jnp.where(index < 2 * D + CONV * 2 * STATE, taps, bias))
    return values.astype(jnp.float32)


def steps_of(own_key, dims, shards, least, top_value):
    def one(dim, parts):
        heights = jax.random.uniform(jax.random.fold_in(jax.random.fold_in(own_key, 6), dim), (parts,), jnp.float32, least / len(shards), top_value / len(shards))
        return jnp.repeat(jnp.exp(heights), dims[dim] // parts).reshape((-1,) + (1,) * (len(dims) - dim - 1))

    level = one(*shards[0])
    for cut in shards[1:]:
        level = level * one(*cut)
    return level


def gaussian(own_key, shape, deviation, most, cuts=(), held_as=jnp.bfloat16):
    loudness = steps_of(own_key, shape, cuts, -0.22, 0.18) if cuts else 1.0
    drawn = jax.random.normal(own_key, shape, jnp.float32) * deviation * loudness
    return jnp.minimum(jnp.maximum(drawn, -most), most).astype(held_as)


def setup_inputs(seed: int = 0) -> dict:
    streams_of = jax.random.split(jax.random.key(seed), 25)
    return {
        "residual": gaussian(streams_of[0], (TOKENS, D), 1.0, 6.0, ((0, 32),), jnp.float32),
        "out_grad": gaussian(streams_of[1], (TOKENS, D), 1.0, 6.0, ((0, 32),), jnp.float32),
        "doc_lengths": draw_doc_lengths(jax.random.fold_in(streams_of[24], 71), 0),
        "mixer_weight": gaussian(streams_of[3], (D, N_TENSOR * IN_TP), D ** -0.5, 0.1875, ((0, 16), (1, 2)), jnp.float32),
        "mixer_first": gaussian(streams_of[4], (D, N_TENSOR * IN_TP), (0.11 * TOKENS ** 0.5), 40.0, ((0, 16), (1, 2)), jnp.float32),
        "mixer_second": jnp.clip(jnp.exp(math.log(1638.4) - 2.7725887 * jax.random.uniform(streams_of[5], (D, N_TENSOR * IN_TP), jnp.float32) ** steps_of(streams_of[5], (D, N_TENSOR * IN_TP), ((0, 16), (1, 2)), -0.2, 0.2)), 102.4, 1638.4),
        "scan_weight": gaussian(streams_of[6], (D, SEQ_W), D ** -0.5, 0.1875, ((0, 16),), jnp.float32),
        "scan_first": gaussian(streams_of[7], (D, SEQ_W), (0.11 * TOKENS ** 0.5), 40.0, ((0, 16),), jnp.float32),
        "scan_second": jnp.clip(jnp.exp(math.log(1638.4) - 2.7725887 * jax.random.uniform(streams_of[8], (D, SEQ_W), jnp.float32) ** steps_of(streams_of[8], (D, SEQ_W), ((0, 16),), -0.2, 0.2)), 102.4, 1638.4),
        "merge_weight": gaussian(streams_of[9], (N_TENSOR * OUT_TP, D), (D // 2) ** -0.5, 0.25, ((0, 2), (1, 16)), jnp.float32),
        "merge_first": gaussian(streams_of[10], (N_TENSOR * OUT_TP, D), (0.11 * TOKENS ** 0.5), 40.0, ((0, 2), (1, 16)), jnp.float32),
        "merge_second": jnp.clip(jnp.exp(math.log(1638.4) - 2.7725887 * jax.random.uniform(streams_of[11], (N_TENSOR * OUT_TP, D), jnp.float32) ** steps_of(streams_of[11], (N_TENSOR * OUT_TP, D), ((0, 2), (1, 16)), -0.2, 0.2)), 102.4, 1638.4),
        "hidden_weight": gaussian(streams_of[12], (D, 2 * FF), D ** -0.5, 0.1875, ((0, 16), (1, 2)), jnp.float32),
        "hidden_first": gaussian(streams_of[13], (D, 2 * FF), (0.11 * TOKENS ** 0.5), 40.0, ((0, 16), (1, 2)), jnp.float32),
        "hidden_second": jnp.clip(jnp.exp(math.log(1638.4) - 2.7725887 * jax.random.uniform(streams_of[14], (D, 2 * FF), jnp.float32) ** steps_of(streams_of[14], (D, 2 * FF), ((0, 16), (1, 2)), -0.2, 0.2)), 102.4, 1638.4),
        "down_weight": gaussian(streams_of[15], (FF, D), FF ** -0.5, 0.125, ((0, 2), (1, 16)), jnp.float32),
        "down_first": gaussian(streams_of[16], (FF, D), (0.11 * TOKENS ** 0.5), 40.0, ((0, 2), (1, 16)), jnp.float32),
        "down_second": jnp.clip(jnp.exp(math.log(1638.4) - 2.7725887 * jax.random.uniform(streams_of[17], (FF, D), jnp.float32) ** steps_of(streams_of[17], (FF, D), ((0, 2), (1, 16)), -0.2, 0.2)), 102.4, 1638.4),
        "head_params": draw_head_params(jax.random.fold_in(streams_of[24], 71), 0),
        "head_first": gaussian(streams_of[19], (HEADS_M, HEAD_COLS), (0.11 * TOKENS ** 0.5), 40.0, ((0, 2),), jnp.float32),
        "head_second": jnp.clip(jnp.exp(math.log(1638.4) - 2.7725887 * jax.random.uniform(streams_of[20], (HEADS_M, HEAD_COLS), jnp.float32) ** steps_of(streams_of[20], (HEADS_M, HEAD_COLS), ((0, 2),), -0.2, 0.2)), 102.4, 1638.4),
        "shared_params": draw_shared_params(jax.random.fold_in(streams_of[24], 71), 0),
        "shared_first": gaussian(streams_of[22], (SMALL_REP,), (0.11 * TOKENS ** 0.5), 40.0, (), jnp.float32),
        "shared_second": jnp.clip(jnp.exp(jax.random.uniform(streams_of[23], (SMALL_REP,), jnp.float32, math.log(102.4), math.log(1638.4))), 102.4, 1638.4),
    }


EPS = 1e-05
THETA = 10000.0
HIGH = lax.Precision.HIGHEST

@jax.custom_vjp
def low(v):
    return lax.optimization_barrier(v.astype(jnp.bfloat16)).astype(jnp.float32)

@jax.custom_vjp
def low_back(v):
    return v

def low_keep(v):
    return (low(v), None)

def low_pass(kept, grad):
    return (grad,)

def back_keep(v):
    return (v, None)

def back_low(kept, grad):
    return (low(grad),)
low.defvjp(low_keep, low_pass)
low_back.defvjp(back_keep, back_low)

def product(left, right):
    return jnp.dot(left, right, precision=HIGH, preferred_element_type=jnp.float32)

def scaled_norm(values, gain):
    return values * lax.rsqrt(lax.optimization_barrier(jnp.mean(values * values, axis=-1, keepdims=True)) + EPS) * gain

def doc_index(lens, count):
    place = jnp.arange(count, dtype=jnp.int32)
    ends = jnp.cumsum(lens).astype(jnp.int32)
    after = place[:, None] >= ends[None, :]
    seg = lax.optimization_barrier(jnp.sum(after.astype(jnp.int32), axis=1)).astype(jnp.int32)
    start = lax.optimization_barrier(jnp.sum(jnp.where(after, lens[None, :], 0), axis=1)).astype(jnp.int32)
    return (seg, place - start)

def causal_conv(values, taps, bias, seg):
    length = values.shape[0]
    total = bias[None, :] + taps[CONV - 1][None, :] * values
    for shift in range(1, CONV):
        moved = jnp.pad(values, ((shift, 0), (0, 0)))[:length]
        keep = jnp.pad(seg, (shift, 0), constant_values=-1)[:length] == seg
        total = total + taps[CONV - 1 - shift][None, :] * jnp.where(keep[:, None], moved, 0.0)
    return total

def rotate(values, pos):
    half = HEAD_A // 2
    freq = THETA ** (-jnp.arange(half, dtype=jnp.float32) * 2.0 / HEAD_A)
    angle = pos.astype(jnp.float32)[:, None] * freq[None, :]
    cosine = jnp.cos(angle)[:, None, :]
    sine = jnp.sin(angle)[:, None, :]
    first = values[..., :half]
    second = values[..., half:]
    return jnp.concatenate([first * cosine - second * sine, second * cosine + first * sine], axis=-1)

def mixer(pmat, scan, heads, conv_shared, seg, pos, tpos):
    length = pmat.shape[0]
    count = heads.shape[0]
    width = count * HEAD_M
    qheads = HEADS_Q * count // HEADS_M
    kheads = HEADS_KV * count // HEADS_M
    gates = pmat[:, :width]
    chans = pmat[:, width:2 * width]
    qpart = pmat[:, 2 * width:2 * width + qheads * HEAD_A]
    kpart = pmat[:, 2 * width + qheads * HEAD_A:2 * width + (qheads + kheads) * HEAD_A]
    vpart = pmat[:, 2 * width + (qheads + kheads) * HEAD_A:2 * width + (qheads + 2 * kheads) * HEAD_A]
    taps = jnp.stack([heads[:, k * HEAD_M:(k + 1) * HEAD_M].reshape(-1) for k in range(CONV)])
    bias = heads[:, CONV * HEAD_M:(CONV + 1) * HEAD_M].reshape(-1)
    conv_chans = jax.nn.silu(causal_conv(chans, taps, bias, seg))
    states = jax.nn.silu(causal_conv(scan[:, :2 * STATE], conv_shared[:CONV], conv_shared[CONV], seg))
    in_state = states[:, :STATE]
    out_state = states[:, STATE:]
    base = (CONV + 1) * HEAD_M
    rates = jnp.exp(heads[:, base])
    skip = heads[:, base + 1]
    dt_bias = heads[:, base + 2]
    step_raw = lax.dynamic_slice_in_dim(scan, 2 * STATE + tpos * count, count, 1)
    steps = jax.nn.softplus(step_raw + dt_bias[None, :])
    cum = jnp.cumsum(-rates[None, :] * steps, axis=0)
    place = jnp.arange(length, dtype=jnp.int32)
    same = (seg[:, None] == seg[None, :]) & (place[:, None] >= place[None, :])
    gap = cum.T[:, :, None] - cum.T[:, None, :]
    decay = jnp.where(same[None], jnp.exp(jnp.where(same[None], gap, 0.0)), 0.0)
    inner = jnp.dot(out_state, in_state.T, precision=HIGH)
    heads_x = conv_chans.reshape(length, count, HEAD_M)
    weighted = heads_x * steps[:, :, None]
    outputs = jnp.einsum('hts,shp->thp', decay * inner[None], weighted, precision=HIGH)
    outputs = outputs + skip[None, :, None] * heads_x
    outputs = outputs * jax.nn.silu(gates.reshape(length, count, HEAD_M))
    query = rotate(qpart.reshape(length, qheads, HEAD_A), pos).reshape(length, kheads, qheads // kheads, HEAD_A)
    keys = rotate(kpart.reshape(length, kheads, HEAD_A), pos)
    vals = vpart.reshape(length, kheads, HEAD_A)
    scores = jnp.einsum('tkgd,skd->kgts', query, keys, precision=HIGH) * HEAD_A ** (-0.5)
    scores = jnp.where(same[None, None], scores, -1e+30)
    probs = jax.nn.softmax(scores, axis=-1)
    attended = jnp.einsum('kgts,skd->tkgd', probs, vals, precision=HIGH).reshape(length, qheads * HEAD_A)
    return jnp.concatenate([outputs.reshape(length, width), attended], axis=1)

def swiglu(gate, upper):
    return jax.nn.silu(gate) * upper

def group_forward(block, lens, mixw, scanw, mergew, hiddenw, downw, heads, shared):
    seg, pos = doc_index(lens, GRP_TOK)
    gain_one = shared[:D]
    gain_two = shared[D:2 * D]
    conv_shared = shared[2 * D:].reshape(CONV + 1, 2 * STATE)
    first_in = low(scaled_norm(block, gain_one))
    scan = low(low_back(product(first_in, scanw)))
    pmat = low(low_back(product(first_in, mixw)))
    count = HEADS_M // N_TENSOR
    pieces = []
    for tpos in range(N_TENSOR):
        pieces.append(mixer(pmat[:, tpos * IN_TP:(tpos + 1) * IN_TP], scan, heads[tpos * count:(tpos + 1) * count], conv_shared, seg, pos, tpos))
    joined = low(jnp.concatenate(pieces, axis=1))
    middle = block + low_back(product(joined, mergew))
    second_in = low(scaled_norm(middle, gain_two))
    gate_up = low_back(product(second_in, hiddenw))
    units = FF // N_TENSOR
    acts = []
    for tpos in range(N_TENSOR):
        acts.append(swiglu(gate_up[:, 2 * tpos * units:(2 * tpos + 1) * units], gate_up[:, (2 * tpos + 1) * units:(2 * tpos + 2) * units]))
    activ = low(jnp.concatenate(acts, axis=1))
    return middle + low_back(product(activ, downw))

def adamw(weight, first, second, grad, rate, decay):
    first = 0.9 * first + 0.1 * grad
    second = 0.95 * second + 0.05 * grad * grad
    fixed_one = first / (1.0 - 0.9 ** STEP)
    fixed_two = second / (1.0 - 0.95 ** STEP)
    weight = weight - rate * (fixed_one / (jnp.sqrt(fixed_two) + 1e-08) + decay * weight)
    return (first, second, weight)

def reference(residual, out_grad, doc_lengths, mixer_weight, mixer_first, mixer_second, scan_weight, scan_first, scan_second, merge_weight, merge_first, merge_second, hidden_weight, hidden_first, hidden_second, down_weight, down_first, down_second, head_params, head_first, head_second, shared_params, shared_first, shared_second):

    def forward(resid, mixw, scanw, mergew, hiddenw, downw, heads, shared):
        mixw = low(mixw)
        scanw = low(scanw)
        mergew = low(mergew)
        hiddenw = low(hiddenw)
        downw = low(downw)

        def one_group(pair):
            return group_forward(pair[0], pair[1], mixw, scanw, mergew, hiddenw, downw, heads, shared)
        blocks = lax.map(jax.checkpoint(one_group), (resid.reshape(N_DP, GRP_TOK, D), doc_lengths))
        return blocks.reshape(TOKENS, D)
    block_out, backward = jax.vjp(forward, residual, mixer_weight, scan_weight, merge_weight, hidden_weight, down_weight, head_params, shared_params)
    grads = backward(out_grad)
    mixer_new = adamw(mixer_weight, mixer_first, mixer_second, grads[1], 0.02, 0.1)
    scan_new = adamw(scan_weight, scan_first, scan_second, grads[2], 0.02, 0.1)
    merge_new = adamw(merge_weight, merge_first, merge_second, grads[3], 0.02, 0.1)
    hidden_new = adamw(hidden_weight, hidden_first, hidden_second, grads[4], 0.02, 0.1)
    down_new = adamw(down_weight, down_first, down_second, grads[5], 0.02, 0.1)
    head_new = adamw(head_params, head_first, head_second, grads[6], 0.2, 0.0)
    shared_new = adamw(shared_params, shared_first, shared_second, grads[7], 0.2, 0.0)
    return (block_out, grads[0], mixer_new[0], mixer_new[1], mixer_new[2], scan_new[0], scan_new[1], scan_new[2], merge_new[0], merge_new[1], merge_new[2], hidden_new[0], hidden_new[1], hidden_new[2], down_new[0], down_new[1], down_new[2], head_new[0], head_new[1], head_new[2], shared_new[0], shared_new[1], shared_new[2])
```

```python
import jax
import jax.numpy as jnp
from jax import lax
from jax.sharding import PartitionSpec as P

D = 1024
HEADS_M = 24
HEAD_M = 64
STATE = 128
CONV = 4
HEADS_Q = 8
HEADS_KV = 2
HEAD_A = 64
STEP = 10
CORES = 2


EPS = 1e-05
THETA = 10000.0
HIGH = lax.Precision.DEFAULT


def scaled_norm(values, gain):
    return values * lax.rsqrt(jnp.mean(values * values, axis=-1, keepdims=True) + EPS) * gain


def doc_index(lens, count):
    place = jnp.arange(count, dtype=jnp.int32)
    ends = jnp.cumsum(lens)
    after = place[:, None] >= ends[None, :]
    seg = jnp.sum(after.astype(jnp.int32), axis=1)
    start = jnp.sum(jnp.where(after, lens[None, :], 0), axis=1)
    return (seg, place - start)


def causal_conv(values, taps, bias, seg):
    length = values.shape[0]
    total = bias[None, :] + taps[CONV - 1][None, :] * values
    for shift in range(1, CONV):
        moved = jnp.pad(values, ((shift, 0), (0, 0)))[:length]
        keep = jnp.pad(seg, (shift, 0), constant_values=-1)[:length] == seg
        total = total + taps[CONV - 1 - shift][None, :] * jnp.where(keep[:, None], moved, 0.0)
    return total


def rotate(values, pos):
    half = HEAD_A // 2
    freq = THETA ** (-jnp.arange(half, dtype=jnp.float32) * 2.0 / HEAD_A)
    angle = pos.astype(jnp.float32)[:, None] * freq[None, :]
    cosine = jnp.cos(angle)[:, None, :]
    sine = jnp.sin(angle)[:, None, :]
    first = values[..., :half]
    second = values[..., half:]
    return jnp.concatenate(
        [first * cosine - second * sine, second * cosine + first * sine], axis=-1
    )


def mixer(pmat, scan, heads, conv_shared, seg, pos, tpos):
    length = pmat.shape[0]
    count = heads.shape[0]
    width = count * HEAD_M
    qheads = HEADS_Q * count // HEADS_M
    kheads = HEADS_KV * count // HEADS_M
    gates = pmat[:, :width]
    chans = pmat[:, width : 2 * width]
    qpart = pmat[:, 2 * width : 2 * width + qheads * HEAD_A]
    kpart = pmat[:, 2 * width + qheads * HEAD_A : 2 * width + (qheads + kheads) * HEAD_A]
    vpart = pmat[
        :, 2 * width + (qheads + kheads) * HEAD_A : 2 * width + (qheads + 2 * kheads) * HEAD_A
    ]
    taps = jnp.stack([heads[:, k * HEAD_M : (k + 1) * HEAD_M].reshape(-1) for k in range(CONV)])
    bias = heads[:, CONV * HEAD_M : (CONV + 1) * HEAD_M].reshape(-1)
    conv_chans = jax.nn.silu(causal_conv(chans, taps, bias, seg))
    states = jax.nn.silu(
        causal_conv(scan[:, : 2 * STATE], conv_shared[:CONV], conv_shared[CONV], seg)
    )
    in_state = states[:, :STATE]
    out_state = states[:, STATE:]
    base = (CONV + 1) * HEAD_M
    rates = jnp.exp(heads[:, base])
    skip = heads[:, base + 1]
    dt_bias = heads[:, base + 2]
    step_raw = lax.dynamic_slice_in_dim(scan, 2 * STATE + tpos * count, count, 1)
    steps = jax.nn.softplus(step_raw + dt_bias[None, :])
    cum = jnp.cumsum(-rates[None, :] * steps, axis=0)
    place = jnp.arange(length, dtype=jnp.int32)
    same = (seg[:, None] == seg[None, :]) & (place[:, None] >= place[None, :])
    gap = cum.T[:, :, None] - cum.T[:, None, :]
    decay = jnp.where(same[None], jnp.exp(jnp.where(same[None], gap, 0.0)), 0.0)
    inner = jnp.dot(out_state, in_state.T, precision=HIGH)
    heads_x = conv_chans.reshape(length, count, HEAD_M)
    weighted = heads_x * steps[:, :, None]
    outputs = jnp.einsum("hts,shp->thp", decay * inner[None], weighted, precision=HIGH)
    outputs = outputs + skip[None, :, None] * heads_x
    outputs = outputs * jax.nn.silu(gates.reshape(length, count, HEAD_M))
    query = rotate(qpart.reshape(length, qheads, HEAD_A), pos).reshape(
        length, kheads, qheads // kheads, HEAD_A
    )
    keys = rotate(kpart.reshape(length, kheads, HEAD_A), pos)
    vals = vpart.reshape(length, kheads, HEAD_A)
    scores = jnp.einsum("tkgd,skd->kgts", query, keys, precision=HIGH) * HEAD_A ** (-0.5)
    scores = jnp.where(same[None, None], scores, -1e30)
    probs = jax.nn.softmax(scores, axis=-1)
    attended = jnp.einsum("kgts,skd->tkgd", probs, vals, precision=HIGH).reshape(
        length, qheads * HEAD_A
    )
    return jnp.concatenate([outputs.reshape(length, width), attended], axis=1)


def swiglu(gate, upper):
    return jax.nn.silu(gate) * upper


def cross(left, right):
    return lax.dot_general(
        left, right, (((0,), (0,)), ((), ())), preferred_element_type=jnp.float32
    )


def dot(left, right):
    return jnp.dot(left, right, preferred_element_type=jnp.float32)


def dot_t(left, right):
    return lax.dot_general(
        left, right, (((1,), (1,)), ((), ())), preferred_element_type=jnp.float32
    )


def adamw(weight, first, second, grad, rate, decay):
    first = 0.9 * first + 0.1 * grad
    second = 0.95 * second + 0.05 * grad * grad
    fixed_one = first / (1.0 - 0.9**STEP)
    fixed_two = second / (1.0 - 0.95**STEP)
    weight = weight - rate * (fixed_one / (jnp.sqrt(fixed_two) + 1e-08) + decay * weight)
    return (first, second, weight)


def to_own(values, chips, core):
    split = values.reshape(values.shape[0], chips, CORES, -1)
    zero = split[:, :, 0, :].reshape(values.shape[0], -1)
    one = split[:, :, 1, :].reshape(values.shape[0], -1)
    return jnp.concatenate(
        [jnp.where(core == 0, zero, one), jnp.where(core == 0, one, zero)], axis=1
    )


def from_own(values, chips, core):
    half = values.shape[1] // CORES
    own, other = values[:, :half], values[:, half:]
    zero = jnp.where(core == 0, own, other).reshape(values.shape[0], chips, 1, -1)
    one = jnp.where(core == 0, other, own).reshape(values.shape[0], chips, 1, -1)
    return jnp.concatenate([zero, one], axis=2).reshape(values.shape[0], -1)


def swap(values, axis, distance):
    count = lax.axis_size(axis)
    return lax.ppermute(values, axis, [(i, i ^ distance) for i in range(count)])


def pair_rows(own, other, tidx):
    return jnp.where(
        tidx == 0,
        jnp.concatenate([own, other], axis=0),
        jnp.concatenate([other, own], axis=0),
    )


def gather_rows(own, tidx):
    return pair_rows(own, swap(own, "tensor", 1), tidx)


def scatter_rows(partial, tidx):
    rows = partial.shape[0] // 2
    upper, lower = partial[:rows], partial[rows:]
    mine = jnp.where(tidx == 0, upper, lower)
    theirs = jnp.where(tidx == 0, lower, upper).astype(jnp.bfloat16)
    return mine + swap(theirs, "tensor", 1).astype(jnp.float32)


def gather_weight(shard, groups):
    own = lax.all_gather(shard, "dp", axis=0, tiled=True, axis_index_groups=groups)
    return own, swap(own, "dp", 1)


def into_model(values, weight):
    own, other = weight
    return jnp.concatenate([dot_t(values, own), dot_t(values, other)], axis=1)


def from_model(values, weight):
    own, other = weight
    half = own.shape[0]
    return dot(values[:, :half], own) + dot(values[:, half:], other)


def both_cores(model_side, inner_side):
    half = model_side.shape[1] // CORES
    model = jnp.concatenate([model_side[:, :half], swap(model_side[:, half:], "dp", 1)], axis=0)
    inner = jnp.concatenate([inner_side, swap(inner_side, "dp", 1)], axis=0)
    return model, inner


def weight_grad(model_side, inner_side, groups):
    model, inner = both_cores(model_side, inner_side)
    grad = cross(model, inner).astype(jnp.bfloat16)
    return lax.psum_scatter(
        grad, "dp", scatter_dimension=0, axis_index_groups=groups, tiled=True
    ).astype(jnp.float32)


def sum_all(values, axis):
    distance = 1
    while distance < lax.axis_size(axis):
        values = values + swap(values, axis, distance)
        distance *= 2
    return values


def per_device(
    residual,
    out_grad,
    doc_lengths,
    mixer_weight,
    mixer_first,
    mixer_second,
    scan_weight,
    scan_first,
    scan_second,
    merge_weight,
    merge_first,
    merge_second,
    hidden_weight,
    hidden_first,
    hidden_second,
    down_weight,
    down_first,
    down_second,
    head_params,
    head_first,
    head_second,
    shared_params,
    shared_first,
    shared_second,
):
    low = jnp.bfloat16
    tidx = lax.axis_index("tensor")
    count = lax.axis_size("dp")
    chips = count // CORES
    core = lax.axis_index("dp") % CORES
    groups = [[i * CORES + c for i in range(chips)] for c in range(CORES)]
    group = residual.shape[0] * lax.axis_size("tensor")
    seg, pos = doc_index(doc_lengths[0], group)
    conv_shared = shared_params[2 * D :].reshape(CONV + 1, 2 * STATE)

    first_shard = jnp.concatenate([mixer_weight.astype(low), scan_weight.astype(low)], axis=1)
    mix_cols = mixer_weight.shape[1]
    first_w = gather_weight(first_shard, groups)
    merge_w = gather_weight(merge_weight.astype(low).T, groups)
    hidden_w = gather_weight(hidden_weight.astype(low), groups)
    down_w = gather_weight(down_weight.astype(low).T, groups)
    mix_w = (first_w[0][:, :mix_cols], first_w[1][:, :mix_cols])
    scan_w = (first_w[0][:, mix_cols:], first_w[1][:, mix_cols:])

    gains = to_own(shared_params[: 2 * D].reshape(2, D), chips, core)
    resid = to_own(residual, chips, core)
    cotangent = to_own(out_grad, chips, core)

    normed_one, norm_back_one = jax.vjp(scaled_norm, resid, gains[0])
    first_all = gather_rows(normed_one.astype(low), tidx)
    grad_feed = gather_rows(cotangent.astype(low), tidx)
    projected = from_model(first_all, mix_w).astype(low)
    scan_all = from_model(first_all, scan_w).astype(low)

    def mixer_local(pmat, scan, heads, conv):
        return mixer(pmat, scan, heads, conv, seg, pos, tidx)

    joined, mixer_back = jax.vjp(
        mixer_local,
        projected.astype(jnp.float32),
        scan_all.astype(jnp.float32),
        head_params,
        conv_shared,
    )
    joined_low = joined.astype(low)
    middle = resid + scatter_rows(into_model(joined_low, merge_w), tidx)
    normed_two, norm_back_two = jax.vjp(scaled_norm, middle, gains[1])
    second_all = gather_rows(normed_two.astype(low), tidx)
    gate_up = from_model(second_all, hidden_w)
    units = gate_up.shape[1] // 2
    activ, swiglu_back = jax.vjp(swiglu, gate_up[:, :units], gate_up[:, units:])
    activ_low = activ.astype(low)
    block_own = middle + scatter_rows(into_model(activ_low, down_w), tidx)
    block_out = from_own(block_own, chips, core)

    down_sum = weight_grad(grad_feed, activ_low, groups).T
    grad_activ = from_model(grad_feed, down_w)
    grad_gate, grad_upper = swiglu_back(grad_activ)
    grad_gu = jnp.concatenate([grad_gate, grad_upper], axis=1).astype(low)
    hidden_sum = weight_grad(second_all, grad_gu, groups)
    grad_second = scatter_rows(into_model(grad_gu, hidden_w), tidx)
    grad_middle_part, gain_two_grad = norm_back_two(grad_second)
    grad_middle = cotangent + grad_middle_part
    grad_mixed = gather_rows(grad_middle.astype(low), tidx)
    merge_sum = weight_grad(grad_mixed, joined_low, groups).T
    grad_joined = from_model(grad_mixed, merge_w)
    grad_proj, grad_scan, head_grad, conv_grad = mixer_back(grad_joined)
    grad_proj_low = grad_proj.astype(low)
    grad_scan_part = grad_scan.astype(low)
    grad_scan_low = (grad_scan + swap(grad_scan_part, "tensor", 1).astype(jnp.float32)).astype(low)
    first_sum = weight_grad(
        first_all, jnp.concatenate([grad_proj_low, grad_scan_low], axis=1), groups
    )
    mixer_sum, scan_sum = first_sum[:, :mix_cols], first_sum[:, mix_cols:]
    grad_first = scatter_rows(
        into_model(grad_proj_low, mix_w) + into_model(grad_scan_part, scan_w), tidx
    )
    grad_resid_part, gain_one_grad = norm_back_one(grad_first)
    input_grad = from_own(grad_middle + grad_resid_part, chips, core)

    gain_grads = from_own(jnp.stack([gain_one_grad, gain_two_grad]), chips, core)
    shared_part = jnp.concatenate([gain_grads.reshape(-1), conv_grad.reshape(-1)])
    small = jnp.concatenate([shared_part, head_grad.reshape(-1)])
    small = sum_all(small, "dp")
    split = shared_part.shape[0]
    shared_sum = sum_all(small[:split], "tensor")
    head_sum = small[split:].reshape(head_grad.shape)

    mixer_new = adamw(mixer_weight, mixer_first, mixer_second, mixer_sum, 0.02, 0.1)
    scan_new = adamw(scan_weight, scan_first, scan_second, scan_sum, 0.02, 0.1)
    merge_new = adamw(merge_weight, merge_first, merge_second, merge_sum, 0.02, 0.1)
    hidden_new = adamw(hidden_weight, hidden_first, hidden_second, hidden_sum, 0.02, 0.1)
    down_new = adamw(down_weight, down_first, down_second, down_sum, 0.02, 0.1)
    head_new = adamw(head_params, head_first, head_second, head_sum, 0.2, 0.0)
    shared_new = adamw(shared_params, shared_first, shared_second, shared_sum, 0.2, 0.0)
    return (
        block_out,
        input_grad,
        *mixer_new,
        *scan_new,
        *merge_new,
        *hidden_new,
        *down_new,
        *head_new,
        *shared_new,
    )


def solution(mesh):
    return jax.shard_map(
        per_device,
        mesh=mesh,
        in_specs=(
            P(("dp", "tensor"), None),
            P(("dp", "tensor"), None),
            P("dp", None),
            P("dp", "tensor"),
            P("dp", "tensor"),
            P("dp", "tensor"),
            P("dp", None),
            P("dp", None),
            P("dp", None),
            P("tensor", "dp"),
            P("tensor", "dp"),
            P("tensor", "dp"),
            P("dp", "tensor"),
            P("dp", "tensor"),
            P("dp", "tensor"),
            P("tensor", "dp"),
            P("tensor", "dp"),
            P("tensor", "dp"),
            P("tensor", None),
            P("tensor", None),
            P("tensor", None),
            P(),
            P(),
            P(),
        ),
        out_specs=(
            P(("dp", "tensor"), None),
            P(("dp", "tensor"), None),
            P("dp", "tensor"),
            P("dp", "tensor"),
            P("dp", "tensor"),
            P("dp", None),
            P("dp", None),
            P("dp", None),
            P("tensor", "dp"),
            P("tensor", "dp"),
            P("tensor", "dp"),
            P("dp", "tensor"),
            P("dp", "tensor"),
            P("dp", "tensor"),
            P("tensor", "dp"),
            P("tensor", "dp"),
            P("tensor", "dp"),
            P("tensor", None),
            P("tensor", None),
            P("tensor", None),
            P(),
            P(),
            P(),
        ),
        check_vma=False,
    )
```

```python
import jax
import jax.numpy as jnp
from jax import lax
from jax.experimental import pallas as pl
from jax.experimental.pallas import tpu as pltpu
from jax.sharding import PartitionSpec as P

D = 1024
HEADS_M = 24
HEAD_M = 64
STATE = 128
CONV = 4
HEADS_Q = 8
HEADS_KV = 2
HEAD_A = 64
STEP = 10
CORES = 2


EPS = 1e-05
THETA = 10000.0
HIGH = lax.Precision.DEFAULT


def scaled_norm(values, gain):
    return values * lax.rsqrt(jnp.mean(values * values, axis=-1, keepdims=True) + EPS) * gain


def doc_index(lens, count):
    place = jnp.arange(count, dtype=jnp.int32)
    ends = jnp.cumsum(lens)
    after = place[:, None] >= ends[None, :]
    seg = jnp.sum(after.astype(jnp.int32), axis=1)
    start = jnp.sum(jnp.where(after, lens[None, :], 0), axis=1)
    return (seg, place - start)


def causal_conv(values, taps, bias, seg):
    length = values.shape[0]
    total = bias[None, :] + taps[CONV - 1][None, :] * values
    for shift in range(1, CONV):
        moved = jnp.pad(values, ((shift, 0), (0, 0)))[:length]
        keep = jnp.pad(seg, (shift, 0), constant_values=-1)[:length] == seg
        total = total + taps[CONV - 1 - shift][None, :] * jnp.where(keep[:, None], moved, 0.0)
    return total


def rotate(values, pos):
    half = HEAD_A // 2
    freq = THETA ** (-jnp.arange(half, dtype=jnp.float32) * 2.0 / HEAD_A)
    angle = pos.astype(jnp.float32)[:, None] * freq[None, :]
    cosine = jnp.cos(angle)[:, None, :]
    sine = jnp.sin(angle)[:, None, :]
    first = values[..., :half]
    second = values[..., half:]
    return jnp.concatenate(
        [first * cosine - second * sine, second * cosine + first * sine], axis=-1
    )


def mixer(pmat, scan, heads, conv_shared, seg, pos, tpos):
    length = pmat.shape[0]
    count = heads.shape[0]
    width = count * HEAD_M
    qheads = HEADS_Q * count // HEADS_M
    kheads = HEADS_KV * count // HEADS_M
    gates = pmat[:, :width]
    chans = pmat[:, width : 2 * width]
    qpart = pmat[:, 2 * width : 2 * width + qheads * HEAD_A]
    kpart = pmat[:, 2 * width + qheads * HEAD_A : 2 * width + (qheads + kheads) * HEAD_A]
    vpart = pmat[
        :, 2 * width + (qheads + kheads) * HEAD_A : 2 * width + (qheads + 2 * kheads) * HEAD_A
    ]
    taps = jnp.stack([heads[:, k * HEAD_M : (k + 1) * HEAD_M].reshape(-1) for k in range(CONV)])
    bias = heads[:, CONV * HEAD_M : (CONV + 1) * HEAD_M].reshape(-1)
    conv_chans = jax.nn.silu(causal_conv(chans, taps, bias, seg))
    states = jax.nn.silu(
        causal_conv(scan[:, : 2 * STATE], conv_shared[:CONV], conv_shared[CONV], seg)
    )
    in_state = states[:, :STATE]
    out_state = states[:, STATE:]
    base = (CONV + 1) * HEAD_M
    rates = jnp.exp(heads[:, base])
    skip = heads[:, base + 1]
    dt_bias = heads[:, base + 2]
    step_raw = lax.dynamic_slice_in_dim(scan, 2 * STATE + tpos * count, count, 1)
    steps = jax.nn.softplus(step_raw + dt_bias[None, :])
    cum = jnp.cumsum(-rates[None, :] * steps, axis=0)
    place = jnp.arange(length, dtype=jnp.int32)
    same = (seg[:, None] == seg[None, :]) & (place[:, None] >= place[None, :])
    gap = cum.T[:, :, None] - cum.T[:, None, :]
    decay = jnp.where(same[None], jnp.exp(jnp.where(same[None], gap, 0.0)), 0.0)
    inner = jnp.dot(out_state, in_state.T, precision=HIGH)
    heads_x = conv_chans.reshape(length, count, HEAD_M)
    weighted = heads_x * steps[:, :, None]
    outputs = jnp.einsum("hts,shp->thp", decay * inner[None], weighted, precision=HIGH)
    outputs = outputs + skip[None, :, None] * heads_x
    outputs = outputs * jax.nn.silu(gates.reshape(length, count, HEAD_M))
    query = rotate(qpart.reshape(length, qheads, HEAD_A), pos).reshape(
        length, kheads, qheads // kheads, HEAD_A
    )
    keys = rotate(kpart.reshape(length, kheads, HEAD_A), pos)
    vals = vpart.reshape(length, kheads, HEAD_A)
    scores = jnp.einsum("tkgd,skd->kgts", query, keys, precision=HIGH) * HEAD_A ** (-0.5)
    scores = jnp.where(same[None, None], scores, -1e30)
    probs = jax.nn.softmax(scores, axis=-1)
    attended = jnp.einsum("kgts,skd->tkgd", probs, vals, precision=HIGH).reshape(
        length, qheads * HEAD_A
    )
    return jnp.concatenate([outputs.reshape(length, width), attended], axis=1)


def swiglu(gate, upper):
    return jax.nn.silu(gate) * upper


def cross(left, right):
    return lax.dot_general(
        left, right, (((0,), (0,)), ((), ())), preferred_element_type=jnp.float32
    )


def dot(left, right):
    return jnp.dot(left, right, preferred_element_type=jnp.float32)


def dot_t(left, right):
    return lax.dot_general(
        left, right, (((1,), (1,)), ((), ())), preferred_element_type=jnp.float32
    )


def adamw(weight, first, second, grad, rate, decay):
    first = 0.9 * first + 0.1 * grad
    second = 0.95 * second + 0.05 * grad * grad
    fixed_one = first / (1.0 - 0.9**STEP)
    fixed_two = second / (1.0 - 0.95**STEP)
    weight = weight - rate * (fixed_one / (jnp.sqrt(fixed_two) + 1e-08) + decay * weight)
    return (first, second, weight)


def to_own(values, chips, core):
    split = values.reshape(values.shape[0], chips, CORES, -1)
    zero = split[:, :, 0, :].reshape(values.shape[0], -1)
    one = split[:, :, 1, :].reshape(values.shape[0], -1)
    return jnp.concatenate(
        [jnp.where(core == 0, zero, one), jnp.where(core == 0, one, zero)], axis=1
    )


def from_own(values, chips, core):
    half = values.shape[1] // CORES
    own, other = values[:, :half], values[:, half:]
    zero = jnp.where(core == 0, own, other).reshape(values.shape[0], chips, 1, -1)
    one = jnp.where(core == 0, other, own).reshape(values.shape[0], chips, 1, -1)
    return jnp.concatenate([zero, one], axis=2).reshape(values.shape[0], -1)


def swap(values, axis, distance):
    count = lax.axis_size(axis)
    return lax.ppermute(values, axis, [(i, i ^ distance) for i in range(count)])


def pair_rows(own, other, tidx):
    return jnp.where(
        tidx == 0,
        jnp.concatenate([own, other], axis=0),
        jnp.concatenate([other, own], axis=0),
    )


def gather_rows(own, tidx):
    return pair_rows(own, swap(own, "tensor", 1), tidx)


def scatter_rows(partial, tidx):
    rows = partial.shape[0] // 2
    upper, lower = partial[:rows], partial[rows:]
    mine = jnp.where(tidx == 0, upper, lower)
    theirs = jnp.where(tidx == 0, lower, upper).astype(jnp.bfloat16)
    return mine + swap(theirs, "tensor", 1).astype(jnp.float32)


RING_CHIPS = 8


def ring_chip(place):
    place = place % RING_CHIPS
    half = RING_CHIPS // 2
    if isinstance(place, int):
        return 2 * place if place < half else 2 * (RING_CHIPS - 1 - place) + 1
    return jnp.where(place < half, 2 * place, 2 * (RING_CHIPS - 1 - place) + 1)


def ring_place(chip):
    return jnp.where(chip % 2 == 0, chip // 2, RING_CHIPS - 1 - chip // 2)


def ring_step(values, way):
    pairs = [
        (CORES * ring_chip(p) + c, CORES * ring_chip(p + way) + c)
        for p in range(RING_CHIPS)
        for c in range(CORES)
    ]
    return lax.ppermute(values, "dp", pairs)


def place_pieces(pieces, offsets, columns, rows):
    count = len(pieces)
    height, low = pieces[0].shape[0], pieces[0].dtype

    def kernel(offset_ref, *refs):
        out_ref, sem = refs[count], refs[count + 1]
        copies = []
        for i in range(count):
            start = pl.multiple_of(offset_ref[i] * height, height)
            copies.append(
                pltpu.make_async_copy(
                    refs[i],
                    out_ref.at[pl.ds(start, height), pl.ds(columns[i], pieces[i].shape[1])],
                    sem.at[i],
                )
            )
        for copy in copies:
            copy.start()
        for copy in copies:
            copy.wait()

    width = max(c + p.shape[1] for c, p in zip(columns, pieces))
    return pl.pallas_call(
        kernel,
        out_shape=jax.ShapeDtypeStruct((rows, width), low),
        in_specs=[pl.BlockSpec(memory_space=pltpu.SMEM)]
        + [pl.BlockSpec(memory_space=pl.ANY)] * count,
        out_specs=pl.BlockSpec(memory_space=pl.ANY),
        scratch_shapes=[pltpu.SemaphoreType.DMA((count,))],
        name="place_pieces",
    )(offsets, *pieces)


def ring_gather(shard, cuts, place):
    pieces, offsets, columns, marks = [], [], [], []
    chains = [[shard[:, a:b]] for a, b, _ in cuts]
    for step in range(1, RING_CHIPS):
        for chain, (_, _, way) in zip(chains, cuts):
            chain.append(ring_step(chain[-1], way))
        marks.append(chains[0][-1])
    for chain, (a, _, way) in zip(chains, cuts):
        for step, piece in enumerate(chain):
            pieces.append(piece)
            offsets.append(ring_chip(place - way * step))
            columns.append(a)
    own = place_pieces(
        pieces, jnp.stack(offsets).astype(jnp.int32), columns, RING_CHIPS * shard.shape[0]
    )
    return (own, swap(own, "dp", 1)), marks


def ring_reduce(grad, cuts, place):
    rows = grad.shape[0] // RING_CHIPS

    def local(chip, a, b):
        return lax.dynamic_slice(grad, (chip * rows, a), (rows, b - a))

    sums = [None] * len(cuts)
    for step in range(1, RING_CHIPS + 1):
        for i, (a, b, way) in enumerate(cuts):
            part = local(ring_chip(place - way * step), a, b)
            if step > 1:
                part = part + sums[i].astype(jnp.float32)
            if step < RING_CHIPS:
                part = ring_step(part.astype(jnp.bfloat16), way)
            sums[i] = part
    return jnp.concatenate(sums, axis=1)


def after(values, mark):
    return lax.optimization_barrier((values, mark))[0]


def halves(width):
    return ((0, width // 2, 1), (width // 2, width, -1))


def quarters(width):
    cut = [width * i // 4 // 128 * 128 for i in range(4)] + [width]
    return tuple((cut[i], cut[i + 1], 1 if i % 2 == 0 else -1) for i in range(4))


def gather_weights(first, merge, hidden, down, chips, place):
    if chips == RING_CHIPS:
        first_w, marks = ring_gather(first, quarters(first.shape[1]), place)
        merge_w, _ = ring_gather(after(merge, marks[4]), halves(merge.shape[1]), place)
        hidden_w, more = ring_gather(after(hidden, marks[6]), halves(hidden.shape[1]), place)
        down_w, _ = ring_gather(after(down, more[4]), halves(down.shape[1]), place)
        return first_w, merge_w, hidden_w, down_w
    groups = core_groups(chips)
    full = []
    for shard in (first, merge, hidden, down):
        own = lax.all_gather(shard, "dp", axis=0, tiled=True, axis_index_groups=groups)
        full.append((own, swap(own, "dp", 1)))
    return tuple(full)


def core_groups(chips):
    return [[i * CORES + c for i in range(chips)] for c in range(CORES)]


def into_model(values, weight):
    own, other = weight
    return jnp.concatenate([dot_t(values, own), dot_t(values, other)], axis=1)


def from_model(values, weight):
    own, other = weight
    half = own.shape[0]
    return dot(values[:, :half], own) + dot(values[:, half:], other)


def both_cores(model_side, inner_side):
    half = model_side.shape[1] // CORES
    model = jnp.concatenate([model_side[:, :half], swap(model_side[:, half:], "dp", 1)], axis=0)
    inner = jnp.concatenate([inner_side, swap(inner_side, "dp", 1)], axis=0)
    return model, inner


def weight_grad(model_side, inner_side, chips, place, cut):
    model, inner = both_cores(model_side, inner_side)
    grad = cross(model, inner)
    if chips == RING_CHIPS:
        return ring_reduce(grad, cut(grad.shape[1]), place)
    return lax.psum_scatter(
        grad.astype(jnp.bfloat16),
        "dp",
        scatter_dimension=0,
        axis_index_groups=core_groups(chips),
        tiled=True,
    ).astype(jnp.float32)


def sum_all(values, axis):
    distance = 1
    while distance < lax.axis_size(axis):
        values = values + swap(values, axis, distance)
        distance *= 2
    return values


def per_device(
    residual,
    out_grad,
    doc_lengths,
    mixer_weight,
    mixer_first,
    mixer_second,
    scan_weight,
    scan_first,
    scan_second,
    merge_weight,
    merge_first,
    merge_second,
    hidden_weight,
    hidden_first,
    hidden_second,
    down_weight,
    down_first,
    down_second,
    head_params,
    head_first,
    head_second,
    shared_params,
    shared_first,
    shared_second,
):
    low = jnp.bfloat16
    tidx = lax.axis_index("tensor")
    count = lax.axis_size("dp")
    chips = count // CORES
    core = lax.axis_index("dp") % CORES
    place = ring_place(lax.axis_index("dp") // CORES)
    group = residual.shape[0] * lax.axis_size("tensor")
    seg, pos = doc_index(doc_lengths[0], group)
    conv_shared = shared_params[2 * D :].reshape(CONV + 1, 2 * STATE)

    mix_cols = mixer_weight.shape[1]
    scan_cols = scan_weight.shape[1]
    both_cols = mix_cols + scan_cols
    spare = jnp.zeros((mixer_weight.shape[0], -both_cols % 256), low)
    first_shard = jnp.concatenate(
        [mixer_weight.astype(low), scan_weight.astype(low), spare], axis=1
    )
    first_w, merge_w, hidden_w, down_w = gather_weights(
        first_shard,
        merge_weight.astype(low).T,
        hidden_weight.astype(low),
        down_weight.astype(low).T,
        chips,
        place,
    )
    mix_w = (first_w[0][:, :mix_cols], first_w[1][:, :mix_cols])
    scan_w = (first_w[0][:, mix_cols:both_cols], first_w[1][:, mix_cols:both_cols])

    gains = to_own(shared_params[: 2 * D].reshape(2, D), chips, core)
    resid = to_own(residual, chips, core)
    cotangent = to_own(out_grad, chips, core)

    normed_one, norm_back_one = jax.vjp(scaled_norm, resid, gains[0])
    first_all = gather_rows(normed_one.astype(low), tidx)
    grad_feed = gather_rows(cotangent.astype(low), tidx)
    projected = from_model(first_all, mix_w).astype(low)
    scan_all = from_model(first_all, scan_w).astype(low)

    def mixer_local(pmat, scan, heads, conv):
        return mixer(pmat, scan, heads, conv, seg, pos, tidx)

    joined, mixer_back = jax.vjp(
        mixer_local,
        projected.astype(jnp.float32),
        scan_all.astype(jnp.float32),
        head_params,
        conv_shared,
    )
    joined_low = joined.astype(low)
    middle = resid + scatter_rows(into_model(joined_low, merge_w), tidx)
    normed_two, norm_back_two = jax.vjp(scaled_norm, middle, gains[1])
    second_all = gather_rows(normed_two.astype(low), tidx)
    gate_up = from_model(second_all, hidden_w)
    units = gate_up.shape[1] // 2
    activ, swiglu_back = jax.vjp(swiglu, gate_up[:, :units], gate_up[:, units:])
    activ_low = activ.astype(low)
    block_own = middle + scatter_rows(into_model(activ_low, down_w), tidx)
    block_out = from_own(block_own, chips, core)

    down_sum = weight_grad(grad_feed, activ_low, chips, place, halves).T
    grad_activ = from_model(grad_feed, down_w)
    grad_gate, grad_upper = swiglu_back(grad_activ)
    grad_gu = jnp.concatenate([grad_gate, grad_upper], axis=1).astype(low)
    hidden_sum = weight_grad(second_all, grad_gu, chips, place, halves)
    grad_second = scatter_rows(into_model(grad_gu, hidden_w), tidx)
    grad_middle_part, gain_two_grad = norm_back_two(grad_second)
    grad_middle = cotangent + grad_middle_part
    grad_mixed = gather_rows(grad_middle.astype(low), tidx)
    merge_sum = weight_grad(grad_mixed, joined_low, chips, place, halves).T
    grad_joined = from_model(grad_mixed, merge_w)
    grad_proj, grad_scan, head_grad, conv_grad = mixer_back(grad_joined)
    grad_proj_low = grad_proj.astype(low)
    grad_scan_part = grad_scan.astype(low)
    grad_scan_low = (grad_scan + swap(grad_scan_part, "tensor", 1).astype(jnp.float32)).astype(low)
    first_sum = weight_grad(
        first_all,
        jnp.concatenate(
            [grad_proj_low, grad_scan_low, jnp.zeros((group, spare.shape[1]), low)], axis=1
        ),
        chips,
        place,
        quarters,
    )
    mixer_sum, scan_sum = first_sum[:, :mix_cols], first_sum[:, mix_cols:both_cols]
    grad_first = scatter_rows(
        into_model(grad_proj_low, mix_w) + into_model(grad_scan_part, scan_w), tidx
    )
    grad_resid_part, gain_one_grad = norm_back_one(grad_first)
    input_grad = from_own(grad_middle + grad_resid_part, chips, core)

    gain_grads = from_own(jnp.stack([gain_one_grad, gain_two_grad]), chips, core)
    shared_part = jnp.concatenate([gain_grads.reshape(-1), conv_grad.reshape(-1)])
    small = jnp.concatenate([shared_part, head_grad.reshape(-1)])
    small = sum_all(small, "dp")
    split = shared_part.shape[0]
    shared_sum = sum_all(small[:split], "tensor")
    head_sum = small[split:].reshape(head_grad.shape)

    mixer_new = adamw(mixer_weight, mixer_first, mixer_second, mixer_sum, 0.02, 0.1)
    scan_new = adamw(scan_weight, scan_first, scan_second, scan_sum, 0.02, 0.1)
    merge_new = adamw(merge_weight, merge_first, merge_second, merge_sum, 0.02, 0.1)
    hidden_new = adamw(hidden_weight, hidden_first, hidden_second, hidden_sum, 0.02, 0.1)
    down_new = adamw(down_weight, down_first, down_second, down_sum, 0.02, 0.1)
    head_new = adamw(head_params, head_first, head_second, head_sum, 0.2, 0.0)
    shared_new = adamw(shared_params, shared_first, shared_second, shared_sum, 0.2, 0.0)
    return (
        block_out,
        input_grad,
        *mixer_new,
        *scan_new,
        *merge_new,
        *hidden_new,
        *down_new,
        *head_new,
        *shared_new,
    )


def solution(mesh):
    return jax.shard_map(
        per_device,
        mesh=mesh,
        in_specs=(
            P(("dp", "tensor"), None),
            P(("dp", "tensor"), None),
            P("dp", None),
            P("dp", "tensor"),
            P("dp", "tensor"),
            P("dp", "tensor"),
            P("dp", None),
            P("dp", None),
            P("dp", None),
            P("tensor", "dp"),
            P("tensor", "dp"),
            P("tensor", "dp"),
            P("dp", "tensor"),
            P("dp", "tensor"),
            P("dp", "tensor"),
            P("tensor", "dp"),
            P("tensor", "dp"),
            P("tensor", "dp"),
            P("tensor", None),
            P("tensor", None),
            P("tensor", None),
            P(),
            P(),
            P(),
        ),
        out_specs=(
            P(("dp", "tensor"), None),
            P(("dp", "tensor"), None),
            P("dp", "tensor"),
            P("dp", "tensor"),
            P("dp", "tensor"),
            P("dp", None),
            P("dp", None),
            P("dp", None),
            P("tensor", "dp"),
            P("tensor", "dp"),
            P("tensor", "dp"),
            P("dp", "tensor"),
            P("dp", "tensor"),
            P("dp", "tensor"),
            P("tensor", "dp"),
            P("tensor", "dp"),
            P("tensor", "dp"),
            P("tensor", None),
            P("tensor", None),
            P("tensor", None),
            P(),
            P(),
            P(),
        ),
        check_vma=False,
    )
```

```python
import jax
import jax.numpy as jnp
from jax import lax
from jax.experimental import pallas as pl
from jax.experimental.pallas import tpu as pltpu
from jax.sharding import PartitionSpec as P

D = 1024
HEADS_M = 24
HEAD_M = 64
STATE = 128
CONV = 4
HEADS_Q = 8
HEADS_KV = 2
HEAD_A = 64
STEP = 10
CORES = 2


EPS = 1e-05
THETA = 10000.0
HIGH = lax.Precision.DEFAULT


def scaled_norm(values, gain):
    return values * lax.rsqrt(jnp.mean(values * values, axis=-1, keepdims=True) + EPS) * gain


def doc_index(lens, count):
    place = jnp.arange(count, dtype=jnp.int32)
    ends = jnp.cumsum(lens)
    after = place[:, None] >= ends[None, :]
    seg = jnp.sum(after.astype(jnp.int32), axis=1)
    start = jnp.sum(jnp.where(after, lens[None, :], 0), axis=1)
    return (seg, place - start)


def causal_conv(values, taps, bias, seg):
    length = values.shape[0]
    total = bias[None, :] + taps[CONV - 1][None, :] * values
    for shift in range(1, CONV):
        moved = jnp.pad(values, ((shift, 0), (0, 0)))[:length]
        keep = jnp.pad(seg, (shift, 0), constant_values=-1)[:length] == seg
        total = total + taps[CONV - 1 - shift][None, :] * jnp.where(keep[:, None], moved, 0.0)
    return total


def rotate(values, pos):
    half = HEAD_A // 2
    freq = THETA ** (-jnp.arange(half, dtype=jnp.float32) * 2.0 / HEAD_A)
    angle = pos.astype(jnp.float32)[:, None] * freq[None, :]
    cosine = jnp.cos(angle)[:, None, :]
    sine = jnp.sin(angle)[:, None, :]
    first = values[..., :half]
    second = values[..., half:]
    return jnp.concatenate(
        [first * cosine - second * sine, second * cosine + first * sine], axis=-1
    )


def mixer(pmat, scan, heads, conv_shared, seg, pos, tpos):
    length = pmat.shape[0]
    count = heads.shape[0]
    width = count * HEAD_M
    qheads = HEADS_Q * count // HEADS_M
    kheads = HEADS_KV * count // HEADS_M
    gates = pmat[:, :width]
    chans = pmat[:, width : 2 * width]
    qpart = pmat[:, 2 * width : 2 * width + qheads * HEAD_A]
    kpart = pmat[:, 2 * width + qheads * HEAD_A : 2 * width + (qheads + kheads) * HEAD_A]
    vpart = pmat[
        :, 2 * width + (qheads + kheads) * HEAD_A : 2 * width + (qheads + 2 * kheads) * HEAD_A
    ]
    taps = jnp.stack([heads[:, k * HEAD_M : (k + 1) * HEAD_M].reshape(-1) for k in range(CONV)])
    bias = heads[:, CONV * HEAD_M : (CONV + 1) * HEAD_M].reshape(-1)
    conv_chans = jax.nn.silu(causal_conv(chans, taps, bias, seg))
    states = jax.nn.silu(
        causal_conv(scan[:, : 2 * STATE], conv_shared[:CONV], conv_shared[CONV], seg)
    )
    in_state = states[:, :STATE]
    out_state = states[:, STATE:]
    base = (CONV + 1) * HEAD_M
    rates = jnp.exp(heads[:, base])
    skip = heads[:, base + 1]
    dt_bias = heads[:, base + 2]
    step_raw = lax.dynamic_slice_in_dim(scan, 2 * STATE + tpos * count, count, 1)
    steps = jax.nn.softplus(step_raw + dt_bias[None, :])
    cum = jnp.cumsum(-rates[None, :] * steps, axis=0)
    place = jnp.arange(length, dtype=jnp.int32)
    same = (seg[:, None] == seg[None, :]) & (place[:, None] >= place[None, :])
    gap = cum.T[:, :, None] - cum.T[:, None, :]
    decay = jnp.where(same[None], jnp.exp(jnp.where(same[None], gap, 0.0)), 0.0)
    inner = jnp.dot(out_state, in_state.T, precision=HIGH)
    heads_x = conv_chans.reshape(length, count, HEAD_M)
    weighted = heads_x * steps[:, :, None]
    outputs = jnp.einsum("hts,shp->thp", decay * inner[None], weighted, precision=HIGH)
    outputs = outputs + skip[None, :, None] * heads_x
    outputs = outputs * jax.nn.silu(gates.reshape(length, count, HEAD_M))
    query = rotate(qpart.reshape(length, qheads, HEAD_A), pos).reshape(
        length, kheads, qheads // kheads, HEAD_A
    )
    keys = rotate(kpart.reshape(length, kheads, HEAD_A), pos)
    vals = vpart.reshape(length, kheads, HEAD_A)
    scores = jnp.einsum("tkgd,skd->kgts", query, keys, precision=HIGH) * HEAD_A ** (-0.5)
    scores = jnp.where(same[None, None], scores, -1e30)
    probs = jax.nn.softmax(scores, axis=-1)
    attended = jnp.einsum("kgts,skd->tkgd", probs, vals, precision=HIGH).reshape(
        length, qheads * HEAD_A
    )
    return jnp.concatenate([outputs.reshape(length, width), attended], axis=1)


def swiglu(gate, upper):
    return jax.nn.silu(gate) * upper


def cross(left, right):
    return lax.dot_general(
        left, right, (((0,), (0,)), ((), ())), preferred_element_type=jnp.float32
    )


def dot(left, right):
    return jnp.dot(left, right, preferred_element_type=jnp.float32)


def dot_t(left, right):
    return lax.dot_general(
        left, right, (((1,), (1,)), ((), ())), preferred_element_type=jnp.float32
    )


def adamw(weight, first, second, grad, rate, decay):
    first = 0.9 * first + 0.1 * grad
    second = 0.95 * second + 0.05 * grad * grad
    fixed_one = first / (1.0 - 0.9**STEP)
    fixed_two = second / (1.0 - 0.95**STEP)
    weight = weight - rate * (fixed_one / (jnp.sqrt(fixed_two) + 1e-08) + decay * weight)
    return (first, second, weight)


def swap(values, axis, distance):
    count = lax.axis_size(axis)
    return lax.ppermute(values, axis, [(i, i ^ distance) for i in range(count)])


def pair_rows(own, other, tidx):
    return jnp.where(
        tidx == 0,
        jnp.concatenate([own, other], axis=0),
        jnp.concatenate([other, own], axis=0),
    )


def gather_rows(own, tidx):
    return pair_rows(own, swap(own, "tensor", 1), tidx)


def scatter_rows(partial, tidx):
    rows = partial.shape[0] // 2
    upper, lower = partial[:rows], partial[rows:]
    mine = jnp.where(tidx == 0, upper, lower)
    theirs = jnp.where(tidx == 0, lower, upper).astype(jnp.bfloat16)
    return mine + swap(theirs, "tensor", 1).astype(jnp.float32)


RING_CHIPS = 8


def ring_chip(place):
    place = place % RING_CHIPS
    half = RING_CHIPS // 2
    if isinstance(place, int):
        return 2 * place if place < half else 2 * (RING_CHIPS - 1 - place) + 1
    return jnp.where(place < half, 2 * place, 2 * (RING_CHIPS - 1 - place) + 1)


def ring_place(chip):
    return jnp.where(chip % 2 == 0, chip // 2, RING_CHIPS - 1 - chip // 2)


def ring_step(values):
    pairs = []
    for p in range(RING_CHIPS):
        pairs.append((CORES * ring_chip(p), CORES * ring_chip(p + 1)))
        pairs.append((CORES * ring_chip(p + 1) + 1, CORES * ring_chip(p) + 1))
    return lax.ppermute(values, "dp", pairs)


def place_rows(pieces, blocks):
    count = len(pieces)
    height, width = pieces[0].shape

    def kernel(block_ref, *refs):
        for i in range(count):
            start = pl.multiple_of(block_ref[i] * height, height)
            refs[count][pl.ds(start, height), :] = refs[i][...]

    return pl.pallas_call(
        kernel,
        out_shape=jax.ShapeDtypeStruct((count * height, width), pieces[0].dtype),
        in_specs=[pl.BlockSpec(memory_space=pltpu.SMEM)]
        + [pl.BlockSpec(memory_space=pltpu.VMEM)] * count,
        out_specs=pl.BlockSpec(memory_space=pltpu.VMEM),
        compiler_params=pltpu.CompilerParams(vmem_limit_bytes=40 * 2**20),
        name="place_rows",
    )(blocks, *pieces)


def ring_gather(shard, place, core):
    way = 1 - 2 * core
    own = [shard]
    other = [swap(shard, "dp", 1)]
    for _ in range(1, RING_CHIPS):
        own.append(ring_step(own[-1]))
        other.append(swap(own[-1], "dp", 1))
    blocks = [CORES * ring_chip(place - way * k) + core for k in range(RING_CHIPS)]
    blocks += [CORES * ring_chip(place + way * k) + 1 - core for k in range(RING_CHIPS)]
    return place_rows(own + other, jnp.stack(blocks).astype(jnp.int32))


def ring_reduce(grad, place, core):
    rows = grad.shape[0] // RING_CHIPS
    way = 1 - 2 * core
    middle = grad.shape[1] // 2 // 128 * 128
    cuts = ((0, middle), (middle, grad.shape[1]))
    sums = [None] * len(cuts)
    for step in range(1, RING_CHIPS + 1):
        start = ring_chip(place - way * step) * rows
        for i, (a, b) in enumerate(cuts):
            part = lax.dynamic_slice(grad, (start, a), (rows, b - a))
            if step > 1:
                part = part + sums[i].astype(jnp.float32)
            if step < RING_CHIPS:
                part = ring_step(part.astype(jnp.bfloat16))
            sums[i] = part
    return jnp.concatenate(sums, axis=1)


def own_half(values, core):
    half = values.shape[1] // CORES
    left, right = values[:, :half], values[:, half:]
    return jnp.where(core == 0, left, right), jnp.where(core == 0, right, left)


def chip_grad(model_side, inner_side, core):
    keep, give = own_half(inner_side, core)
    return cross(model_side, keep) + cross(
        swap(model_side, "dp", 1), swap(give, "dp", 1)
    )


def own_rows(summed, core):
    rows = summed.shape[0] // CORES
    upper, lower = summed[:rows], summed[rows:]
    mine = jnp.where(core == 0, upper, lower)
    give = jnp.where(core == 0, lower, upper).astype(jnp.bfloat16)
    taken = swap(give, "dp", 1).astype(jnp.float32)
    return jnp.where(core == 0, mine, taken), jnp.where(core == 0, taken, mine)


def join_halves(halves, a, b):
    return jnp.concatenate([halves[0][:, a:b], halves[1][:, a:b]], axis=1)


def sum_all(values, axis):
    distance = 1
    while distance < lax.axis_size(axis):
        values = values + swap(values, axis, distance)
        distance *= 2
    return values


def per_device(
    residual,
    out_grad,
    doc_lengths,
    mixer_weight,
    mixer_first,
    mixer_second,
    scan_weight,
    scan_first,
    scan_second,
    merge_weight,
    merge_first,
    merge_second,
    hidden_weight,
    hidden_first,
    hidden_second,
    down_weight,
    down_first,
    down_second,
    head_params,
    head_first,
    head_second,
    shared_params,
    shared_first,
    shared_second,
):
    low = jnp.bfloat16
    tidx = lax.axis_index("tensor")
    count = lax.axis_size("dp")
    chips = count // CORES
    core = lax.axis_index("dp") % CORES
    place = ring_place(lax.axis_index("dp") // CORES)
    group = residual.shape[0] * lax.axis_size("tensor")
    seg, pos = doc_index(doc_lengths[0], group)
    conv_shared = shared_params[2 * D :].reshape(CONV + 1, 2 * STATE)

    ring = chips == RING_CHIPS
    mix_cols = mixer_weight.shape[1]
    both_cols = mix_cols + scan_weight.shape[1]
    spare = jnp.zeros((mixer_weight.shape[0], -both_cols % 256), low)
    first_shard = jnp.concatenate(
        [mixer_weight.astype(low), scan_weight.astype(low), spare], axis=1
    )
    rest_shard = jnp.concatenate(
        [hidden_weight.astype(low), down_weight.astype(low).T, merge_weight.astype(low).T],
        axis=1,
    )
    hidden_cols, down_cols = hidden_weight.shape[1], down_weight.shape[0]
    rest_w = lax.all_gather(rest_shard, "dp", axis=0, tiled=True)
    if ring:
        first_w = ring_gather(first_shard, place, core)
    else:
        first_w = lax.all_gather(first_shard, "dp", axis=0, tiled=True)
    mix_w, scan_w = first_w[:, :mix_cols], first_w[:, mix_cols:both_cols]
    hidden_w = rest_w[:, :hidden_cols]
    down_w = rest_w[:, hidden_cols : hidden_cols + down_cols]
    merge_w = rest_w[:, hidden_cols + down_cols :]

    normed_one, norm_back_one = jax.vjp(scaled_norm, residual, shared_params[:D])
    first_all = gather_rows(normed_one.astype(low), tidx)
    grad_feed = gather_rows(out_grad.astype(low), tidx)
    projected = dot(first_all, mix_w).astype(low)
    scan_all = dot(first_all, scan_w).astype(low)

    def mixer_local(pmat, scan, heads, conv):
        return mixer(pmat, scan, heads, conv, seg, pos, tidx)

    joined, mixer_back = jax.vjp(
        mixer_local,
        projected.astype(jnp.float32),
        scan_all.astype(jnp.float32),
        head_params,
        conv_shared,
    )
    joined_low = joined.astype(low)
    middle = residual + scatter_rows(dot_t(joined_low, merge_w), tidx)
    normed_two, norm_back_two = jax.vjp(scaled_norm, middle, shared_params[D : 2 * D])
    second_all = gather_rows(normed_two.astype(low), tidx)
    gate_up = dot(second_all, hidden_w)
    units = gate_up.shape[1] // 2
    activ, swiglu_back = jax.vjp(swiglu, gate_up[:, :units], gate_up[:, units:])
    activ_low = activ.astype(low)
    block_out = middle + scatter_rows(dot_t(activ_low, down_w), tidx)

    grad_activ = dot(grad_feed, down_w)
    grad_gate, grad_upper = swiglu_back(grad_activ)
    grad_gu = jnp.concatenate([grad_gate, grad_upper], axis=1).astype(low)
    grad_second = scatter_rows(dot_t(grad_gu, hidden_w), tidx)
    grad_middle_part, gain_two_grad = norm_back_two(grad_second)
    grad_middle = out_grad + grad_middle_part
    grad_mixed = gather_rows(grad_middle.astype(low), tidx)
    grad_joined = dot(grad_mixed, merge_w)
    if ring:
        rest_grad = jnp.concatenate(
            [
                chip_grad(second_all, grad_gu, core),
                chip_grad(grad_feed, activ_low, core),
                chip_grad(grad_mixed, joined_low, core),
            ],
            axis=1,
        )
        rest_grad = rest_grad.astype(low)
        grad_joined, rest_grad = lax.optimization_barrier((grad_joined, rest_grad))
        rest_sum = lax.psum_scatter(
            rest_grad,
            "dp",
            scatter_dimension=0,
            axis_index_groups=[[i * CORES + c for i in range(chips)] for c in range(CORES)],
            tiled=True,
        ).astype(jnp.float32)
    grad_proj, grad_scan, head_grad, conv_grad = mixer_back(grad_joined)
    grad_proj_low = grad_proj.astype(low)
    grad_scan_part = grad_scan.astype(low)
    grad_scan_low = (grad_scan + swap(grad_scan_part, "tensor", 1).astype(jnp.float32)).astype(low)
    grad_first = scatter_rows(
        dot_t(grad_proj_low, mix_w) + dot_t(grad_scan_part, scan_w), tidx
    )
    grad_resid_part, gain_one_grad = norm_back_one(grad_first)
    input_grad = grad_middle + grad_resid_part

    first_inner = jnp.concatenate(
        [grad_proj_low, grad_scan_low, jnp.zeros((group, spare.shape[1]), low)], axis=1
    )
    if ring:
        rest_halves = own_rows(rest_sum, core)
        a, b = hidden_cols // CORES, (hidden_cols + down_cols) // CORES
        hidden_sum = join_halves(rest_halves, 0, a)
        down_sum = join_halves(rest_halves, a, b).T
        merge_sum = join_halves(rest_halves, b, rest_sum.shape[1]).T
        first_sum = ring_reduce(chip_grad(first_all, first_inner, core), place, core)
        first_sum = join_halves(own_rows(first_sum, core), 0, first_sum.shape[1])
    else:
        whole = jnp.concatenate(
            [
                cross(first_all, first_inner),
                cross(second_all, grad_gu),
                cross(grad_feed, activ_low),
                cross(grad_mixed, joined_low),
            ],
            axis=1,
        ).astype(low)
        whole = lax.psum_scatter(whole, "dp", scatter_dimension=0, tiled=True)
        whole = whole.astype(jnp.float32)
        a = first_inner.shape[1]
        first_sum = whole[:, :a]
        hidden_sum = whole[:, a : a + hidden_cols]
        a = a + hidden_cols
        down_sum = whole[:, a : a + down_cols].T
        merge_sum = whole[:, a + down_cols :].T
    mixer_sum, scan_sum = first_sum[:, :mix_cols], first_sum[:, mix_cols:both_cols]

    shared_part = jnp.concatenate([gain_one_grad, gain_two_grad, conv_grad.reshape(-1)])
    small = jnp.concatenate([shared_part, head_grad.reshape(-1)])
    small = sum_all(small, "dp")
    split = shared_part.shape[0]
    shared_sum = sum_all(small[:split], "tensor")
    head_sum = small[split:].reshape(head_grad.shape)

    mixer_new = adamw(mixer_weight, mixer_first, mixer_second, mixer_sum, 0.02, 0.1)
    scan_new = adamw(scan_weight, scan_first, scan_second, scan_sum, 0.02, 0.1)
    merge_new = adamw(merge_weight, merge_first, merge_second, merge_sum, 0.02, 0.1)
    hidden_new = adamw(hidden_weight, hidden_first, hidden_second, hidden_sum, 0.02, 0.1)
    down_new = adamw(down_weight, down_first, down_second, down_sum, 0.02, 0.1)
    head_new = adamw(head_params, head_first, head_second, head_sum, 0.2, 0.0)
    shared_new = adamw(shared_params, shared_first, shared_second, shared_sum, 0.2, 0.0)
    return (
        block_out,
        input_grad,
        *mixer_new,
        *scan_new,
        *merge_new,
        *hidden_new,
        *down_new,
        *head_new,
        *shared_new,
    )


def solution(mesh):
    return jax.shard_map(
        per_device,
        mesh=mesh,
        in_specs=(
            P(("dp", "tensor"), None),
            P(("dp", "tensor"), None),
            P("dp", None),
            P("dp", "tensor"),
            P("dp", "tensor"),
            P("dp", "tensor"),
            P("dp", None),
            P("dp", None),
            P("dp", None),
            P("tensor", "dp"),
            P("tensor", "dp"),
            P("tensor", "dp"),
            P("dp", "tensor"),
            P("dp", "tensor"),
            P("dp", "tensor"),
            P("tensor", "dp"),
            P("tensor", "dp"),
            P("tensor", "dp"),
            P("tensor", None),
            P("tensor", None),
            P("tensor", None),
            P(),
            P(),
            P(),
        ),
        out_specs=(
            P(("dp", "tensor"), None),
            P(("dp", "tensor"), None),
            P("dp", "tensor"),
            P("dp", "tensor"),
            P("dp", "tensor"),
            P("dp", None),
            P("dp", None),
            P("dp", None),
            P("tensor", "dp"),
            P("tensor", "dp"),
            P("tensor", "dp"),
            P("dp", "tensor"),
            P("dp", "tensor"),
            P("dp", "tensor"),
            P("tensor", "dp"),
            P("tensor", "dp"),
            P("tensor", "dp"),
            P("tensor", None),
            P("tensor", None),
            P("tensor", None),
            P(),
            P(),
            P(),
        ),
        check_vma=False,
    )
```

```python
import jax
import jax.numpy as jnp
from jax import lax
from jax.experimental import pallas as pl
from jax.experimental.pallas import tpu as pltpu
from jax.sharding import PartitionSpec as P

D = 1024
HEADS_M = 24
HEAD_M = 64
STATE = 128
CONV = 4
HEADS_Q = 8
HEADS_KV = 2
HEAD_A = 64
STEP = 10
CORES = 2


EPS = 1e-05
THETA = 10000.0
HIGH = lax.Precision.HIGHEST


def scaled_norm(values, gain):
    return values * lax.rsqrt(jnp.mean(values * values, axis=-1, keepdims=True) + EPS) * gain


def doc_index(lens, count):
    place = jnp.arange(count, dtype=jnp.int32)
    ends = jnp.cumsum(lens)
    after = place[:, None] >= ends[None, :]
    seg = jnp.sum(after.astype(jnp.int32), axis=1)
    start = jnp.sum(jnp.where(after, lens[None, :], 0), axis=1)
    return (seg, place - start)


HEADS = HEADS_M // 2
WIDTH = HEADS * HEAD_M
QCOLS = HEADS_Q // 2 * HEAD_A
LANES = 128


def exact_dot(left, right, dims=((1,), (0,))):
    return lax.dot_general(
        left, right, (dims, ((), ())), precision=HIGH, preferred_element_type=jnp.float32
    )


def low_dot(left, right, dims=((1,), (0,))):
    return lax.dot_general(
        left.astype(jnp.bfloat16),
        right.astype(jnp.bfloat16),
        (dims, ((), ())),
        preferred_element_type=jnp.float32,
    )


ROWS = ((0,), (0,))
COLS = ((1,), (1,))


def lane_of(shape):
    return lax.broadcasted_iota(jnp.int32, shape, 1)


def shifted(values, pos, shift):
    return jnp.where(pos >= shift, pltpu.roll(values, shift, 0), 0.0)


def conv_forward(values, rows, pos):
    total = rows[CONV : CONV + 1] + rows[CONV - 1 : CONV] * values
    for shift in range(1, CONV):
        tap = rows[CONV - 1 - shift : CONV - shift]
        total = total + tap * shifted(values, pos, shift)
    return total


def conv_backward(grad, values, rows, pos):
    length = values.shape[0]
    back = rows[CONV - 1 : CONV] * grad
    taps = [jnp.sum(grad * values, axis=0, keepdims=True)]
    for shift in range(1, CONV):
        tap = rows[CONV - 1 - shift : CONV - shift]
        kept = jnp.where(pos >= shift, grad, 0.0)
        back = back + tap * pltpu.roll(kept, length - shift, 0)
        taps.append(jnp.sum(kept * pltpu.roll(values, shift, 0), axis=0, keepdims=True))
    return back, taps[::-1] + [jnp.sum(grad, axis=0, keepdims=True)]


def swap_pairs(values):
    first = lane_of(values.shape) % HEAD_A < HEAD_A // 2
    half = HEAD_A // 2
    return jnp.where(first, pltpu.roll(values, LANES - half, 1), pltpu.roll(values, half, 1))


def turn(values, cosine, sine):
    return values * cosine + swap_pairs(values) * sine


def turn_back(values, cosine, sine):
    return values * cosine + swap_pairs(values * sine)


def half_lanes(values, which):
    mine = lane_of(values.shape) // HEAD_A == which
    return jnp.where(mine, values, jnp.zeros_like(values))


def mixer_parts(p_ref, conv_ref, bc_ref, head_ref, sel_ref, spread_ref, pos_ref, segs_ref, segt_ref):
    length = p_ref.shape[0]
    base = 2 * WIDTH + QCOLS + 2 * HEAD_A
    pos = pos_ref[...]
    wide = p_ref[:, WIDTH : 2 * WIDTH].astype(jnp.float32)
    chans_pre = conv_forward(wide, conv_ref[...], pos)
    chans_sig = jax.nn.sigmoid(chans_pre)
    states = p_ref[:, base : base + 2 * STATE].astype(jnp.float32)
    states_pre = conv_forward(states, bc_ref[...], pos)
    states_sig = jax.nn.sigmoid(states_pre)
    raw = p_ref[:, base + 2 * STATE : base + 2 * STATE + LANES].astype(jnp.float32)
    step_pre = exact_dot(raw, sel_ref[...]) + head_ref[1:2]
    steps = jnp.maximum(step_pre, 0.0) + jnp.log1p(jnp.exp(-jnp.abs(step_pre)))
    rates = head_ref[0:1]
    row = lax.broadcasted_iota(jnp.int32, (length, length), 0)
    column = lax.broadcasted_iota(jnp.int32, (length, length), 1)
    before = (row >= column).astype(jnp.float32)
    cum = exact_dot(before, -rates * steps)
    same = (segs_ref[...] == segt_ref[...]) & (row >= column)
    steps_wide = exact_dot(steps, spread_ref[...])
    chans = chans_pre * chans_sig
    states_out = states_pre * states_sig
    in_state, out_state = states_out[:, :STATE], states_out[:, STATE:]
    inner = jnp.where(same, exact_dot(out_state, in_state, COLS), 0.0)
    return dict(
        pos=pos, wide=wide, chans_pre=chans_pre, chans_sig=chans_sig, chans=chans,
        states=states, states_pre=states_pre, states_sig=states_sig, in_state=in_state,
        out_state=out_state, step_pre=step_pre, steps=steps, rates=rates, before=before,
        cum=cum, cum_t=cum.T, same=same, steps_wide=steps_wide, inner=inner,
        weighted=(steps_wide * chans).astype(jnp.bfloat16),
    )


def decay_of(parts, head):
    gap = parts["cum"][:, head : head + 1] - parts["cum_t"][head : head + 1, :]
    return jnp.exp(jnp.minimum(gap, 0.0))


def attention_parts(p_ref, cos_ref, sin_ref):
    cosine, sine = cos_ref[...], sin_ref[...]
    pairs = []
    for i in range(QCOLS // LANES):
        a = 2 * WIDTH + i * LANES
        query = turn(p_ref[:, a : a + LANES].astype(jnp.float32), cosine, sine)
        pairs.append((query * HEAD_A ** (-0.5)).astype(jnp.bfloat16))
    a = 2 * WIDTH + QCOLS
    both = p_ref[:, a : a + LANES].astype(jnp.float32)
    key = half_lanes(turn(both, cosine, sine), 0)
    value = half_lanes(both, 1)
    keys = (key.astype(jnp.bfloat16), pltpu.roll(key, HEAD_A, 1).astype(jnp.bfloat16))
    values = (pltpu.roll(value, HEAD_A, 1).astype(jnp.bfloat16), value.astype(jnp.bfloat16))
    return pairs, keys, values


def attention_probs(query, key, same):
    scores = jnp.where(same, low_dot(query, key, COLS), -1e30)
    top = jnp.max(scores, axis=1, keepdims=True)
    raised = jnp.exp(scores - top)
    return raised / jnp.sum(raised, axis=1, keepdims=True)


def forward_kernel(
    p_ref, conv_ref, bc_ref, head_ref, sel_ref, spread_ref, pos_ref, segs_ref, segt_ref,
    cos_ref, sin_ref, cat_ref, y_ref,
):
    parts = mixer_parts(
        p_ref, conv_ref, bc_ref, head_ref, sel_ref, spread_ref, pos_ref, segs_ref, segt_ref
    )
    for i in range(WIDTH // LANES):
        a = i * LANES
        tile = parts["weighted"][:, a : a + LANES]
        out = jnp.zeros((p_ref.shape[0], LANES), jnp.float32)
        for which in range(2):
            mixed = decay_of(parts, 2 * i + which) * parts["inner"]
            out = out + low_dot(mixed, half_lanes(tile, which))
        y_ref[:, a : a + LANES] = out
        gate = p_ref[:, a : a + LANES].astype(jnp.float32)
        out = out + conv_ref[CONV + 1 : CONV + 2, a : a + LANES] * parts["chans"][:, a : a + LANES]
        cat_ref[:, a : a + LANES] = (out * gate * jax.nn.sigmoid(gate)).astype(cat_ref.dtype)
    pairs, keys, values = attention_parts(p_ref, cos_ref, sin_ref)
    for i, query in enumerate(pairs):
        out = jnp.zeros((p_ref.shape[0], LANES), jnp.float32)
        for which in range(2):
            probs = attention_probs(query, keys[which], parts["same"])
            out = out + low_dot(probs, values[which])
        a = WIDTH + i * LANES
        cat_ref[:, a : a + LANES] = out.astype(cat_ref.dtype)


def backward_kernel(
    p_ref, conv_ref, bc_ref, head_ref, sel_ref, spread_ref, pos_ref, segs_ref, segt_ref,
    cos_ref, sin_ref, y_ref, grad_ref, dp_ref, dconv_ref, dbc_ref, dhead_ref,
):
    length = p_ref.shape[0]
    low = dp_ref.dtype
    parts = mixer_parts(
        p_ref, conv_ref, bc_ref, head_ref, sel_ref, spread_ref, pos_ref, segs_ref, segt_ref
    )
    pos, chans = parts["pos"], parts["chans"]
    gate = p_ref[:, :WIDTH].astype(jnp.float32)
    gate_sig = jax.nn.sigmoid(gate)
    grad = grad_ref[:, :WIDTH]
    skip = conv_ref[CONV + 1 : CONV + 2]
    outputs = y_ref[...]
    dgate = grad * (outputs + skip * chans) * gate_sig * (1.0 + gate * (1.0 - gate_sig))
    dp_ref[:, :WIDTH] = dgate.astype(low)
    dy = grad * gate * gate_sig
    dy_low = dy.astype(jnp.bfloat16)
    dweighted = []
    dinner = jnp.zeros((length, length), jnp.float32)
    for i in range(WIDTH // LANES):
        a = i * LANES
        tile = parts["weighted"][:, a : a + LANES]
        out = jnp.zeros((length, LANES), jnp.float32)
        for which in range(2):
            decay = decay_of(parts, 2 * i + which)
            dy_half = half_lanes(dy_low[:, a : a + LANES], which)
            out = out + low_dot(decay * parts["inner"], dy_half, ROWS)
            dinner = dinner + low_dot(dy_half, tile, COLS) * decay
        dweighted.append(out)
    dweighted = jnp.concatenate(dweighted, axis=1)
    spread = spread_ref[...]
    weighted = parts["weighted"].astype(jnp.float32)
    dcum = exact_dot(dy_low.astype(jnp.float32) * outputs - weighted * dweighted, spread, COLS)
    dsteps = exact_dot(dweighted * chans, spread, COLS)
    dchans = skip * dy + parts["steps_wide"] * dweighted
    drate = exact_dot(parts["before"], dcum, ROWS)
    dsteps = (dsteps - parts["rates"] * drate) * jax.nn.sigmoid(parts["step_pre"])
    dlog = jnp.sum(-parts["rates"] * parts["steps"] * drate, axis=0, keepdims=True)
    dbias = jnp.sum(dsteps, axis=0, keepdims=True)
    dhead_ref[...] = jnp.concatenate([dlog, dbias, jnp.zeros((6, LANES), jnp.float32)], axis=0)
    base = 2 * WIDTH + QCOLS + 2 * HEAD_A
    draw = exact_dot(dsteps, sel_ref[...], COLS)
    dp_ref[:, base + 2 * STATE :] = draw.astype(low)

    sig, pre = parts["chans_sig"], parts["chans_pre"]
    dpre = dchans * sig * (1.0 + pre * (1.0 - sig))
    back, rows = conv_backward(dpre, parts["wide"], conv_ref[...], pos)
    dp_ref[:, WIDTH : 2 * WIDTH] = back.astype(low)
    rows.append(jnp.sum(dy * chans, axis=0, keepdims=True))
    dconv_ref[...] = jnp.concatenate(rows + [jnp.zeros((2, WIDTH), jnp.float32)], axis=0)

    dinner = jnp.where(parts["same"], dinner, 0.0)
    dstates = jnp.concatenate(
        [exact_dot(dinner, parts["out_state"], ROWS), exact_dot(dinner, parts["in_state"])],
        axis=1,
    )
    sig, pre = parts["states_sig"], parts["states_pre"]
    dpre = dstates * sig * (1.0 + pre * (1.0 - sig))
    back, rows = conv_backward(dpre, parts["states"], bc_ref[...], pos)
    dp_ref[:, base : base + 2 * STATE] = back.astype(low)
    dbc_ref[...] = jnp.concatenate(rows + [jnp.zeros((3, 2 * STATE), jnp.float32)], axis=0)

    pairs, keys, values = attention_parts(p_ref, cos_ref, sin_ref)
    cosine, sine = cos_ref[...], sin_ref[...]
    dkeys = [jnp.zeros((length, LANES), jnp.float32) for _ in range(2)]
    dvalues = [jnp.zeros((length, LANES), jnp.float32) for _ in range(2)]
    for i, query in enumerate(pairs):
        a = WIDTH + i * LANES
        datt = grad_ref[:, a : a + LANES].astype(jnp.bfloat16)
        dquery = jnp.zeros((length, LANES), jnp.float32)
        for which in range(2):
            probs = attention_probs(query, keys[which], parts["same"])
            dprobs = low_dot(datt, values[which], COLS)
            dscores = probs * (dprobs - jnp.sum(probs * dprobs, axis=1, keepdims=True))
            dscores = dscores.astype(jnp.bfloat16)
            dquery = dquery + low_dot(dscores, keys[which])
            dkeys[which] = dkeys[which] + low_dot(dscores, query, ROWS)
            dvalues[which] = dvalues[which] + low_dot(probs, datt, ROWS)
        a = 2 * WIDTH + i * LANES
        dquery = turn_back(dquery * HEAD_A ** (-0.5), cosine, sine)
        dp_ref[:, a : a + LANES] = dquery.astype(low)
    dkey = half_lanes(dkeys[0], 0) + pltpu.roll(half_lanes(dkeys[1], 1), HEAD_A, 1)
    dvalue = pltpu.roll(half_lanes(dvalues[0], 0), HEAD_A, 1) + half_lanes(dvalues[1], 1)
    a = 2 * WIDTH + QCOLS
    dboth = half_lanes(turn_back(dkey, cosine, sine), 0) + dvalue
    dp_ref[:, a : a + LANES] = dboth.astype(low)


def local_call(kernel, outs, name):
    space = pl.BlockSpec(memory_space=pltpu.VMEM)
    return lambda *args: pl.pallas_call(
        kernel,
        out_shape=outs,
        in_specs=[space] * len(args),
        out_specs=[space] * len(outs),
        compiler_params=pltpu.CompilerParams(vmem_limit_bytes=56 * 2**20),
        name=name,
    )(*args)


def mixer_consts(head_params, conv_shared, seg, pos, tidx):
    rows = [
        head_params[:, k * HEAD_M : (k + 1) * HEAD_M].reshape(1, -1) for k in range(CONV + 1)
    ]
    base = (CONV + 1) * HEAD_M
    skip = jnp.repeat(head_params[:, base + 1], HEAD_M)[None, :]
    conv = jnp.concatenate(rows + [skip, jnp.zeros((2, WIDTH), jnp.float32)], axis=0)
    bc = jnp.pad(conv_shared, ((0, 3), (0, 0)))
    heads = jnp.stack([jnp.exp(head_params[:, base]), head_params[:, base + 2]])
    heads = jnp.pad(heads, ((0, 6), (0, LANES - HEADS)))
    i = jnp.arange(LANES)
    sel = (i[:, None] == HEADS * tidx + i[None, :]) & (i[None, :] < HEADS)
    spread = i[:, None] == jnp.arange(WIDTH)[None, :] // HEAD_M
    half = HEAD_A // 2
    freq = THETA ** (-jnp.arange(half, dtype=jnp.float32) * 2.0 / HEAD_A)
    angle = pos.astype(jnp.float32)[:, None] * freq[None, :]
    cosine, sine = jnp.cos(angle), jnp.sin(angle)
    return (
        conv,
        bc,
        heads,
        sel.astype(jnp.float32),
        spread.astype(jnp.float32),
        pos[:, None],
        seg[:, None],
        seg[None, :],
        jnp.concatenate([cosine] * 4, axis=1),
        jnp.concatenate([-sine, sine, -sine, sine], axis=1),
    )


def mixer_forward(projected, consts):
    length = projected.shape[0]
    outs = [
        jax.ShapeDtypeStruct((length, WIDTH + QCOLS), jnp.bfloat16),
        jax.ShapeDtypeStruct((length, WIDTH), jnp.float32),
    ]
    return local_call(forward_kernel, outs, "mixer_forward")(projected, *consts)


def mixer_backward(projected, consts, outputs, grad):
    outs = [
        jax.ShapeDtypeStruct(projected.shape, jnp.bfloat16),
        jax.ShapeDtypeStruct((8, WIDTH), jnp.float32),
        jax.ShapeDtypeStruct((8, 2 * STATE), jnp.float32),
        jax.ShapeDtypeStruct((8, LANES), jnp.float32),
    ]
    grad_proj, conv, bc, heads = local_call(backward_kernel, outs, "mixer_backward")(
        projected, *consts, outputs, grad
    )
    cols = [conv[k].reshape(HEADS, HEAD_M) for k in range(CONV + 1)]
    skip = jnp.sum(conv[CONV + 1].reshape(HEADS, HEAD_M), axis=1, keepdims=True)
    head_grad = jnp.concatenate(
        cols + [heads[0, :HEADS, None], skip, heads[1, :HEADS, None]], axis=1
    )
    return grad_proj, head_grad, bc[: CONV + 1]


def swiglu(gate, upper):
    return jax.nn.silu(gate) * upper


def cross(left, right):
    return lax.dot_general(
        left, right, (((0,), (0,)), ((), ())), preferred_element_type=jnp.float32
    )


def dot(left, right):
    return jnp.dot(left, right, preferred_element_type=jnp.float32)


def dot_t(left, right):
    return lax.dot_general(
        left, right, (((1,), (1,)), ((), ())), preferred_element_type=jnp.float32
    )


def adamw(weight, first, second, grad, rate, decay):
    first = 0.9 * first + 0.1 * grad
    second = 0.95 * second + 0.05 * grad * grad
    fixed_one = first / (1.0 - 0.9**STEP)
    fixed_two = second / (1.0 - 0.95**STEP)
    weight = weight - rate * (fixed_one / (jnp.sqrt(fixed_two) + 1e-08) + decay * weight)
    return (first, second, weight)


def swap(values, axis, distance):
    count = lax.axis_size(axis)
    return lax.ppermute(values, axis, [(i, i ^ distance) for i in range(count)])


def pair_rows(own, other, tidx):
    return jnp.where(
        tidx == 0,
        jnp.concatenate([own, other], axis=0),
        jnp.concatenate([other, own], axis=0),
    )


def gather_rows(own, tidx):
    return pair_rows(own, swap(own, "tensor", 1), tidx)


def scatter_rows(partial, tidx):
    rows = partial.shape[0] // 2
    upper, lower = partial[:rows], partial[rows:]
    mine = jnp.where(tidx == 0, upper, lower)
    theirs = jnp.where(tidx == 0, lower, upper).astype(jnp.bfloat16)
    return mine + swap(theirs, "tensor", 1).astype(jnp.float32)


RING_CHIPS = 8


def ring_chip(place):
    place = place % RING_CHIPS
    half = RING_CHIPS // 2
    if isinstance(place, int):
        return 2 * place if place < half else 2 * (RING_CHIPS - 1 - place) + 1
    return jnp.where(place < half, 2 * place, 2 * (RING_CHIPS - 1 - place) + 1)


def ring_place(chip):
    return jnp.where(chip % 2 == 0, chip // 2, RING_CHIPS - 1 - chip // 2)


def ring_step(values):
    pairs = []
    for p in range(RING_CHIPS):
        pairs.append((CORES * ring_chip(p), CORES * ring_chip(p + 1)))
        pairs.append((CORES * ring_chip(p + 1) + 1, CORES * ring_chip(p) + 1))
    return lax.ppermute(values, "dp", pairs)


def place_rows(pieces, blocks):
    count = len(pieces)
    height, width = pieces[0].shape

    def kernel(block_ref, *refs):
        for i in range(count):
            start = pl.multiple_of(block_ref[i] * height, height)
            refs[count][pl.ds(start, height), :] = refs[i][...]

    return pl.pallas_call(
        kernel,
        out_shape=jax.ShapeDtypeStruct((count * height, width), pieces[0].dtype),
        in_specs=[pl.BlockSpec(memory_space=pltpu.SMEM)]
        + [pl.BlockSpec(memory_space=pltpu.VMEM)] * count,
        out_specs=pl.BlockSpec(memory_space=pltpu.VMEM),
        compiler_params=pltpu.CompilerParams(vmem_limit_bytes=40 * 2**20),
        name="place_rows",
    )(blocks, *pieces)


def ring_gather(shard, place, core):
    way = 1 - 2 * core
    own = [shard]
    other = [swap(shard, "dp", 1)]
    for _ in range(1, RING_CHIPS):
        own.append(ring_step(own[-1]))
        other.append(swap(own[-1], "dp", 1))
    blocks = [CORES * ring_chip(place - way * k) + core for k in range(RING_CHIPS)]
    blocks += [CORES * ring_chip(place + way * k) + 1 - core for k in range(RING_CHIPS)]
    return place_rows(own + other, jnp.stack(blocks).astype(jnp.int32)), own[2]


def ring_reduce(grad, place, core):
    rows = grad.shape[0] // RING_CHIPS
    way = 1 - 2 * core
    middle = grad.shape[1] // 2 // 128 * 128
    cuts = ((0, middle), (middle, grad.shape[1]))
    sums = [None] * len(cuts)
    for step in range(1, RING_CHIPS + 1):
        start = ring_chip(place - way * step) * rows
        for i, (a, b) in enumerate(cuts):
            part = lax.dynamic_slice(grad, (start, a), (rows, b - a))
            if step > 1:
                part = part + sums[i].astype(jnp.float32)
            if step < RING_CHIPS:
                part = ring_step(part.astype(jnp.bfloat16))
            sums[i] = part
        if step == 2:
            mark = sums[0]
    return jnp.concatenate(sums, axis=1), mark


def own_half(values, core):
    half = values.shape[1] // CORES
    left, right = values[:, :half], values[:, half:]
    return jnp.where(core == 0, left, right), jnp.where(core == 0, right, left)


def chip_grad(model_side, inner_side, core):
    keep, give = own_half(inner_side, core)
    return cross(model_side, keep) + cross(
        swap(model_side, "dp", 1), swap(give, "dp", 1)
    )


def own_rows(summed, core):
    rows = summed.shape[0] // CORES
    upper, lower = summed[:rows], summed[rows:]
    mine = jnp.where(core == 0, upper, lower)
    give = jnp.where(core == 0, lower, upper).astype(jnp.bfloat16)
    taken = swap(give, "dp", 1).astype(jnp.float32)
    return jnp.where(core == 0, mine, taken), jnp.where(core == 0, taken, mine)


def join_halves(halves, a, b):
    return jnp.concatenate([halves[0][:, a:b], halves[1][:, a:b]], axis=1)


def sum_all(values, axis):
    distance = 1
    while distance < lax.axis_size(axis):
        values = values + swap(values, axis, distance)
        distance *= 2
    return values


def per_device(
    residual,
    out_grad,
    doc_lengths,
    mixer_weight,
    mixer_first,
    mixer_second,
    scan_weight,
    scan_first,
    scan_second,
    merge_weight,
    merge_first,
    merge_second,
    hidden_weight,
    hidden_first,
    hidden_second,
    down_weight,
    down_first,
    down_second,
    head_params,
    head_first,
    head_second,
    shared_params,
    shared_first,
    shared_second,
):
    low = jnp.bfloat16
    tidx = lax.axis_index("tensor")
    count = lax.axis_size("dp")
    chips = count // CORES
    core = lax.axis_index("dp") % CORES
    place = ring_place(lax.axis_index("dp") // CORES)
    group = residual.shape[0] * lax.axis_size("tensor")
    seg, pos = doc_index(doc_lengths[0], group)
    conv_shared = shared_params[2 * D :].reshape(CONV + 1, 2 * STATE)

    ring = chips == RING_CHIPS
    mix_cols = mixer_weight.shape[1]
    both_cols = mix_cols + scan_weight.shape[1]
    spare = jnp.zeros((mixer_weight.shape[0], -both_cols % 256), low)
    first_shard = jnp.concatenate(
        [mixer_weight.astype(low), scan_weight.astype(low), spare], axis=1
    )
    rest_shard = jnp.concatenate(
        [hidden_weight.astype(low), down_weight.astype(low).T, merge_weight.astype(low).T],
        axis=1,
    )
    hidden_cols, down_cols = hidden_weight.shape[1], down_weight.shape[0]
    if ring:
        first_w, mark = ring_gather(first_shard, place, core)
        rest_shard = lax.optimization_barrier((rest_shard, mark))[0]
    else:
        first_w = lax.all_gather(first_shard, "dp", axis=0, tiled=True)
    rest_w = lax.all_gather(rest_shard, "dp", axis=0, tiled=True)
    hidden_w = rest_w[:, :hidden_cols]
    down_w = rest_w[:, hidden_cols : hidden_cols + down_cols]
    merge_w = rest_w[:, hidden_cols + down_cols :]

    consts = mixer_consts(head_params, conv_shared, seg, pos, tidx)
    normed_one, norm_back_one = jax.vjp(scaled_norm, residual, shared_params[:D])
    first_all = gather_rows(normed_one.astype(low), tidx)
    grad_feed = gather_rows(out_grad.astype(low), tidx)
    projected = dot(first_all, first_w).astype(low)
    joined_low, outputs = mixer_forward(projected, consts)
    middle = residual + scatter_rows(dot_t(joined_low, merge_w), tidx)
    normed_two, norm_back_two = jax.vjp(scaled_norm, middle, shared_params[D : 2 * D])
    second_all = gather_rows(normed_two.astype(low), tidx)
    gate_up = dot(second_all, hidden_w)
    units = gate_up.shape[1] // 2
    activ, swiglu_back = jax.vjp(swiglu, gate_up[:, :units], gate_up[:, units:])
    activ_low = activ.astype(low)
    block_out = middle + scatter_rows(dot_t(activ_low, down_w), tidx)

    grad_activ = dot(grad_feed, down_w)
    grad_gate, grad_upper = swiglu_back(grad_activ)
    grad_gu = jnp.concatenate([grad_gate, grad_upper], axis=1).astype(low)
    grad_second = scatter_rows(dot_t(grad_gu, hidden_w), tidx)
    grad_middle_part, gain_two_grad = norm_back_two(grad_second)
    grad_middle = out_grad + grad_middle_part
    grad_mixed = gather_rows(grad_middle.astype(low), tidx)
    grad_joined = dot(grad_mixed, merge_w)
    if ring:
        rest_grad = jnp.concatenate(
            [
                chip_grad(second_all, grad_gu, core),
                chip_grad(grad_feed, activ_low, core),
                chip_grad(grad_mixed, joined_low, core),
            ],
            axis=1,
        )
        rest_grad = rest_grad.astype(low)
        grad_joined, rest_grad = lax.optimization_barrier((grad_joined, rest_grad))
        rest_sum = lax.psum_scatter(
            rest_grad,
            "dp",
            scatter_dimension=0,
            axis_index_groups=[[i * CORES + c for i in range(chips)] for c in range(CORES)],
            tiled=True,
        )
    grad_proj, head_grad, conv_grad = mixer_backward(projected, consts, outputs, grad_joined)
    grad_first = scatter_rows(dot_t(grad_proj, first_w), tidx)
    grad_resid_part, gain_one_grad = norm_back_one(grad_first)
    input_grad = grad_middle + grad_resid_part

    shared_part = jnp.concatenate([gain_one_grad, gain_two_grad, conv_grad.reshape(-1)])
    small = jnp.concatenate([shared_part, head_grad.reshape(-1)])
    if ring:
        first_sum, mark = ring_reduce(chip_grad(first_all, grad_proj, core), place, core)
        small = lax.optimization_barrier((small, mark))[0]
        first_sum = join_halves(own_rows(first_sum, core), 0, first_sum.shape[1])
        rest_halves = own_rows(rest_sum.astype(jnp.float32), core)
        a, b = hidden_cols // CORES, (hidden_cols + down_cols) // CORES
        hidden_sum = join_halves(rest_halves, 0, a)
        down_sum = join_halves(rest_halves, a, b).T
        merge_sum = join_halves(rest_halves, b, rest_sum.shape[1]).T
    else:
        whole = jnp.concatenate(
            [
                cross(first_all, grad_proj),
                cross(second_all, grad_gu),
                cross(grad_feed, activ_low),
                cross(grad_mixed, joined_low),
            ],
            axis=1,
        ).astype(low)
        whole = lax.psum_scatter(whole, "dp", scatter_dimension=0, tiled=True)
        whole = whole.astype(jnp.float32)
        a = grad_proj.shape[1]
        first_sum = whole[:, :a]
        hidden_sum = whole[:, a : a + hidden_cols]
        a = a + hidden_cols
        down_sum = whole[:, a : a + down_cols].T
        merge_sum = whole[:, a + down_cols :].T
    mixer_sum, scan_sum = first_sum[:, :mix_cols], first_sum[:, mix_cols:both_cols]
    scan_sum = scan_sum + swap(scan_sum, "tensor", 1)

    small = sum_all(small, "dp")
    split = shared_part.shape[0]
    shared_sum = sum_all(small[:split], "tensor")
    head_sum = small[split:].reshape(head_grad.shape)

    mixer_new = adamw(mixer_weight, mixer_first, mixer_second, mixer_sum, 0.02, 0.1)
    scan_new = adamw(scan_weight, scan_first, scan_second, scan_sum, 0.02, 0.1)
    merge_new = adamw(merge_weight, merge_first, merge_second, merge_sum, 0.02, 0.1)
    hidden_new = adamw(hidden_weight, hidden_first, hidden_second, hidden_sum, 0.02, 0.1)
    down_new = adamw(down_weight, down_first, down_second, down_sum, 0.02, 0.1)
    head_new = adamw(head_params, head_first, head_second, head_sum, 0.2, 0.0)
    shared_new = adamw(shared_params, shared_first, shared_second, shared_sum, 0.2, 0.0)
    return (
        block_out,
        input_grad,
        *mixer_new,
        *scan_new,
        *merge_new,
        *hidden_new,
        *down_new,
        *head_new,
        *shared_new,
    )


def solution(mesh):
    return jax.shard_map(
        per_device,
        mesh=mesh,
        in_specs=(
            P(("dp", "tensor"), None),
            P(("dp", "tensor"), None),
            P("dp", None),
            P("dp", "tensor"),
            P("dp", "tensor"),
            P("dp", "tensor"),
            P("dp", None),
            P("dp", None),
            P("dp", None),
            P("tensor", "dp"),
            P("tensor", "dp"),
            P("tensor", "dp"),
            P("dp", "tensor"),
            P("dp", "tensor"),
            P("dp", "tensor"),
            P("tensor", "dp"),
            P("tensor", "dp"),
            P("tensor", "dp"),
            P("tensor", None),
            P("tensor", None),
            P("tensor", None),
            P(),
            P(),
            P(),
        ),
        out_specs=(
            P(("dp", "tensor"), None),
            P(("dp", "tensor"), None),
            P("dp", "tensor"),
            P("dp", "tensor"),
            P("dp", "tensor"),
            P("dp", None),
            P("dp", None),
            P("dp", None),
            P("tensor", "dp"),
            P("tensor", "dp"),
            P("tensor", "dp"),
            P("dp", "tensor"),
            P("dp", "tensor"),
            P("dp", "tensor"),
            P("tensor", "dp"),
            P("tensor", "dp"),
            P("tensor", "dp"),
            P("tensor", None),
            P("tensor", None),
            P("tensor", None),
            P(),
            P(),
            P(),
        ),
        check_vma=False,
    )
```

```python
import jax
import jax.numpy as jnp
from jax import lax
from jax.experimental import pallas as pl
from jax.experimental.pallas import tpu as pltpu
from jax.sharding import PartitionSpec as P

D = 1024
HEADS_M = 24
HEAD_M = 64
STATE = 128
CONV = 4
HEADS_Q = 8
HEADS_KV = 2
HEAD_A = 64
STEP = 10
CORES = 2


EPS = 1e-05
THETA = 10000.0
HIGH = lax.Precision.HIGHEST


def scaled_norm(values, gain):
    return values * lax.rsqrt(jnp.mean(values * values, axis=-1, keepdims=True) + EPS) * gain


def doc_index(lens, count):
    place = jnp.arange(count, dtype=jnp.int32)
    ends = jnp.cumsum(lens)
    after = place[:, None] >= ends[None, :]
    seg = jnp.sum(after.astype(jnp.int32), axis=1)
    start = jnp.sum(jnp.where(after, lens[None, :], 0), axis=1)
    return (seg, place - start)


HEADS = HEADS_M // 2
WIDTH = HEADS * HEAD_M
QCOLS = HEADS_Q // 2 * HEAD_A
LANES = 128
RATE_COL = (CONV + 1) * HEAD_M
SKIP_COL = RATE_COL + 1
BIAS_COL = RATE_COL + 2


def exact_dot(left, right, dims=((1,), (0,))):
    return lax.dot_general(
        left, right, (dims, ((), ())), precision=HIGH, preferred_element_type=jnp.float32
    )


def low_dot(left, right, dims=((1,), (0,))):
    return lax.dot_general(
        left.astype(jnp.bfloat16),
        right.astype(jnp.bfloat16),
        (dims, ((), ())),
        preferred_element_type=jnp.float32,
    )


ROWS = ((0,), (0,))
COLS = ((1,), (1,))


def lane_of(shape):
    return lax.broadcasted_iota(jnp.int32, shape, 1)


def shifted(values, pos, shift):
    return jnp.where(pos >= shift, pltpu.roll(values, shift, 0), 0.0)


def conv_forward(values, rows, pos):
    total = rows[CONV : CONV + 1] + rows[CONV - 1 : CONV] * values
    for shift in range(1, CONV):
        tap = rows[CONV - 1 - shift : CONV - shift]
        total = total + tap * shifted(values, pos, shift)
    return total


def conv_backward(grad, values, rows, pos):
    length = values.shape[0]
    back = rows[CONV - 1 : CONV] * grad
    taps = [jnp.sum(grad * values, axis=0, keepdims=True)]
    for shift in range(1, CONV):
        tap = rows[CONV - 1 - shift : CONV - shift]
        kept = jnp.where(pos >= shift, grad, 0.0)
        back = back + tap * pltpu.roll(kept, length - shift, 0)
        taps.append(jnp.sum(kept * pltpu.roll(values, shift, 0), axis=0, keepdims=True))
    return back, taps[::-1] + [jnp.sum(grad, axis=0, keepdims=True)]


def swap_pairs(values):
    first = lane_of(values.shape) % HEAD_A < HEAD_A // 2
    half = HEAD_A // 2
    return jnp.where(first, pltpu.roll(values, LANES - half, 1), pltpu.roll(values, half, 1))


def turn(values, cosine, sine):
    return values * cosine + swap_pairs(values) * sine


def turn_back(values, cosine, sine):
    return values * cosine + swap_pairs(values * sine)


def half_lanes(values, which):
    mine = lane_of(values.shape) // HEAD_A == which
    return jnp.where(mine, values, jnp.zeros_like(values))


def column_to_lanes(column):
    shape = (column.shape[0], LANES)
    row = lax.broadcasted_iota(jnp.int32, shape, 0)
    mine = (row == lane_of(shape)) & (row < HEADS)
    return jnp.sum(jnp.where(mine, column, 0.0), axis=0, keepdims=True)


def conv_rows(heads_ref):
    tiles = [heads_ref[:, j * LANES : (j + 1) * LANES] for j in range(3)]
    rolled = [pltpu.roll(tile, HEAD_M, 1) for tile in tiles]
    left = lane_of((1, LANES)) < HEAD_M
    rows = []
    for k in range(CONV + 1):
        kinds = (tiles[k // 2], rolled[k // 2])
        even, odd = kinds[k % 2], kinds[1 - k % 2]
        pieces = [
            jnp.where(left, even[h : h + 1], odd[h + 1 : h + 2]) for h in range(0, HEADS, 2)
        ]
        rows.append(jnp.concatenate(pieces, axis=1))
    skip = heads_ref[:, SKIP_COL : SKIP_COL + 1]
    pieces = [jnp.where(left, skip[h : h + 1], skip[h + 1 : h + 2]) for h in range(0, HEADS, 2)]
    rows.append(jnp.concatenate(pieces, axis=1))
    return jnp.concatenate(rows + [jnp.zeros((2, WIDTH), jnp.float32)], axis=0)


def head_rows(rows, dlog, dbias):
    left = lane_of((1, LANES)) < HEAD_M
    lane = lane_of((1, LANES))
    out = []
    for i in range(HEADS // 2):
        tile = rows[:, i * LANES : (i + 1) * LANES]
        kinds = (tile, pltpu.roll(tile, HEAD_M, 1))
        for which in range(2):
            h = 2 * i + which
            piece = [kinds[(which + k) % 2][k : k + 1] for k in range(CONV + 1)]
            dskip = jnp.sum(
                half_lanes(tile[CONV + 1 : CONV + 2], which), axis=1, keepdims=True
            )
            last = jnp.where(lane == HEAD_M, dlog[:, h : h + 1], 0.0)
            last = jnp.where(lane == HEAD_M + 1, dskip, last)
            last = jnp.where(lane == HEAD_M + 2, dbias[:, h : h + 1], last)
            tiles = [
                jnp.where(left, piece[0], piece[1]),
                jnp.where(left, piece[2], piece[3]),
                jnp.where(left, piece[4], last),
            ]
            out.append(jnp.concatenate(tiles, axis=1))
    out.append(jnp.zeros((16 - HEADS, 3 * LANES), jnp.float32))
    return jnp.concatenate(out, axis=0)


def documents(lens_ref, place):
    seg, start, end = jnp.zeros_like(place), jnp.zeros_like(place), 0
    for k in range(lens_ref.shape[0]):
        end = end + lens_ref[k]
        after = place >= end
        seg = seg + jnp.where(after, 1, 0)
        start = start + jnp.where(after, lens_ref[k], 0)
    return seg, place - start


def mixer_parts(tidx_ref, lens_ref, p_ref, heads_ref, bc_ref):
    length = p_ref.shape[0]
    base = 2 * WIDTH + QCOLS + 2 * HEAD_A
    conv = conv_rows(heads_ref)
    bc = bc_ref[...]
    row = lax.broadcasted_iota(jnp.int32, (length, length), 0)
    column = lax.broadcasted_iota(jnp.int32, (length, length), 1)
    seg, pos = documents(lens_ref, lax.broadcasted_iota(jnp.int32, (length, 1), 0))
    seg_across, _ = documents(lens_ref, lax.broadcasted_iota(jnp.int32, (1, length), 1))
    same = (seg == seg_across) & (row >= column)
    wide = p_ref[:, WIDTH : 2 * WIDTH].astype(jnp.float32)
    chans_pre = conv_forward(wide, conv, pos)
    chans_sig = jax.nn.sigmoid(chans_pre)
    states = p_ref[:, base : base + 2 * STATE].astype(jnp.float32)
    states_pre = conv_forward(states, bc, pos)
    states_sig = jax.nn.sigmoid(states_pre)
    raw = p_ref[:, base + 2 * STATE : base + 2 * STATE + LANES].astype(jnp.float32)
    i = lax.broadcasted_iota(jnp.int32, (LANES, LANES), 0)
    j = lane_of((LANES, LANES))
    sel = ((i == HEADS * tidx_ref[0] + j) & (j < HEADS)).astype(jnp.float32)
    i = lax.broadcasted_iota(jnp.int32, (LANES, WIDTH), 0)
    spread = (i == lane_of((LANES, WIDTH)) // HEAD_M).astype(jnp.float32)
    rates = column_to_lanes(jnp.exp(heads_ref[:, RATE_COL : RATE_COL + 1]))
    bias = column_to_lanes(heads_ref[:, BIAS_COL : BIAS_COL + 1])
    step_pre = exact_dot(raw, sel) + bias
    steps = jnp.maximum(step_pre, 0.0) + jnp.log1p(jnp.exp(-jnp.abs(step_pre)))
    before = (row >= column).astype(jnp.float32)
    cum = exact_dot(before, -rates * steps)
    steps_wide = exact_dot(steps, spread)
    chans = chans_pre * chans_sig
    states_out = states_pre * states_sig
    in_state, out_state = states_out[:, :STATE], states_out[:, STATE:]
    inner = jnp.where(same, exact_dot(out_state, in_state, COLS), 0.0)
    return dict(
        pos=pos, wide=wide, chans_pre=chans_pre, chans_sig=chans_sig, chans=chans,
        states=states, states_pre=states_pre, states_sig=states_sig, in_state=in_state,
        out_state=out_state, step_pre=step_pre, steps=steps, rates=rates, before=before,
        cum=cum, cum_t=cum.T, same=same, steps_wide=steps_wide, inner=inner, conv=conv, bc=bc,
        sel=sel, spread=spread, weighted=(steps_wide * chans).astype(jnp.bfloat16),
    )


def decay_of(parts, head):
    gap = parts["cum"][:, head : head + 1] - parts["cum_t"][head : head + 1, :]
    return jnp.exp(jnp.minimum(gap, 0.0))


def attention_parts(p_ref, cos_ref, sin_ref):
    cosine, sine = cos_ref[...], sin_ref[...]
    pairs = []
    for i in range(QCOLS // LANES):
        a = 2 * WIDTH + i * LANES
        query = turn(p_ref[:, a : a + LANES].astype(jnp.float32), cosine, sine)
        pairs.append((query * HEAD_A ** (-0.5)).astype(jnp.bfloat16))
    a = 2 * WIDTH + QCOLS
    both = p_ref[:, a : a + LANES].astype(jnp.float32)
    key = half_lanes(turn(both, cosine, sine), 0)
    value = half_lanes(both, 1)
    keys = (key.astype(jnp.bfloat16), pltpu.roll(key, HEAD_A, 1).astype(jnp.bfloat16))
    values = (pltpu.roll(value, HEAD_A, 1).astype(jnp.bfloat16), value.astype(jnp.bfloat16))
    return pairs, keys, values


def attention_probs(query, key, same):
    scores = jnp.where(same, low_dot(query, key, COLS), -1e30)
    top = jnp.max(scores, axis=1, keepdims=True)
    raised = jnp.exp(scores - top)
    return raised / jnp.sum(raised, axis=1, keepdims=True)


def forward_kernel(
    tidx_ref, lens_ref, p_ref, heads_ref, bc_ref, cos_ref, sin_ref, cat_ref, y_ref
):
    parts = mixer_parts(tidx_ref, lens_ref, p_ref, heads_ref, bc_ref)
    for i in range(WIDTH // LANES):
        a = i * LANES
        tile = parts["weighted"][:, a : a + LANES]
        out = jnp.zeros((p_ref.shape[0], LANES), jnp.float32)
        for which in range(2):
            mixed = decay_of(parts, 2 * i + which) * parts["inner"]
            out = out + low_dot(mixed, half_lanes(tile, which))
        y_ref[:, a : a + LANES] = out
        gate = p_ref[:, a : a + LANES].astype(jnp.float32)
        out = out + parts["conv"][CONV + 1 : CONV + 2, a : a + LANES] * parts["chans"][:, a : a + LANES]
        cat_ref[:, a : a + LANES] = (out * gate * jax.nn.sigmoid(gate)).astype(cat_ref.dtype)
    pairs, keys, values = attention_parts(p_ref, cos_ref, sin_ref)
    for i, query in enumerate(pairs):
        out = jnp.zeros((p_ref.shape[0], LANES), jnp.float32)
        for which in range(2):
            probs = attention_probs(query, keys[which], parts["same"])
            out = out + low_dot(probs, values[which])
        a = WIDTH + i * LANES
        cat_ref[:, a : a + LANES] = out.astype(cat_ref.dtype)


def backward_kernel(
    tidx_ref, lens_ref, p_ref, heads_ref, bc_ref, cos_ref, sin_ref, y_ref, grad_ref,
    dp_ref, dheads_ref, dbc_ref,
):
    length = p_ref.shape[0]
    low = dp_ref.dtype
    parts = mixer_parts(tidx_ref, lens_ref, p_ref, heads_ref, bc_ref)
    pos, chans = parts["pos"], parts["chans"]
    gate = p_ref[:, :WIDTH].astype(jnp.float32)
    gate_sig = jax.nn.sigmoid(gate)
    grad = grad_ref[:, :WIDTH]
    skip = parts["conv"][CONV + 1 : CONV + 2]
    outputs = y_ref[...]
    dgate = grad * (outputs + skip * chans) * gate_sig * (1.0 + gate * (1.0 - gate_sig))
    dp_ref[:, :WIDTH] = dgate.astype(low)
    dy = grad * gate * gate_sig
    dy_low = dy.astype(jnp.bfloat16)
    dweighted = []
    dinner = jnp.zeros((length, length), jnp.float32)
    for i in range(WIDTH // LANES):
        a = i * LANES
        tile = parts["weighted"][:, a : a + LANES]
        out = jnp.zeros((length, LANES), jnp.float32)
        for which in range(2):
            decay = decay_of(parts, 2 * i + which)
            dy_half = half_lanes(dy_low[:, a : a + LANES], which)
            out = out + low_dot(decay * parts["inner"], dy_half, ROWS)
            dinner = dinner + low_dot(dy_half, tile, COLS) * decay
        dweighted.append(out)
    dweighted = jnp.concatenate(dweighted, axis=1)
    spread = parts["spread"]
    weighted = parts["weighted"].astype(jnp.float32)
    dcum = exact_dot(dy_low.astype(jnp.float32) * outputs - weighted * dweighted, spread, COLS)
    dsteps = exact_dot(dweighted * chans, spread, COLS)
    dchans = skip * dy + parts["steps_wide"] * dweighted
    drate = exact_dot(parts["before"], dcum, ROWS)
    dsteps = (dsteps - parts["rates"] * drate) * jax.nn.sigmoid(parts["step_pre"])
    dlog = jnp.sum(-parts["rates"] * parts["steps"] * drate, axis=0, keepdims=True)
    dbias = jnp.sum(dsteps, axis=0, keepdims=True)
    base = 2 * WIDTH + QCOLS + 2 * HEAD_A
    draw = exact_dot(dsteps, parts["sel"], COLS)
    dp_ref[:, base + 2 * STATE :] = draw.astype(low)

    sig, pre = parts["chans_sig"], parts["chans_pre"]
    dpre = dchans * sig * (1.0 + pre * (1.0 - sig))
    back, rows = conv_backward(dpre, parts["wide"], parts["conv"], pos)
    dp_ref[:, WIDTH : 2 * WIDTH] = back.astype(low)
    rows.append(jnp.sum(dy * chans, axis=0, keepdims=True))
    rows = jnp.concatenate(rows + [jnp.zeros((2, WIDTH), jnp.float32)], axis=0)
    dheads_ref[...] = head_rows(rows, dlog, dbias)

    dinner = jnp.where(parts["same"], dinner, 0.0)
    dstates = jnp.concatenate(
        [exact_dot(dinner, parts["out_state"], ROWS), exact_dot(dinner, parts["in_state"])],
        axis=1,
    )
    sig, pre = parts["states_sig"], parts["states_pre"]
    dpre = dstates * sig * (1.0 + pre * (1.0 - sig))
    back, rows = conv_backward(dpre, parts["states"], parts["bc"], pos)
    dp_ref[:, base : base + 2 * STATE] = back.astype(low)
    dbc_ref[...] = jnp.concatenate(rows, axis=0)

    pairs, keys, values = attention_parts(p_ref, cos_ref, sin_ref)
    cosine, sine = cos_ref[...], sin_ref[...]
    dkeys = [jnp.zeros((length, LANES), jnp.float32) for _ in range(2)]
    dvalues = [jnp.zeros((length, LANES), jnp.float32) for _ in range(2)]
    for i, query in enumerate(pairs):
        a = WIDTH + i * LANES
        datt = grad_ref[:, a : a + LANES].astype(jnp.bfloat16)
        dquery = jnp.zeros((length, LANES), jnp.float32)
        for which in range(2):
            probs = attention_probs(query, keys[which], parts["same"])
            dprobs = low_dot(datt, values[which], COLS)
            dscores = probs * (dprobs - jnp.sum(probs * dprobs, axis=1, keepdims=True))
            dscores = dscores.astype(jnp.bfloat16)
            dquery = dquery + low_dot(dscores, keys[which])
            dkeys[which] = dkeys[which] + low_dot(dscores, query, ROWS)
            dvalues[which] = dvalues[which] + low_dot(probs, datt, ROWS)
        a = 2 * WIDTH + i * LANES
        dquery = turn_back(dquery * HEAD_A ** (-0.5), cosine, sine)
        dp_ref[:, a : a + LANES] = dquery.astype(low)
    dkey = half_lanes(dkeys[0], 0) + pltpu.roll(half_lanes(dkeys[1], 1), HEAD_A, 1)
    dvalue = pltpu.roll(half_lanes(dvalues[0], 0), HEAD_A, 1) + half_lanes(dvalues[1], 1)
    a = 2 * WIDTH + QCOLS
    dboth = half_lanes(turn_back(dkey, cosine, sine), 0) + dvalue
    dp_ref[:, a : a + LANES] = dboth.astype(low)


def local_call(kernel, outs, name, scalars=0):
    space = pl.BlockSpec(memory_space=pltpu.VMEM)
    scalar = pl.BlockSpec(memory_space=pltpu.SMEM)
    return lambda *args: pl.pallas_call(
        kernel,
        out_shape=[jax.ShapeDtypeStruct(shape, dtype) for shape, dtype in outs],
        in_specs=[scalar] * scalars + [space] * (len(args) - scalars),
        out_specs=[space] * len(outs),
        compiler_params=pltpu.CompilerParams(vmem_limit_bytes=56 * 2**20),
        name=name,
    )(*args)


def mixer_consts(head_params, conv_shared, lens, tidx, length):
    _, pos = doc_index(lens, length)
    half = HEAD_A // 2
    freq = THETA ** (-jnp.arange(half, dtype=jnp.float32) * 2.0 / HEAD_A)
    angle = pos.astype(jnp.float32)[:, None] * freq[None, :]
    cosine, sine = jnp.cos(angle), jnp.sin(angle)
    heads = jnp.pad(
        head_params, ((0, 16 - HEADS), (0, 3 * LANES - head_params.shape[1]))
    )
    scalars = (jnp.reshape(tidx, (1,)).astype(jnp.int32), lens)
    return scalars, (
        heads,
        conv_shared,
        jnp.concatenate([cosine] * 4, axis=1),
        jnp.concatenate([-sine, sine, -sine, sine], axis=1),
    )


def mixer_forward(projected, consts):
    length = projected.shape[0]
    outs = [((length, WIDTH + QCOLS), jnp.bfloat16), ((length, WIDTH), jnp.float32)]
    scalars, arrays = consts
    return local_call(forward_kernel, outs, "mixer_forward", 2)(*scalars, projected, *arrays)


def mixer_backward(projected, consts, outputs, grad):
    outs = [
        (projected.shape, jnp.bfloat16),
        ((16, 3 * LANES), jnp.float32),
        ((CONV + 1, 2 * STATE), jnp.float32),
    ]
    scalars, arrays = consts
    grad_proj, heads, bc = local_call(backward_kernel, outs, "mixer_backward", 2)(
        *scalars, projected, *arrays, outputs, grad
    )
    return grad_proj, heads[:HEADS, : BIAS_COL + 1], bc


def feed_kernel(x_ref, grad_ref, w_ref, act_ref, dgu_ref, dx_ref):
    units = act_ref.shape[1]
    gate_up = dot(x_ref[...], w_ref[:, : 2 * units])
    gate, upper = gate_up[:, :units], gate_up[:, units:]
    sig = jax.nn.sigmoid(gate)
    raised = gate * sig
    act_ref[...] = (raised * upper).astype(act_ref.dtype)
    grad = dot(grad_ref[...], w_ref[:, 2 * units : 3 * units])
    dgate = grad * upper * sig * (1.0 + gate * (1.0 - sig))
    dgu_ref[:, :units] = dgate.astype(dgu_ref.dtype)
    dgu_ref[:, units:] = (grad * raised).astype(dgu_ref.dtype)
    dx_ref[...] = dot_t(dgu_ref[...], w_ref[:, : 2 * units])


def feed_forward_back(values, grad, weight, units):
    length, width = values.shape
    outs = [
        ((length, units), jnp.bfloat16),
        ((length, 2 * units), jnp.bfloat16),
        ((length, width), jnp.float32),
    ]
    return local_call(feed_kernel, outs, "feed_forward_back")(values, grad, weight)


def weight_grads(sides, dtype):
    width = sum(side[1].shape[1] for side in sides)
    model = sides[0][0].shape[1]
    block = 256

    def kernel(*refs):
        out_ref, a = refs[-1], 0
        for i in range(len(sides)):
            x, y, other_x, other_y = refs[4 * i : 4 * i + 4]
            b = a + y.shape[1]
            for r in range(0, model, block):
                part = cross(x[:, r : r + block], y[...])
                part = part + cross(other_x[:, r : r + block], other_y[...])
                out_ref[r : r + block, a:b] = part.astype(out_ref.dtype)
            a = b

    flat = [value for side in sides for value in side]
    return local_call(kernel, [((model, width), dtype)], "weight_grads")(*flat)[0]


def cross(left, right):
    return lax.dot_general(
        left, right, (((0,), (0,)), ((), ())), preferred_element_type=jnp.float32
    )


def dot(left, right):
    return jnp.dot(left, right, preferred_element_type=jnp.float32)


def dot_t(left, right):
    return lax.dot_general(
        left, right, (((1,), (1,)), ((), ())), preferred_element_type=jnp.float32
    )


def adamw(weight, first, second, grad, rate, decay):
    first = 0.9 * first + 0.1 * grad
    second = 0.95 * second + 0.05 * grad * grad
    fixed_one = first / (1.0 - 0.9**STEP)
    fixed_two = second / (1.0 - 0.95**STEP)
    weight = weight - rate * (fixed_one / (jnp.sqrt(fixed_two) + 1e-08) + decay * weight)
    return (first, second, weight)


def swap(values, axis, distance):
    count = lax.axis_size(axis)
    return lax.ppermute(values, axis, [(i, i ^ distance) for i in range(count)])


def pair_rows(own, other, tidx):
    return jnp.where(
        tidx == 0,
        jnp.concatenate([own, other], axis=0),
        jnp.concatenate([other, own], axis=0),
    )


def gather_rows(own, tidx):
    return pair_rows(own, swap(own, "tensor", 1), tidx)


def scatter_rows(partial, tidx):
    rows = partial.shape[0] // 2
    upper, lower = partial[:rows], partial[rows:]
    mine = jnp.where(tidx == 0, upper, lower)
    theirs = jnp.where(tidx == 0, lower, upper).astype(jnp.bfloat16)
    return mine + swap(theirs, "tensor", 1).astype(jnp.float32)


RING_CHIPS = 8


def ring_chip(place):
    place = place % RING_CHIPS
    half = RING_CHIPS // 2
    if isinstance(place, int):
        return 2 * place if place < half else 2 * (RING_CHIPS - 1 - place) + 1
    return jnp.where(place < half, 2 * place, 2 * (RING_CHIPS - 1 - place) + 1)


def ring_place(chip):
    return jnp.where(chip % 2 == 0, chip // 2, RING_CHIPS - 1 - chip // 2)


def ring_step(values):
    pairs = []
    for p in range(RING_CHIPS):
        pairs.append((CORES * ring_chip(p), CORES * ring_chip(p + 1)))
        pairs.append((CORES * ring_chip(p + 1) + 1, CORES * ring_chip(p) + 1))
    return lax.ppermute(values, "dp", pairs)


def place_rows(pieces, blocks, values=None, columns=0):
    count = len(pieces)
    height, width = pieces[0].shape
    low = pieces[0].dtype
    extra = [] if values is None else [values]

    def kernel(block_ref, *refs):
        out_ref = refs[count + len(extra)]
        for i in range(count):
            start = pl.multiple_of(block_ref[i] * height, height)
            out_ref[pl.ds(start, height), :] = refs[i][...]
        if extra:
            refs[-1][...] = dot(refs[count][...], out_ref[:, :columns]).astype(low)

    outs = [((count * height, width), low)]
    if extra:
        outs.append(((values.shape[0], columns), low))
    return local_call(kernel, outs, "place_rows", 1)(blocks, *pieces, *extra)


def ring_gather(shard, place, core):
    way = 1 - 2 * core
    own = [shard]
    other = [swap(shard, "dp", 1)]
    for _ in range(1, RING_CHIPS):
        own.append(ring_step(own[-1]))
        other.append(swap(own[-1], "dp", 1))
    blocks = [CORES * ring_chip(place - way * k) + core for k in range(RING_CHIPS)]
    blocks += [CORES * ring_chip(place + way * k) + 1 - core for k in range(RING_CHIPS)]
    return own + other, jnp.stack(blocks).astype(jnp.int32), own


def ring_reduce(grad, place, core):
    rows = grad.shape[0] // RING_CHIPS
    way = 1 - 2 * core
    middle = grad.shape[1] // 2 // 128 * 128
    cuts = ((0, middle), (middle, grad.shape[1]))
    sums = [None] * len(cuts)
    for step in range(1, RING_CHIPS + 1):
        start = ring_chip(place - way * step) * rows
        for i, (a, b) in enumerate(cuts):
            part = lax.dynamic_slice(grad, (start, a), (rows, b - a))
            if step > 1:
                part = part + sums[i].astype(jnp.float32)
            if step < RING_CHIPS:
                part = ring_step(part.astype(jnp.bfloat16))
            sums[i] = part
        if step == 2:
            mark = sums[0]
    return jnp.concatenate(sums, axis=1), mark


def own_half(values, core):
    half = values.shape[1] // CORES
    left, right = values[:, :half], values[:, half:]
    return jnp.where(core == 0, left, right), jnp.where(core == 0, right, left)


def both_cores(model_side, inner_side, core):
    keep, give = own_half(inner_side, core)
    return model_side, keep, swap(model_side, "dp", 1), swap(give, "dp", 1)


def own_rows(summed, core):
    rows = summed.shape[0] // CORES
    upper, lower = summed[:rows], summed[rows:]
    mine = jnp.where(core == 0, upper, lower)
    give = jnp.where(core == 0, lower, upper).astype(jnp.bfloat16)
    taken = swap(give, "dp", 1).astype(jnp.float32)
    return jnp.where(core == 0, mine, taken), jnp.where(core == 0, taken, mine)


def join_halves(halves, a, b):
    return jnp.concatenate([halves[0][:, a:b], halves[1][:, a:b]], axis=1)


def sum_all(values, axis):
    distance = 1
    while distance < lax.axis_size(axis):
        values = values + swap(values, axis, distance)
        distance *= 2
    return values


def per_device(
    residual,
    out_grad,
    doc_lengths,
    mixer_weight,
    mixer_first,
    mixer_second,
    scan_weight,
    scan_first,
    scan_second,
    merge_weight,
    merge_first,
    merge_second,
    hidden_weight,
    hidden_first,
    hidden_second,
    down_weight,
    down_first,
    down_second,
    head_params,
    head_first,
    head_second,
    shared_params,
    shared_first,
    shared_second,
):
    low = jnp.bfloat16
    tidx = lax.axis_index("tensor")
    count = lax.axis_size("dp")
    chips = count // CORES
    core = lax.axis_index("dp") % CORES
    place = ring_place(lax.axis_index("dp") // CORES)
    group = residual.shape[0] * lax.axis_size("tensor")
    conv_shared = shared_params[2 * D :].reshape(CONV + 1, 2 * STATE)

    ring = chips == RING_CHIPS
    mix_cols = mixer_weight.shape[1]
    both_cols = mix_cols + scan_weight.shape[1]
    spare = jnp.zeros((mixer_weight.shape[0], -both_cols % 256), low)
    first_cols = both_cols + spare.shape[1]
    units = down_weight.shape[0]
    first_shard = jnp.concatenate(
        [mixer_weight.astype(low), scan_weight.astype(low), spare, merge_weight.astype(low).T],
        axis=1,
    )
    rest_shard = jnp.concatenate(
        [hidden_weight.astype(low), down_weight.astype(low).T], axis=1
    )
    consts = mixer_consts(head_params, conv_shared, doc_lengths[0], tidx, group)
    normed_one, norm_back_one = jax.vjp(scaled_norm, residual, shared_params[:D])
    first_all = gather_rows(normed_one.astype(low), tidx)
    grad_feed = gather_rows(out_grad.astype(low), tidx)
    if ring:
        pieces, blocks, own = ring_gather(first_shard, place, core)
        first_w, projected = place_rows(pieces, blocks, first_all, first_cols)
        rest_shard = lax.optimization_barrier((rest_shard, own[5]))[0]
        pieces, blocks, _ = ring_gather(rest_shard, place, core)
        rest_w = place_rows(pieces, blocks)[0]
    else:
        first_w = lax.all_gather(first_shard, "dp", axis=0, tiled=True)
        rest_w = lax.all_gather(rest_shard, "dp", axis=0, tiled=True)
        projected = dot(first_all, first_w[:, :first_cols]).astype(low)
    merge_w = first_w[:, first_cols:]
    joined_low, outputs = mixer_forward(projected, consts)
    middle = residual + scatter_rows(dot_t(joined_low, merge_w), tidx)
    normed_two, norm_back_two = jax.vjp(scaled_norm, middle, shared_params[D : 2 * D])
    second_all = gather_rows(normed_two.astype(low), tidx)
    activ_low, grad_gu, grad_second = feed_forward_back(second_all, grad_feed, rest_w, units)
    grad_second = scatter_rows(grad_second, tidx)
    block_out = middle + scatter_rows(dot_t(activ_low, rest_w[:, 2 * units :]), tidx)
    grad_middle_part, gain_two_grad = norm_back_two(grad_second)
    grad_middle = out_grad + grad_middle_part
    grad_mixed = gather_rows(grad_middle.astype(low), tidx)
    grad_joined = dot(grad_mixed, merge_w)
    if ring:
        rest_grad = weight_grads(
            [both_cores(second_all, grad_gu, core), both_cores(grad_feed, activ_low, core)], low
        )
        grad_joined, rest_grad = lax.optimization_barrier((grad_joined, rest_grad))
        rest_sum = lax.psum_scatter(
            rest_grad,
            "dp",
            scatter_dimension=0,
            axis_index_groups=[[i * CORES + c for i in range(chips)] for c in range(CORES)],
            tiled=True,
        )
    grad_proj, head_grad, conv_grad = mixer_backward(projected, consts, outputs, grad_joined)
    grad_first = scatter_rows(dot_t(grad_proj, first_w[:, :first_cols]), tidx)
    grad_resid_part, gain_one_grad = norm_back_one(grad_first)
    input_grad = grad_middle + grad_resid_part

    shared_part = jnp.concatenate([gain_one_grad, gain_two_grad, conv_grad.reshape(-1)])
    small = jnp.concatenate([shared_part, head_grad.reshape(-1)])
    if ring:
        first_grad = weight_grads(
            [both_cores(first_all, grad_proj, core), both_cores(grad_mixed, joined_low, core)],
            jnp.float32,
        )
        first_sum, mark = ring_reduce(first_grad, place, core)
        small = lax.optimization_barrier((small, mark))[0]
        first_halves = own_rows(first_sum, core)
        a = first_cols // CORES
        merge_sum = join_halves(first_halves, a, first_sum.shape[1]).T
        first_sum = join_halves(first_halves, 0, a)
        rest_halves = own_rows(rest_sum.astype(jnp.float32), core)
        hidden_sum = join_halves(rest_halves, 0, units)
        down_sum = join_halves(rest_halves, units, rest_sum.shape[1]).T
    else:
        whole = jnp.concatenate(
            [
                cross(first_all, grad_proj),
                cross(second_all, grad_gu),
                cross(grad_feed, activ_low),
                cross(grad_mixed, joined_low),
            ],
            axis=1,
        ).astype(low)
        whole = lax.psum_scatter(whole, "dp", scatter_dimension=0, tiled=True)
        whole = whole.astype(jnp.float32)
        a = grad_proj.shape[1]
        first_sum = whole[:, :a]
        hidden_sum = whole[:, a : a + 2 * units]
        a = a + 2 * units
        down_sum = whole[:, a : a + units].T
        merge_sum = whole[:, a + units :].T
    mixer_sum, scan_sum = first_sum[:, :mix_cols], first_sum[:, mix_cols:both_cols]
    scan_sum = scan_sum + swap(scan_sum, "tensor", 1)

    small = sum_all(small, "dp")
    split = shared_part.shape[0]
    shared_sum = sum_all(small[:split], "tensor")
    head_sum = small[split:].reshape(head_grad.shape)

    mixer_new = adamw(mixer_weight, mixer_first, mixer_second, mixer_sum, 0.02, 0.1)
    scan_new = adamw(scan_weight, scan_first, scan_second, scan_sum, 0.02, 0.1)
    merge_new = adamw(merge_weight, merge_first, merge_second, merge_sum, 0.02, 0.1)
    hidden_new = adamw(hidden_weight, hidden_first, hidden_second, hidden_sum, 0.02, 0.1)
    down_new = adamw(down_weight, down_first, down_second, down_sum, 0.02, 0.1)
    head_new = adamw(head_params, head_first, head_second, head_sum, 0.2, 0.0)
    shared_new = adamw(shared_params, shared_first, shared_second, shared_sum, 0.2, 0.0)
    return (
        block_out,
        input_grad,
        *mixer_new,
        *scan_new,
        *merge_new,
        *hidden_new,
        *down_new,
        *head_new,
        *shared_new,
    )


def solution(mesh):
    return jax.shard_map(
        per_device,
        mesh=mesh,
        in_specs=(
            P(("dp", "tensor"), None),
            P(("dp", "tensor"), None),
            P("dp", None),
            P("dp", "tensor"),
            P("dp", "tensor"),
            P("dp", "tensor"),
            P("dp", None),
            P("dp", None),
            P("dp", None),
            P("tensor", "dp"),
            P("tensor", "dp"),
            P("tensor", "dp"),
            P("dp", "tensor"),
            P("dp", "tensor"),
            P("dp", "tensor"),
            P("tensor", "dp"),
            P("tensor", "dp"),
            P("tensor", "dp"),
            P("tensor", None),
            P("tensor", None),
            P("tensor", None),
            P(),
            P(),
            P(),
        ),
        out_specs=(
            P(("dp", "tensor"), None),
            P(("dp", "tensor"), None),
            P("dp", "tensor"),
            P("dp", "tensor"),
            P("dp", "tensor"),
            P("dp", None),
            P("dp", None),
            P("dp", None),
            P("tensor", "dp"),
            P("tensor", "dp"),
            P("tensor", "dp"),
            P("dp", "tensor"),
            P("dp", "tensor"),
            P("dp", "tensor"),
            P("tensor", "dp"),
            P("tensor", "dp"),
            P("tensor", "dp"),
            P("tensor", None),
            P("tensor", None),
            P("tensor", None),
            P(),
            P(),
            P(),
        ),
        check_vma=False,
    )
```

```python
import jax
import jax.numpy as jnp
from jax import lax
from jax.experimental import pallas as pl
from jax.experimental.pallas import tpu as pltpu
from jax.sharding import PartitionSpec as P

D = 1024
HEADS_M = 24
HEAD_M = 64
STATE = 128
CONV = 4
HEADS_Q = 8
HEADS_KV = 2
HEAD_A = 64
STEP = 10
CORES = 2


EPS = 1e-05
THETA = 10000.0
HIGH = lax.Precision.HIGHEST


def scaled_norm(values, gain):
    return values * lax.rsqrt(jnp.mean(values * values, axis=-1, keepdims=True) + EPS) * gain


def doc_index(lens, count):
    place = jnp.arange(count, dtype=jnp.int32)
    ends = jnp.cumsum(lens)
    after = place[:, None] >= ends[None, :]
    seg = jnp.sum(after.astype(jnp.int32), axis=1)
    start = jnp.sum(jnp.where(after, lens[None, :], 0), axis=1)
    return (seg, place - start)


HEADS = HEADS_M // 2
WIDTH = HEADS * HEAD_M
QCOLS = HEADS_Q // 2 * HEAD_A
LANES = 128
RATE_COL = (CONV + 1) * HEAD_M
SKIP_COL = RATE_COL + 1
BIAS_COL = RATE_COL + 2


def exact_dot(left, right, dims=((1,), (0,))):
    return lax.dot_general(
        left, right, (dims, ((), ())), precision=HIGH, preferred_element_type=jnp.float32
    )


def low_dot(left, right, dims=((1,), (0,))):
    return lax.dot_general(
        left.astype(jnp.bfloat16),
        right.astype(jnp.bfloat16),
        (dims, ((), ())),
        preferred_element_type=jnp.float32,
    )


ROWS = ((0,), (0,))
COLS = ((1,), (1,))


def lane_of(shape):
    return lax.broadcasted_iota(jnp.int32, shape, 1)


def shifted(values, pos, shift):
    return jnp.where(pos >= shift, pltpu.roll(values, shift, 0), 0.0)


def conv_forward(values, rows, pos):
    total = rows[CONV : CONV + 1] + rows[CONV - 1 : CONV] * values
    for shift in range(1, CONV):
        tap = rows[CONV - 1 - shift : CONV - shift]
        total = total + tap * shifted(values, pos, shift)
    return total


def conv_backward(grad, values, rows, pos):
    length = values.shape[0]
    back = rows[CONV - 1 : CONV] * grad
    taps = [jnp.sum(grad * values, axis=0, keepdims=True)]
    for shift in range(1, CONV):
        tap = rows[CONV - 1 - shift : CONV - shift]
        kept = jnp.where(pos >= shift, grad, 0.0)
        back = back + tap * pltpu.roll(kept, length - shift, 0)
        taps.append(jnp.sum(kept * pltpu.roll(values, shift, 0), axis=0, keepdims=True))
    return back, taps[::-1] + [jnp.sum(grad, axis=0, keepdims=True)]


def swap_pairs(values):
    first = lane_of(values.shape) % HEAD_A < HEAD_A // 2
    half = HEAD_A // 2
    return jnp.where(first, pltpu.roll(values, LANES - half, 1), pltpu.roll(values, half, 1))


def turn(values, cosine, sine):
    return values * cosine + swap_pairs(values) * sine


def turn_back(values, cosine, sine):
    return values * cosine + swap_pairs(values * sine)


def half_lanes(values, which):
    mine = lane_of(values.shape) // HEAD_A == which
    return jnp.where(mine, values, jnp.zeros_like(values))


def column_to_lanes(column):
    shape = (column.shape[0], LANES)
    row = lax.broadcasted_iota(jnp.int32, shape, 0)
    mine = (row == lane_of(shape)) & (row < HEADS)
    return jnp.sum(jnp.where(mine, column, 0.0), axis=0, keepdims=True)


def conv_rows(heads_ref):
    tiles = [heads_ref[:, j * LANES : (j + 1) * LANES] for j in range(3)]
    rolled = [pltpu.roll(tile, HEAD_M, 1) for tile in tiles]
    left = lane_of((1, LANES)) < HEAD_M
    rows = []
    for k in range(CONV + 1):
        kinds = (tiles[k // 2], rolled[k // 2])
        even, odd = kinds[k % 2], kinds[1 - k % 2]
        pieces = [
            jnp.where(left, even[h : h + 1], odd[h + 1 : h + 2]) for h in range(0, HEADS, 2)
        ]
        rows.append(jnp.concatenate(pieces, axis=1))
    skip = heads_ref[:, SKIP_COL : SKIP_COL + 1]
    pieces = [jnp.where(left, skip[h : h + 1], skip[h + 1 : h + 2]) for h in range(0, HEADS, 2)]
    rows.append(jnp.concatenate(pieces, axis=1))
    return jnp.concatenate(rows + [jnp.zeros((2, WIDTH), jnp.float32)], axis=0)


def head_rows(rows, dlog, dbias):
    left = lane_of((1, LANES)) < HEAD_M
    lane = lane_of((1, LANES))
    out = []
    for i in range(HEADS // 2):
        tile = rows[:, i * LANES : (i + 1) * LANES]
        kinds = (tile, pltpu.roll(tile, HEAD_M, 1))
        for which in range(2):
            h = 2 * i + which
            piece = [kinds[(which + k) % 2][k : k + 1] for k in range(CONV + 1)]
            dskip = jnp.sum(
                half_lanes(tile[CONV + 1 : CONV + 2], which), axis=1, keepdims=True
            )
            last = jnp.where(lane == HEAD_M, dlog[:, h : h + 1], 0.0)
            last = jnp.where(lane == HEAD_M + 1, dskip, last)
            last = jnp.where(lane == HEAD_M + 2, dbias[:, h : h + 1], last)
            tiles = [
                jnp.where(left, piece[0], piece[1]),
                jnp.where(left, piece[2], piece[3]),
                jnp.where(left, piece[4], last),
            ]
            out.append(jnp.concatenate(tiles, axis=1))
    out.append(jnp.zeros((16 - HEADS, 3 * LANES), jnp.float32))
    return jnp.concatenate(out, axis=0)


def documents(lens_ref, place):
    seg, start, end = jnp.zeros_like(place), jnp.zeros_like(place), 0
    for k in range(lens_ref.shape[0]):
        end = end + lens_ref[k]
        after = place >= end
        seg = seg + jnp.where(after, 1, 0)
        start = start + jnp.where(after, lens_ref[k], 0)
    return seg, place - start


def split_rows(values, tidx, mine_ref, theirs_ref):
    half = values.shape[0] // 2
    upper, lower = values[:half], values[half:]
    mine_ref[...] = jnp.where(tidx == 0, upper, lower)
    theirs_ref[...] = jnp.where(tidx == 0, lower, upper).astype(theirs_ref.dtype)


def split_columns(left, right, core, keep_ref, give_ref):
    keep_ref[...] = jnp.where(core == 0, left, right)
    give_ref[...] = jnp.where(core == 0, right, left)


def mixer_parts(tidx_ref, lens_ref, p_ref, heads_ref, bc_ref):
    length = p_ref.shape[0]
    base = 2 * WIDTH + QCOLS + 2 * HEAD_A
    conv = conv_rows(heads_ref)
    bc = bc_ref[...]
    row = lax.broadcasted_iota(jnp.int32, (length, length), 0)
    column = lax.broadcasted_iota(jnp.int32, (length, length), 1)
    seg, pos = documents(lens_ref, lax.broadcasted_iota(jnp.int32, (length, 1), 0))
    seg_across, _ = documents(lens_ref, lax.broadcasted_iota(jnp.int32, (1, length), 1))
    same = (seg == seg_across) & (row >= column)
    wide = p_ref[:, WIDTH : 2 * WIDTH].astype(jnp.float32)
    chans_pre = conv_forward(wide, conv, pos)
    chans_sig = jax.nn.sigmoid(chans_pre)
    states = p_ref[:, base : base + 2 * STATE].astype(jnp.float32)
    states_pre = conv_forward(states, bc, pos)
    states_sig = jax.nn.sigmoid(states_pre)
    raw = p_ref[:, base + 2 * STATE : base + 2 * STATE + LANES].astype(jnp.float32)
    i = lax.broadcasted_iota(jnp.int32, (LANES, LANES), 0)
    j = lane_of((LANES, LANES))
    sel = ((i == HEADS * tidx_ref[0] + j) & (j < HEADS)).astype(jnp.float32)
    i = lax.broadcasted_iota(jnp.int32, (LANES, WIDTH), 0)
    spread = (i == lane_of((LANES, WIDTH)) // HEAD_M).astype(jnp.float32)
    rates = column_to_lanes(jnp.exp(heads_ref[:, RATE_COL : RATE_COL + 1]))
    bias = column_to_lanes(heads_ref[:, BIAS_COL : BIAS_COL + 1])
    step_pre = exact_dot(raw, sel) + bias
    steps = jnp.maximum(step_pre, 0.0) + jnp.log1p(jnp.exp(-jnp.abs(step_pre)))
    before = (row >= column).astype(jnp.float32)
    cum = exact_dot(before, -rates * steps)
    steps_wide = exact_dot(steps, spread)
    chans = chans_pre * chans_sig
    states_out = states_pre * states_sig
    in_state, out_state = states_out[:, :STATE], states_out[:, STATE:]
    inner = jnp.where(same, exact_dot(out_state, in_state, COLS), 0.0)
    return dict(
        pos=pos, wide=wide, chans_pre=chans_pre, chans_sig=chans_sig, chans=chans,
        states=states, states_pre=states_pre, states_sig=states_sig, in_state=in_state,
        out_state=out_state, step_pre=step_pre, steps=steps, rates=rates, before=before,
        cum=cum, cum_t=cum.T, same=same, steps_wide=steps_wide, inner=inner, conv=conv, bc=bc,
        sel=sel, spread=spread, weighted=(steps_wide * chans).astype(jnp.bfloat16),
    )


def decay_of(parts, head):
    gap = parts["cum"][:, head : head + 1] - parts["cum_t"][head : head + 1, :]
    return jnp.exp(jnp.minimum(gap, 0.0))


def attention_parts(p_ref, cos_ref, sin_ref):
    cosine, sine = cos_ref[...], sin_ref[...]
    pairs = []
    for i in range(QCOLS // LANES):
        a = 2 * WIDTH + i * LANES
        query = turn(p_ref[:, a : a + LANES].astype(jnp.float32), cosine, sine)
        pairs.append((query * HEAD_A ** (-0.5)).astype(jnp.bfloat16))
    a = 2 * WIDTH + QCOLS
    both = p_ref[:, a : a + LANES].astype(jnp.float32)
    key = half_lanes(turn(both, cosine, sine), 0)
    value = half_lanes(both, 1)
    keys = (key.astype(jnp.bfloat16), pltpu.roll(key, HEAD_A, 1).astype(jnp.bfloat16))
    values = (pltpu.roll(value, HEAD_A, 1).astype(jnp.bfloat16), value.astype(jnp.bfloat16))
    return pairs, keys, values


def attention_probs(query, key, same):
    scores = jnp.where(same, low_dot(query, key, COLS), -1e30)
    top = jnp.max(scores, axis=1, keepdims=True)
    raised = jnp.exp(scores - top)
    return raised / jnp.sum(raised, axis=1, keepdims=True)


def forward_kernel(
    tidx_ref, lens_ref, p_ref, heads_ref, bc_ref, cos_ref, sin_ref, w_ref,
    cat_ref, y_ref, mine_ref, theirs_ref, keep_ref, give_ref,
):
    parts = mixer_parts(tidx_ref, lens_ref, p_ref, heads_ref, bc_ref)
    for i in range(WIDTH // LANES):
        a = i * LANES
        tile = parts["weighted"][:, a : a + LANES]
        out = jnp.zeros((p_ref.shape[0], LANES), jnp.float32)
        for which in range(2):
            mixed = decay_of(parts, 2 * i + which) * parts["inner"]
            out = out + low_dot(mixed, half_lanes(tile, which))
        y_ref[:, a : a + LANES] = out
        gate = p_ref[:, a : a + LANES].astype(jnp.float32)
        out = out + parts["conv"][CONV + 1 : CONV + 2, a : a + LANES] * parts["chans"][:, a : a + LANES]
        cat_ref[:, a : a + LANES] = (out * gate * jax.nn.sigmoid(gate)).astype(cat_ref.dtype)
    pairs, keys, values = attention_parts(p_ref, cos_ref, sin_ref)
    for i, query in enumerate(pairs):
        out = jnp.zeros((p_ref.shape[0], LANES), jnp.float32)
        for which in range(2):
            probs = attention_probs(query, keys[which], parts["same"])
            out = out + low_dot(probs, values[which])
        a = WIDTH + i * LANES
        cat_ref[:, a : a + LANES] = out.astype(cat_ref.dtype)
    cat = cat_ref[...]
    split_rows(dot_t(cat, w_ref[:, p_ref.shape[1] :]), tidx_ref[0], mine_ref, theirs_ref)
    half = cat.shape[1] // 2
    split_columns(cat[:, :half], cat[:, half:], tidx_ref[1], keep_ref, give_ref)


def backward_kernel(
    tidx_ref, lens_ref, p_ref, heads_ref, bc_ref, cos_ref, sin_ref, y_ref, grad_ref,
    dp_ref, dheads_ref, dbc_ref, keep_ref, give_ref,
):
    length = p_ref.shape[0]
    low = dp_ref.dtype
    parts = mixer_parts(tidx_ref, lens_ref, p_ref, heads_ref, bc_ref)
    pos, chans = parts["pos"], parts["chans"]
    gate = p_ref[:, :WIDTH].astype(jnp.float32)
    gate_sig = jax.nn.sigmoid(gate)
    grad = grad_ref[:, :WIDTH]
    skip = parts["conv"][CONV + 1 : CONV + 2]
    outputs = y_ref[...]
    dgate = grad * (outputs + skip * chans) * gate_sig * (1.0 + gate * (1.0 - gate_sig))
    dp_ref[:, :WIDTH] = dgate.astype(low)
    dy = grad * gate * gate_sig
    dy_low = dy.astype(jnp.bfloat16)
    dweighted = []
    dinner = jnp.zeros((length, length), jnp.float32)
    for i in range(WIDTH // LANES):
        a = i * LANES
        tile = parts["weighted"][:, a : a + LANES]
        out = jnp.zeros((length, LANES), jnp.float32)
        for which in range(2):
            decay = decay_of(parts, 2 * i + which)
            dy_half = half_lanes(dy_low[:, a : a + LANES], which)
            out = out + low_dot(decay * parts["inner"], dy_half, ROWS)
            dinner = dinner + low_dot(dy_half, tile, COLS) * decay
        dweighted.append(out)
    dweighted = jnp.concatenate(dweighted, axis=1)
    spread = parts["spread"]
    weighted = parts["weighted"].astype(jnp.float32)
    dcum = exact_dot(dy_low.astype(jnp.float32) * outputs - weighted * dweighted, spread, COLS)
    dsteps = exact_dot(dweighted * chans, spread, COLS)
    dchans = skip * dy + parts["steps_wide"] * dweighted
    drate = exact_dot(parts["before"], dcum, ROWS)
    dsteps = (dsteps - parts["rates"] * drate) * jax.nn.sigmoid(parts["step_pre"])
    dlog = jnp.sum(-parts["rates"] * parts["steps"] * drate, axis=0, keepdims=True)
    dbias = jnp.sum(dsteps, axis=0, keepdims=True)
    base = 2 * WIDTH + QCOLS + 2 * HEAD_A
    draw = exact_dot(dsteps, parts["sel"], COLS)
    dp_ref[:, base + 2 * STATE :] = draw.astype(low)

    sig, pre = parts["chans_sig"], parts["chans_pre"]
    dpre = dchans * sig * (1.0 + pre * (1.0 - sig))
    back, rows = conv_backward(dpre, parts["wide"], parts["conv"], pos)
    dp_ref[:, WIDTH : 2 * WIDTH] = back.astype(low)
    rows.append(jnp.sum(dy * chans, axis=0, keepdims=True))
    rows = jnp.concatenate(rows + [jnp.zeros((2, WIDTH), jnp.float32)], axis=0)
    dheads_ref[...] = head_rows(rows, dlog, dbias)

    dinner = jnp.where(parts["same"], dinner, 0.0)
    dstates = jnp.concatenate(
        [exact_dot(dinner, parts["out_state"], ROWS), exact_dot(dinner, parts["in_state"])],
        axis=1,
    )
    sig, pre = parts["states_sig"], parts["states_pre"]
    dpre = dstates * sig * (1.0 + pre * (1.0 - sig))
    back, rows = conv_backward(dpre, parts["states"], parts["bc"], pos)
    dp_ref[:, base : base + 2 * STATE] = back.astype(low)
    dbc_ref[...] = jnp.concatenate(rows, axis=0)

    pairs, keys, values = attention_parts(p_ref, cos_ref, sin_ref)
    cosine, sine = cos_ref[...], sin_ref[...]
    dkeys = [jnp.zeros((length, LANES), jnp.float32) for _ in range(2)]
    dvalues = [jnp.zeros((length, LANES), jnp.float32) for _ in range(2)]
    for i, query in enumerate(pairs):
        a = WIDTH + i * LANES
        datt = grad_ref[:, a : a + LANES].astype(jnp.bfloat16)
        dquery = jnp.zeros((length, LANES), jnp.float32)
        for which in range(2):
            probs = attention_probs(query, keys[which], parts["same"])
            dprobs = low_dot(datt, values[which], COLS)
            dscores = probs * (dprobs - jnp.sum(probs * dprobs, axis=1, keepdims=True))
            dscores = dscores.astype(jnp.bfloat16)
            dquery = dquery + low_dot(dscores, keys[which])
            dkeys[which] = dkeys[which] + low_dot(dscores, query, ROWS)
            dvalues[which] = dvalues[which] + low_dot(probs, datt, ROWS)
        a = 2 * WIDTH + i * LANES
        dquery = turn_back(dquery * HEAD_A ** (-0.5), cosine, sine)
        dp_ref[:, a : a + LANES] = dquery.astype(low)
    dkey = half_lanes(dkeys[0], 0) + pltpu.roll(half_lanes(dkeys[1], 1), HEAD_A, 1)
    dvalue = pltpu.roll(half_lanes(dvalues[0], 0), HEAD_A, 1) + half_lanes(dvalues[1], 1)
    a = 2 * WIDTH + QCOLS
    dboth = half_lanes(turn_back(dkey, cosine, sine), 0) + dvalue
    dp_ref[:, a : a + LANES] = dboth.astype(low)
    half = dp_ref.shape[1] // 2
    split_columns(dp_ref[:, :half], dp_ref[:, half:], tidx_ref[1], keep_ref, give_ref)


def local_call(kernel, outs, name, scalars=0):
    space = pl.BlockSpec(memory_space=pltpu.VMEM)
    scalar = pl.BlockSpec(memory_space=pltpu.SMEM)
    return lambda *args: pl.pallas_call(
        kernel,
        out_shape=[jax.ShapeDtypeStruct(shape, dtype) for shape, dtype in outs],
        in_specs=[scalar] * scalars + [space] * (len(args) - scalars),
        out_specs=[space] * len(outs),
        compiler_params=pltpu.CompilerParams(vmem_limit_bytes=56 * 2**20),
        name=name,
    )(*args)


def mixer_consts(head_params, conv_shared, lens, where, length):
    _, pos = doc_index(lens, length)
    half = HEAD_A // 2
    freq = THETA ** (-jnp.arange(half, dtype=jnp.float32) * 2.0 / HEAD_A)
    angle = pos.astype(jnp.float32)[:, None] * freq[None, :]
    cosine, sine = jnp.cos(angle), jnp.sin(angle)
    heads = jnp.pad(
        head_params, ((0, 16 - HEADS), (0, 3 * LANES - head_params.shape[1]))
    )
    scalars = (where, lens)
    return scalars, (
        heads,
        conv_shared,
        jnp.concatenate([cosine] * 4, axis=1),
        jnp.concatenate([-sine, sine, -sine, sine], axis=1),
    )


def mixer_forward(projected, consts, weight):
    length = projected.shape[0]
    width = WIDTH + QCOLS
    outs = [
        ((length, width), jnp.bfloat16),
        ((length, WIDTH), jnp.float32),
        ((length // 2, weight.shape[0]), jnp.float32),
        ((length // 2, weight.shape[0]), jnp.bfloat16),
        ((length, width // 2), jnp.bfloat16),
        ((length, width // 2), jnp.bfloat16),
    ]
    scalars, arrays = consts
    return local_call(forward_kernel, outs, "mixer_forward", 2)(
        *scalars, projected, *arrays, weight
    )


def mixer_backward(projected, consts, outputs, grad):
    length, width = projected.shape
    outs = [
        ((length, width), jnp.bfloat16),
        ((16, 3 * LANES), jnp.float32),
        ((CONV + 1, 2 * STATE), jnp.float32),
        ((length, width // 2), jnp.bfloat16),
        ((length, width // 2), jnp.bfloat16),
    ]
    scalars, arrays = consts
    grad_proj, heads, bc, keep, give = local_call(backward_kernel, outs, "mixer_backward", 2)(
        *scalars, projected, *arrays, outputs, grad
    )
    return grad_proj, heads[:HEADS, : BIAS_COL + 1], bc, keep, give


def feed_kernel(
    where_ref, x_ref, grad_ref, w_ref,
    act_ref, dgu_ref, mine_ref, theirs_ref, keep_ref, give_ref, act_keep_ref, act_give_ref,
):
    units = act_ref.shape[1]
    tidx, core = where_ref[0], where_ref[1]
    gate_up = dot(x_ref[...], w_ref[:, : 2 * units])
    gate, upper = gate_up[:, :units], gate_up[:, units:]
    sig = jax.nn.sigmoid(gate)
    raised = gate * sig
    act = (raised * upper).astype(act_ref.dtype)
    act_ref[...] = act
    split_columns(act[:, : units // 2], act[:, units // 2 :], core, act_keep_ref, act_give_ref)
    grad = dot(grad_ref[...], w_ref[:, 2 * units : 3 * units])
    dgate = (grad * upper * sig * (1.0 + gate * (1.0 - sig))).astype(dgu_ref.dtype)
    dupper = (grad * raised).astype(dgu_ref.dtype)
    dgu_ref[:, :units] = dgate
    dgu_ref[:, units:] = dupper
    split_columns(dgate, dupper, core, keep_ref, give_ref)
    split_rows(dot_t(dgu_ref[...], w_ref[:, : 2 * units]), tidx, mine_ref, theirs_ref)


def feed_forward_back(where, values, grad, weight, units):
    length, width = values.shape
    low = jnp.bfloat16
    outs = [
        ((length, units), low),
        ((length, 2 * units), low),
        ((length // 2, width), jnp.float32),
        ((length // 2, width), low),
        ((length, units), low),
        ((length, units), low),
        ((length, units // 2), low),
        ((length, units // 2), low),
    ]
    return local_call(feed_kernel, outs, "feed_forward_back", 1)(where, values, grad, weight)


def weight_grads(sides, dtype):
    width = sum(side[1].shape[1] for side in sides)
    model = sides[0][0].shape[1]
    block = 256

    def kernel(*refs):
        out_ref, a = refs[-1], 0
        for i in range(len(sides)):
            x, y, other_x, other_y = refs[4 * i : 4 * i + 4]
            b = a + y.shape[1]
            for r in range(0, model, block):
                part = cross(x[:, r : r + block], y[...])
                part = part + cross(other_x[:, r : r + block], other_y[...])
                out_ref[r : r + block, a:b] = part.astype(out_ref.dtype)
            a = b

    flat = [value for side in sides for value in side]
    return local_call(kernel, [((model, width), dtype)], "weight_grads")(*flat)[0]


def cross(left, right):
    return lax.dot_general(
        left, right, (((0,), (0,)), ((), ())), preferred_element_type=jnp.float32
    )


def dot(left, right):
    return jnp.dot(left, right, preferred_element_type=jnp.float32)


def dot_t(left, right):
    return lax.dot_general(
        left, right, (((1,), (1,)), ((), ())), preferred_element_type=jnp.float32
    )


def adamw(weight, first, second, grad, rate, decay):
    first = 0.9 * first + 0.1 * grad
    second = 0.95 * second + 0.05 * grad * grad
    fixed_one = first / (1.0 - 0.9**STEP)
    fixed_two = second / (1.0 - 0.95**STEP)
    weight = weight - rate * (fixed_one / (jnp.sqrt(fixed_two) + 1e-08) + decay * weight)
    return (first, second, weight)


def swap(values, axis, distance):
    count = lax.axis_size(axis)
    return lax.ppermute(values, axis, [(i, i ^ distance) for i in range(count)])


def pair_rows(own, other, tidx):
    return jnp.where(
        tidx == 0,
        jnp.concatenate([own, other], axis=0),
        jnp.concatenate([other, own], axis=0),
    )


def gather_rows(own, tidx):
    return pair_rows(own, swap(own, "tensor", 1), tidx)


def scatter_rows(partial, tidx):
    rows = partial.shape[0] // 2
    upper, lower = partial[:rows], partial[rows:]
    mine = jnp.where(tidx == 0, upper, lower)
    theirs = jnp.where(tidx == 0, lower, upper).astype(jnp.bfloat16)
    return mine + swap(theirs, "tensor", 1).astype(jnp.float32)


RING_CHIPS = 8


def ring_chip(place):
    place = place % RING_CHIPS
    half = RING_CHIPS // 2
    if isinstance(place, int):
        return 2 * place if place < half else 2 * (RING_CHIPS - 1 - place) + 1
    return jnp.where(place < half, 2 * place, 2 * (RING_CHIPS - 1 - place) + 1)


def ring_place(chip):
    return jnp.where(chip % 2 == 0, chip // 2, RING_CHIPS - 1 - chip // 2)


def ring_step(values):
    pairs = []
    for p in range(RING_CHIPS):
        pairs.append((CORES * ring_chip(p), CORES * ring_chip(p + 1)))
        pairs.append((CORES * ring_chip(p + 1) + 1, CORES * ring_chip(p) + 1))
    return lax.ppermute(values, "dp", pairs)


def place_rows(pieces, blocks, values=None, columns=0):
    count = len(pieces)
    height, width = pieces[0].shape
    low = pieces[0].dtype
    extra = [] if values is None else [values]

    def kernel(block_ref, *refs):
        out_ref = refs[count + len(extra)]
        for i in range(count):
            start = pl.multiple_of(block_ref[i] * height, height)
            out_ref[pl.ds(start, height), :] = refs[i][...]
        if extra:
            refs[-1][...] = dot(refs[count][...], out_ref[:, :columns]).astype(low)

    outs = [((count * height, width), low)]
    if extra:
        outs.append(((values.shape[0], columns), low))
    return local_call(kernel, outs, "place_rows", 1)(blocks, *pieces, *extra)


def ring_gather(shard, place, core):
    way = 1 - 2 * core
    own = [shard]
    other = [swap(shard, "dp", 1)]
    for _ in range(1, RING_CHIPS):
        own.append(ring_step(own[-1]))
        other.append(swap(own[-1], "dp", 1))
    blocks = [CORES * ring_chip(place - way * k) + core for k in range(RING_CHIPS)]
    blocks += [CORES * ring_chip(place + way * k) + 1 - core for k in range(RING_CHIPS)]
    return own + other, jnp.stack(blocks).astype(jnp.int32), own


def ring_reduce(chains, place, core, last):
    way = 1 - 2 * core
    sums = [None] * len(chains)
    for step in range(1, RING_CHIPS + 1):
        chip = ring_chip(place - way * step)
        for i, chain in enumerate(chains):
            if step == RING_CHIPS and i == 0:
                sums[0], last = lax.optimization_barrier((sums[0], last))
            parts = []
            for grad, a, b in chain:
                rows = grad.shape[0] // RING_CHIPS
                parts.append(lax.dynamic_slice(grad, (chip * rows, a), (rows, b - a)))
            part = parts[0] if len(parts) == 1 else jnp.concatenate(parts, axis=1)
            if step > 1:
                part = part + sums[i].astype(jnp.float32)
            if step < RING_CHIPS:
                part = ring_step(part.astype(jnp.bfloat16))
            sums[i] = part
        if step == 1:
            first = sums[0]
    return jnp.concatenate(sums, axis=1), first, last


def both_cores(model_side, keep, give):
    return model_side, keep, swap(model_side, "dp", 1), swap(give, "dp", 1)


def own_rows(summed, core):
    rows = summed.shape[0] // CORES
    upper, lower = summed[:rows], summed[rows:]
    mine = jnp.where(core == 0, upper, lower)
    give = jnp.where(core == 0, lower, upper).astype(jnp.bfloat16)
    taken = swap(give, "dp", 1).astype(jnp.float32)
    return jnp.where(core == 0, mine, taken), jnp.where(core == 0, taken, mine)


def join_halves(halves, a, b):
    return jnp.concatenate([halves[0][:, a:b], halves[1][:, a:b]], axis=1)


def sum_all(values, axis):
    distance = 1
    while distance < lax.axis_size(axis):
        values = values + swap(values, axis, distance)
        distance *= 2
    return values


def per_device(
    residual,
    out_grad,
    doc_lengths,
    mixer_weight,
    mixer_first,
    mixer_second,
    scan_weight,
    scan_first,
    scan_second,
    merge_weight,
    merge_first,
    merge_second,
    hidden_weight,
    hidden_first,
    hidden_second,
    down_weight,
    down_first,
    down_second,
    head_params,
    head_first,
    head_second,
    shared_params,
    shared_first,
    shared_second,
):
    low = jnp.bfloat16
    tidx = lax.axis_index("tensor")
    count = lax.axis_size("dp")
    chips = count // CORES
    core = lax.axis_index("dp") % CORES
    place = ring_place(lax.axis_index("dp") // CORES)
    group = residual.shape[0] * lax.axis_size("tensor")
    conv_shared = shared_params[2 * D :].reshape(CONV + 1, 2 * STATE)

    ring = chips == RING_CHIPS
    mix_cols = mixer_weight.shape[1]
    both_cols = mix_cols + scan_weight.shape[1]
    spare = jnp.zeros((mixer_weight.shape[0], -both_cols % 256), low)
    first_cols = both_cols + spare.shape[1]
    units = down_weight.shape[0]
    first_shard = jnp.concatenate(
        [mixer_weight.astype(low), scan_weight.astype(low), spare, merge_weight.astype(low).T],
        axis=1,
    )
    rest_shard = jnp.concatenate(
        [hidden_weight.astype(low), down_weight.astype(low).T], axis=1
    )
    where = jnp.stack([tidx, core]).astype(jnp.int32)
    consts = mixer_consts(head_params, conv_shared, doc_lengths[0], where, group)
    normed_one, norm_back_one = jax.vjp(scaled_norm, residual, shared_params[:D])
    first_all = gather_rows(normed_one.astype(low), tidx)
    grad_feed = gather_rows(out_grad.astype(low), tidx)
    if ring:
        pieces, blocks, own = ring_gather(first_shard, place, core)
        first_w, projected = place_rows(pieces, blocks, first_all, first_cols)
        rest_shard = lax.optimization_barrier((rest_shard, own[4]))[0]
    else:
        first_w = lax.all_gather(first_shard, "dp", axis=0, tiled=True)
        projected = dot(first_all, first_w[:, :first_cols]).astype(low)
    rest_w = lax.all_gather(rest_shard, "dp", axis=0, tiled=True)
    merge_w = first_w[:, first_cols:]
    joined_low, outputs, mine, theirs, joined_keep, joined_give = mixer_forward(
        projected, consts, first_w
    )
    middle = residual + mine + swap(theirs, "tensor", 1).astype(jnp.float32)
    normed_two, norm_back_two = jax.vjp(scaled_norm, middle, shared_params[D : 2 * D])
    second_all = gather_rows(normed_two.astype(low), tidx)
    activ_low, grad_gu, mine, theirs, gu_keep, gu_give, act_keep, act_give = feed_forward_back(
        where, second_all, grad_feed, rest_w, units
    )
    grad_second = mine + swap(theirs, "tensor", 1).astype(jnp.float32)
    grad_middle_part, gain_two_grad = norm_back_two(grad_second)
    grad_middle = out_grad + grad_middle_part
    grad_mixed = gather_rows(grad_middle.astype(low), tidx)
    grad_joined = dot(grad_mixed, merge_w)
    if ring:
        rest_grad = weight_grads(
            [
                both_cores(second_all, gu_keep, gu_give),
                both_cores(grad_feed, act_keep, act_give),
            ],
            low,
        )
        merge_grad = weight_grads([both_cores(grad_mixed, joined_keep, joined_give)], jnp.float32)
        grad_joined, rest_grad = lax.optimization_barrier((grad_joined, rest_grad))
        rest_sum = lax.psum_scatter(
            rest_grad,
            "dp",
            scatter_dimension=0,
            axis_index_groups=[[i * CORES + c for i in range(chips)] for c in range(CORES)],
            tiled=True,
        )
    grad_proj, head_grad, conv_grad, proj_keep, proj_give = mixer_backward(
        projected, consts, outputs, grad_joined
    )
    later = grad_proj
    if ring:
        rest_halves = own_rows(rest_sum.astype(jnp.float32), core)
        hidden_sum = join_halves(rest_halves, 0, units)
        down_sum = join_halves(rest_halves, units, rest_sum.shape[1]).T
        hidden_new = adamw(hidden_weight, hidden_first, hidden_second, hidden_sum, 0.02, 0.1)
        down_new = adamw(down_weight, down_first, down_second, down_sum, 0.02, 0.1)
        first_grad = weight_grads([both_cores(first_all, proj_keep, proj_give)], jnp.float32)
        a = first_cols // CORES
        cut = (a + merge_grad.shape[1]) // 2 // 128 * 128
        chains = [
            [(first_grad, 0, cut)],
            [(first_grad, cut, a), (merge_grad, 0, merge_grad.shape[1])],
        ]
        first_sum, mark, (hidden_new, down_new) = ring_reduce(
            chains, place, core, (hidden_new, down_new)
        )
        later, activ_low = lax.optimization_barrier((grad_proj, activ_low, mark))[:2]
        first_halves = own_rows(first_sum, core)
        merge_sum = join_halves(first_halves, a, first_sum.shape[1]).T
        first_sum = join_halves(first_halves, 0, a)
    else:
        whole = jnp.concatenate(
            [
                cross(first_all, grad_proj),
                cross(second_all, grad_gu),
                cross(grad_feed, activ_low),
                cross(grad_mixed, joined_low),
            ],
            axis=1,
        ).astype(low)
        whole = lax.psum_scatter(whole, "dp", scatter_dimension=0, tiled=True)
        whole = whole.astype(jnp.float32)
        a = grad_proj.shape[1]
        first_sum = whole[:, :a]
        hidden_sum = whole[:, a : a + 2 * units]
        a = a + 2 * units
        down_sum = whole[:, a : a + units].T
        merge_sum = whole[:, a + units :].T
        hidden_new = adamw(hidden_weight, hidden_first, hidden_second, hidden_sum, 0.02, 0.1)
        down_new = adamw(down_weight, down_first, down_second, down_sum, 0.02, 0.1)
    mixer_sum, scan_sum = first_sum[:, :mix_cols], first_sum[:, mix_cols:both_cols]
    scan_sum = scan_sum + swap(scan_sum, "tensor", 1)
    grad_first = scatter_rows(dot_t(later, first_w[:, :first_cols]), tidx)
    grad_resid_part, gain_one_grad = norm_back_one(grad_first)
    input_grad = grad_middle + grad_resid_part
    block_out = middle + scatter_rows(dot_t(activ_low, rest_w[:, 2 * units :]), tidx)

    shared_part = jnp.concatenate([gain_one_grad, gain_two_grad, conv_grad.reshape(-1)])
    small = jnp.concatenate([shared_part, head_grad.reshape(-1)])
    small = sum_all(small, "dp")
    split = shared_part.shape[0]
    shared_sum = sum_all(small[:split], "tensor")
    head_sum = small[split:].reshape(head_grad.shape)

    mixer_new = adamw(mixer_weight, mixer_first, mixer_second, mixer_sum, 0.02, 0.1)
    scan_new = adamw(scan_weight, scan_first, scan_second, scan_sum, 0.02, 0.1)
    merge_new = adamw(merge_weight, merge_first, merge_second, merge_sum, 0.02, 0.1)
    head_new = adamw(head_params, head_first, head_second, head_sum, 0.2, 0.0)
    shared_new = adamw(shared_params, shared_first, shared_second, shared_sum, 0.2, 0.0)
    return (
        block_out,
        input_grad,
        *mixer_new,
        *scan_new,
        *merge_new,
        *hidden_new,
        *down_new,
        *head_new,
        *shared_new,
    )


def solution(mesh):
    return jax.shard_map(
        per_device,
        mesh=mesh,
        in_specs=(
            P(("dp", "tensor"), None),
            P(("dp", "tensor"), None),
            P("dp", None),
            P("dp", "tensor"),
            P("dp", "tensor"),
            P("dp", "tensor"),
            P("dp", None),
            P("dp", None),
            P("dp", None),
            P("tensor", "dp"),
            P("tensor", "dp"),
            P("tensor", "dp"),
            P("dp", "tensor"),
            P("dp", "tensor"),
            P("dp", "tensor"),
            P("tensor", "dp"),
            P("tensor", "dp"),
            P("tensor", "dp"),
            P("tensor", None),
            P("tensor", None),
            P("tensor", None),
            P(),
            P(),
            P(),
        ),
        out_specs=(
            P(("dp", "tensor"), None),
            P(("dp", "tensor"), None),
            P("dp", "tensor"),
            P("dp", "tensor"),
            P("dp", "tensor"),
            P("dp", None),
            P("dp", None),
            P("dp", None),
            P("tensor", "dp"),
            P("tensor", "dp"),
            P("tensor", "dp"),
            P("dp", "tensor"),
            P("dp", "tensor"),
            P("dp", "tensor"),
            P("tensor", "dp"),
            P("tensor", "dp"),
            P("tensor", "dp"),
            P("tensor", None),
            P("tensor", None),
            P("tensor", None),
            P(),
            P(),
            P(),
        ),
        check_vma=False,
    )
```

```python
import jax
import jax.numpy as jnp
from jax import lax
from jax.experimental import pallas as pl
from jax.experimental.pallas import tpu as pltpu
from jax.sharding import PartitionSpec as P

D = 1024
HEADS_M = 24
HEAD_M = 64
STATE = 128
CONV = 4
HEADS_Q = 8
HEADS_KV = 2
HEAD_A = 64
STEP = 10
CORES = 2


EPS = 1e-05
THETA = 10000.0
HIGH = lax.Precision.HIGHEST


def scaled_norm(values, gain):
    return values * lax.rsqrt(jnp.mean(values * values, axis=-1, keepdims=True) + EPS) * gain


def norm_scale(values):
    return lax.rsqrt(jnp.mean(values * values, axis=-1, keepdims=True) + EPS)


def norm_back(values, gain, grad):
    scale = norm_scale(values)
    scaled = grad * gain
    inner = jnp.mean(values * scaled, axis=-1, keepdims=True)
    return scale * scaled - values * (scale * scale * scale * inner)


def doc_index(lens, count):
    place = jnp.arange(count, dtype=jnp.int32)
    ends = jnp.cumsum(lens)
    after = place[:, None] >= ends[None, :]
    seg = jnp.sum(after.astype(jnp.int32), axis=1)
    start = jnp.sum(jnp.where(after, lens[None, :], 0), axis=1)
    return (seg, place - start)


HEADS = HEADS_M // 2
WIDTH = HEADS * HEAD_M
QCOLS = HEADS_Q // 2 * HEAD_A
LANES = 128
RATE_COL = (CONV + 1) * HEAD_M
SKIP_COL = RATE_COL + 1
BIAS_COL = RATE_COL + 2


def exact_dot(left, right, dims=((1,), (0,))):
    return lax.dot_general(
        left, right, (dims, ((), ())), precision=HIGH, preferred_element_type=jnp.float32
    )


def low_dot(left, right, dims=((1,), (0,))):
    return lax.dot_general(
        left.astype(jnp.bfloat16),
        right.astype(jnp.bfloat16),
        (dims, ((), ())),
        preferred_element_type=jnp.float32,
    )


ROWS = ((0,), (0,))
COLS = ((1,), (1,))


def lane_of(shape):
    return lax.broadcasted_iota(jnp.int32, shape, 1)


def shifted(values, pos, shift):
    return jnp.where(pos >= shift, pltpu.roll(values, shift, 0), 0.0)


def conv_forward(values, rows, pos):
    total = rows[CONV : CONV + 1] + rows[CONV - 1 : CONV] * values
    for shift in range(1, CONV):
        tap = rows[CONV - 1 - shift : CONV - shift]
        total = total + tap * shifted(values, pos, shift)
    return total


def conv_backward(grad, values, rows, pos):
    length = values.shape[0]
    back = rows[CONV - 1 : CONV] * grad
    taps = [jnp.sum(grad * values, axis=0, keepdims=True)]
    for shift in range(1, CONV):
        tap = rows[CONV - 1 - shift : CONV - shift]
        kept = jnp.where(pos >= shift, grad, 0.0)
        back = back + tap * pltpu.roll(kept, length - shift, 0)
        taps.append(jnp.sum(kept * pltpu.roll(values, shift, 0), axis=0, keepdims=True))
    return back, taps[::-1] + [jnp.sum(grad, axis=0, keepdims=True)]


def swap_pairs(values):
    first = lane_of(values.shape) % HEAD_A < HEAD_A // 2
    half = HEAD_A // 2
    return jnp.where(first, pltpu.roll(values, LANES - half, 1), pltpu.roll(values, half, 1))


def turn(values, cosine, sine):
    return values * cosine + swap_pairs(values) * sine


def turn_back(values, cosine, sine):
    return values * cosine + swap_pairs(values * sine)


def half_lanes(values, which):
    mine = lane_of(values.shape) // HEAD_A == which
    return jnp.where(mine, values, jnp.zeros_like(values))


def column_to_lanes(column):
    shape = (column.shape[0], LANES)
    row = lax.broadcasted_iota(jnp.int32, shape, 0)
    mine = (row == lane_of(shape)) & (row < HEADS)
    return jnp.sum(jnp.where(mine, column, 0.0), axis=0, keepdims=True)


def conv_rows(heads_ref):
    tiles = [heads_ref[:, j * LANES : (j + 1) * LANES] for j in range(3)]
    rolled = [pltpu.roll(tile, HEAD_M, 1) for tile in tiles]
    left = lane_of((1, LANES)) < HEAD_M
    rows = []
    for k in range(CONV + 1):
        kinds = (tiles[k // 2], rolled[k // 2])
        even, odd = kinds[k % 2], kinds[1 - k % 2]
        pieces = [
            jnp.where(left, even[h : h + 1], odd[h + 1 : h + 2]) for h in range(0, HEADS, 2)
        ]
        rows.append(jnp.concatenate(pieces, axis=1))
    skip = heads_ref[:, SKIP_COL : SKIP_COL + 1]
    pieces = [jnp.where(left, skip[h : h + 1], skip[h + 1 : h + 2]) for h in range(0, HEADS, 2)]
    rows.append(jnp.concatenate(pieces, axis=1))
    return jnp.concatenate(rows + [jnp.zeros((2, WIDTH), jnp.float32)], axis=0)


def head_rows(rows, dlog, dbias):
    left = lane_of((1, LANES)) < HEAD_M
    lane = lane_of((1, LANES))
    out = []
    for i in range(HEADS // 2):
        tile = rows[:, i * LANES : (i + 1) * LANES]
        kinds = (tile, pltpu.roll(tile, HEAD_M, 1))
        for which in range(2):
            h = 2 * i + which
            piece = [kinds[(which + k) % 2][k : k + 1] for k in range(CONV + 1)]
            dskip = jnp.sum(
                half_lanes(tile[CONV + 1 : CONV + 2], which), axis=1, keepdims=True
            )
            last = jnp.where(lane == HEAD_M, dlog[:, h : h + 1], 0.0)
            last = jnp.where(lane == HEAD_M + 1, dskip, last)
            last = jnp.where(lane == HEAD_M + 2, dbias[:, h : h + 1], last)
            tiles = [
                jnp.where(left, piece[0], piece[1]),
                jnp.where(left, piece[2], piece[3]),
                jnp.where(left, piece[4], last),
            ]
            out.append(jnp.concatenate(tiles, axis=1))
    out.append(jnp.zeros((16 - HEADS, 3 * LANES), jnp.float32))
    return jnp.concatenate(out, axis=0)


def documents(lens_ref, place):
    seg, start, end = jnp.zeros_like(place), jnp.zeros_like(place), 0
    for k in range(lens_ref.shape[0]):
        end = end + lens_ref[k]
        after = place >= end
        seg = seg + jnp.where(after, 1, 0)
        start = start + jnp.where(after, lens_ref[k], 0)
    return seg, place - start


def split_rows(values, tidx, mine_ref, theirs_ref):
    half = values.shape[0] // 2
    upper, lower = values[:half], values[half:]
    mine_ref[...] = jnp.where(tidx == 0, upper, lower)
    theirs_ref[...] = jnp.where(tidx == 0, lower, upper).astype(theirs_ref.dtype)


def split_columns(left, right, core, keep_ref, give_ref):
    keep_ref[...] = jnp.where(core == 0, left, right)
    give_ref[...] = jnp.where(core == 0, right, left)


def mixer_parts(tidx_ref, lens_ref, p_ref, heads_ref, bc_ref):
    length = p_ref.shape[0]
    base = 2 * WIDTH + QCOLS + 2 * HEAD_A
    conv = conv_rows(heads_ref)
    bc = bc_ref[...]
    row = lax.broadcasted_iota(jnp.int32, (length, length), 0)
    column = lax.broadcasted_iota(jnp.int32, (length, length), 1)
    seg, pos = documents(lens_ref, lax.broadcasted_iota(jnp.int32, (length, 1), 0))
    seg_across, _ = documents(lens_ref, lax.broadcasted_iota(jnp.int32, (1, length), 1))
    same = (seg == seg_across) & (row >= column)
    wide = p_ref[:, WIDTH : 2 * WIDTH].astype(jnp.float32)
    chans_pre = conv_forward(wide, conv, pos)
    chans_sig = jax.nn.sigmoid(chans_pre)
    states = p_ref[:, base : base + 2 * STATE].astype(jnp.float32)
    states_pre = conv_forward(states, bc, pos)
    states_sig = jax.nn.sigmoid(states_pre)
    raw = p_ref[:, base + 2 * STATE : base + 2 * STATE + LANES].astype(jnp.float32)
    i = lax.broadcasted_iota(jnp.int32, (LANES, LANES), 0)
    j = lane_of((LANES, LANES))
    sel = ((i == HEADS * tidx_ref[0] + j) & (j < HEADS)).astype(jnp.float32)
    i = lax.broadcasted_iota(jnp.int32, (LANES, WIDTH), 0)
    spread = (i == lane_of((LANES, WIDTH)) // HEAD_M).astype(jnp.float32)
    rates = column_to_lanes(jnp.exp(heads_ref[:, RATE_COL : RATE_COL + 1]))
    bias = column_to_lanes(heads_ref[:, BIAS_COL : BIAS_COL + 1])
    step_pre = exact_dot(raw, sel) + bias
    steps = jnp.maximum(step_pre, 0.0) + jnp.log1p(jnp.exp(-jnp.abs(step_pre)))
    before = (row >= column).astype(jnp.float32)
    cum = exact_dot(before, -rates * steps)
    steps_wide = exact_dot(steps, spread)
    chans = chans_pre * chans_sig
    states_out = states_pre * states_sig
    in_state, out_state = states_out[:, :STATE], states_out[:, STATE:]
    inner = jnp.where(same, exact_dot(out_state, in_state, COLS), 0.0)
    return dict(
        pos=pos, wide=wide, chans_pre=chans_pre, chans_sig=chans_sig, chans=chans,
        states=states, states_pre=states_pre, states_sig=states_sig, in_state=in_state,
        out_state=out_state, step_pre=step_pre, steps=steps, rates=rates, before=before,
        cum=cum, cum_t=cum.T, same=same, steps_wide=steps_wide, inner=inner, conv=conv, bc=bc,
        sel=sel, spread=spread, weighted=(steps_wide * chans).astype(jnp.bfloat16),
    )


def decay_of(parts, head):
    gap = parts["cum"][:, head : head + 1] - parts["cum_t"][head : head + 1, :]
    return jnp.exp(jnp.minimum(gap, 0.0))


def attention_parts(p_ref, cos_ref, sin_ref):
    cosine, sine = cos_ref[...], sin_ref[...]
    pairs = []
    for i in range(QCOLS // LANES):
        a = 2 * WIDTH + i * LANES
        query = turn(p_ref[:, a : a + LANES].astype(jnp.float32), cosine, sine)
        pairs.append((query * HEAD_A ** (-0.5)).astype(jnp.bfloat16))
    a = 2 * WIDTH + QCOLS
    both = p_ref[:, a : a + LANES].astype(jnp.float32)
    key = half_lanes(turn(both, cosine, sine), 0)
    value = half_lanes(both, 1)
    keys = (key.astype(jnp.bfloat16), pltpu.roll(key, HEAD_A, 1).astype(jnp.bfloat16))
    values = (pltpu.roll(value, HEAD_A, 1).astype(jnp.bfloat16), value.astype(jnp.bfloat16))
    return pairs, keys, values


def attention_probs(query, key, same):
    scores = jnp.where(same, low_dot(query, key, COLS), -1e30)
    top = jnp.max(scores, axis=1, keepdims=True)
    raised = jnp.exp(scores - top)
    return raised / jnp.sum(raised, axis=1, keepdims=True)


def forward_kernel(
    tidx_ref, lens_ref, p_ref, heads_ref, bc_ref, cos_ref, sin_ref, w_ref,
    cat_ref, y_ref, mine_ref, theirs_ref, keep_ref, give_ref,
):
    parts = mixer_parts(tidx_ref, lens_ref, p_ref, heads_ref, bc_ref)
    for i in range(WIDTH // LANES):
        a = i * LANES
        tile = parts["weighted"][:, a : a + LANES]
        out = jnp.zeros((p_ref.shape[0], LANES), jnp.float32)
        for which in range(2):
            mixed = decay_of(parts, 2 * i + which) * parts["inner"]
            out = out + low_dot(mixed, half_lanes(tile, which))
        y_ref[:, a : a + LANES] = out
        gate = p_ref[:, a : a + LANES].astype(jnp.float32)
        out = out + parts["conv"][CONV + 1 : CONV + 2, a : a + LANES] * parts["chans"][:, a : a + LANES]
        cat_ref[:, a : a + LANES] = (out * gate * jax.nn.sigmoid(gate)).astype(cat_ref.dtype)
    pairs, keys, values = attention_parts(p_ref, cos_ref, sin_ref)
    for i, query in enumerate(pairs):
        out = jnp.zeros((p_ref.shape[0], LANES), jnp.float32)
        for which in range(2):
            probs = attention_probs(query, keys[which], parts["same"])
            out = out + low_dot(probs, values[which])
        a = WIDTH + i * LANES
        cat_ref[:, a : a + LANES] = out.astype(cat_ref.dtype)
    cat = cat_ref[...]
    split_rows(dot_t(cat, w_ref[:, p_ref.shape[1] :]), tidx_ref[0], mine_ref, theirs_ref)
    half = cat.shape[1] // 2
    split_columns(cat[:, :half], cat[:, half:], tidx_ref[1], keep_ref, give_ref)


def backward_kernel(
    tidx_ref, lens_ref, p_ref, heads_ref, bc_ref, cos_ref, sin_ref, y_ref, dmix_ref, w_ref,
    dp_ref, dheads_ref, dbc_ref, keep_ref, give_ref,
):
    length = p_ref.shape[0]
    low = dp_ref.dtype
    parts = mixer_parts(tidx_ref, lens_ref, p_ref, heads_ref, bc_ref)
    pos, chans = parts["pos"], parts["chans"]
    gate = p_ref[:, :WIDTH].astype(jnp.float32)
    gate_sig = jax.nn.sigmoid(gate)
    grad_all = dot(dmix_ref[...], w_ref[:, p_ref.shape[1] :])
    grad = grad_all[:, :WIDTH]
    skip = parts["conv"][CONV + 1 : CONV + 2]
    outputs = y_ref[...]
    dgate = grad * (outputs + skip * chans) * gate_sig * (1.0 + gate * (1.0 - gate_sig))
    dp_ref[:, :WIDTH] = dgate.astype(low)
    dy = grad * gate * gate_sig
    dy_low = dy.astype(jnp.bfloat16)
    dweighted = []
    dinner = jnp.zeros((length, length), jnp.float32)
    for i in range(WIDTH // LANES):
        a = i * LANES
        tile = parts["weighted"][:, a : a + LANES]
        out = jnp.zeros((length, LANES), jnp.float32)
        for which in range(2):
            decay = decay_of(parts, 2 * i + which)
            dy_half = half_lanes(dy_low[:, a : a + LANES], which)
            out = out + low_dot(decay * parts["inner"], dy_half, ROWS)
            dinner = dinner + low_dot(dy_half, tile, COLS) * decay
        dweighted.append(out)
    dweighted = jnp.concatenate(dweighted, axis=1)
    spread = parts["spread"]
    weighted = parts["weighted"].astype(jnp.float32)
    dcum = exact_dot(dy_low.astype(jnp.float32) * outputs - weighted * dweighted, spread, COLS)
    dsteps = exact_dot(dweighted * chans, spread, COLS)
    dchans = skip * dy + parts["steps_wide"] * dweighted
    drate = exact_dot(parts["before"], dcum, ROWS)
    dsteps = (dsteps - parts["rates"] * drate) * jax.nn.sigmoid(parts["step_pre"])
    dlog = jnp.sum(-parts["rates"] * parts["steps"] * drate, axis=0, keepdims=True)
    dbias = jnp.sum(dsteps, axis=0, keepdims=True)
    base = 2 * WIDTH + QCOLS + 2 * HEAD_A
    draw = exact_dot(dsteps, parts["sel"], COLS)
    dp_ref[:, base + 2 * STATE :] = draw.astype(low)

    sig, pre = parts["chans_sig"], parts["chans_pre"]
    dpre = dchans * sig * (1.0 + pre * (1.0 - sig))
    back, rows = conv_backward(dpre, parts["wide"], parts["conv"], pos)
    dp_ref[:, WIDTH : 2 * WIDTH] = back.astype(low)
    rows.append(jnp.sum(dy * chans, axis=0, keepdims=True))
    rows = jnp.concatenate(rows + [jnp.zeros((2, WIDTH), jnp.float32)], axis=0)
    dheads_ref[...] = head_rows(rows, dlog, dbias)

    dinner = jnp.where(parts["same"], dinner, 0.0)
    dstates = jnp.concatenate(
        [exact_dot(dinner, parts["out_state"], ROWS), exact_dot(dinner, parts["in_state"])],
        axis=1,
    )
    sig, pre = parts["states_sig"], parts["states_pre"]
    dpre = dstates * sig * (1.0 + pre * (1.0 - sig))
    back, rows = conv_backward(dpre, parts["states"], parts["bc"], pos)
    dp_ref[:, base : base + 2 * STATE] = back.astype(low)
    dbc_ref[...] = jnp.concatenate(rows, axis=0)

    pairs, keys, values = attention_parts(p_ref, cos_ref, sin_ref)
    cosine, sine = cos_ref[...], sin_ref[...]
    dkeys = [jnp.zeros((length, LANES), jnp.float32) for _ in range(2)]
    dvalues = [jnp.zeros((length, LANES), jnp.float32) for _ in range(2)]
    for i, query in enumerate(pairs):
        a = WIDTH + i * LANES
        datt = grad_all[:, a : a + LANES].astype(jnp.bfloat16)
        dquery = jnp.zeros((length, LANES), jnp.float32)
        for which in range(2):
            probs = attention_probs(query, keys[which], parts["same"])
            dprobs = low_dot(datt, values[which], COLS)
            dscores = probs * (dprobs - jnp.sum(probs * dprobs, axis=1, keepdims=True))
            dscores = dscores.astype(jnp.bfloat16)
            dquery = dquery + low_dot(dscores, keys[which])
            dkeys[which] = dkeys[which] + low_dot(dscores, query, ROWS)
            dvalues[which] = dvalues[which] + low_dot(probs, datt, ROWS)
        a = 2 * WIDTH + i * LANES
        dquery = turn_back(dquery * HEAD_A ** (-0.5), cosine, sine)
        dp_ref[:, a : a + LANES] = dquery.astype(low)
    dkey = half_lanes(dkeys[0], 0) + pltpu.roll(half_lanes(dkeys[1], 1), HEAD_A, 1)
    dvalue = pltpu.roll(half_lanes(dvalues[0], 0), HEAD_A, 1) + half_lanes(dvalues[1], 1)
    a = 2 * WIDTH + QCOLS
    dboth = half_lanes(turn_back(dkey, cosine, sine), 0) + dvalue
    dp_ref[:, a : a + LANES] = dboth.astype(low)
    half = dp_ref.shape[1] // 2
    split_columns(dp_ref[:, :half], dp_ref[:, half:], tidx_ref[1], keep_ref, give_ref)


def local_call(kernel, outs, name, scalars=0, after=0):
    space = pl.BlockSpec(memory_space=pltpu.VMEM)
    scalar = pl.BlockSpec(memory_space=pltpu.SMEM)
    return lambda *args: pl.pallas_call(
        kernel,
        out_shape=[jax.ShapeDtypeStruct(shape, dtype) for shape, dtype in outs],
        in_specs=[scalar] * scalars
        + [space] * (len(args) - scalars - after)
        + [pl.BlockSpec(memory_space=pl.ANY)] * after,
        out_specs=[space] * len(outs),
        compiler_params=pltpu.CompilerParams(vmem_limit_bytes=56 * 2**20),
        name=name,
    )(*args)


def mixer_consts(head_params, conv_shared, lens, where, length):
    _, pos = doc_index(lens, length)
    half = HEAD_A // 2
    freq = THETA ** (-jnp.arange(half, dtype=jnp.float32) * 2.0 / HEAD_A)
    angle = pos.astype(jnp.float32)[:, None] * freq[None, :]
    cosine, sine = jnp.cos(angle), jnp.sin(angle)
    heads = jnp.pad(
        head_params, ((0, 16 - HEADS), (0, 3 * LANES - head_params.shape[1]))
    )
    scalars = (where, lens)
    return scalars, (
        heads,
        conv_shared,
        jnp.concatenate([cosine] * 4, axis=1),
        jnp.concatenate([-sine, sine, -sine, sine], axis=1),
    )


def mixer_forward(projected, consts, weight):
    length = projected.shape[0]
    width = WIDTH + QCOLS
    outs = [
        ((length, width), jnp.bfloat16),
        ((length, WIDTH), jnp.float32),
        ((length // 2, weight.shape[0]), jnp.float32),
        ((length // 2, weight.shape[0]), jnp.bfloat16),
        ((length, width // 2), jnp.bfloat16),
        ((length, width // 2), jnp.bfloat16),
    ]
    scalars, arrays = consts
    return local_call(forward_kernel, outs, "mixer_forward", 2)(
        *scalars, projected, *arrays, weight
    )


def mixer_backward(projected, consts, outputs, grad, weight):
    length, width = projected.shape
    outs = [
        ((length, width), jnp.bfloat16),
        ((16, 3 * LANES), jnp.float32),
        ((CONV + 1, 2 * STATE), jnp.float32),
        ((length, width // 2), jnp.bfloat16),
        ((length, width // 2), jnp.bfloat16),
    ]
    scalars, arrays = consts
    grad_proj, heads, bc, keep, give = local_call(backward_kernel, outs, "mixer_backward", 2)(
        *scalars, projected, *arrays, outputs, grad, weight
    )
    return grad_proj, heads[:HEADS, : BIAS_COL + 1], bc, keep, give


def feed_kernel(
    where_ref, x_ref, grad_ref, w_ref,
    act_ref, dgu_ref, mine_ref, theirs_ref, keep_ref, give_ref, act_keep_ref, act_give_ref,
):
    units = act_ref.shape[1]
    tidx, core = where_ref[0], where_ref[1]
    gate_up = dot(x_ref[...], w_ref[:, : 2 * units])
    gate, upper = gate_up[:, :units], gate_up[:, units:]
    sig = jax.nn.sigmoid(gate)
    raised = gate * sig
    act = (raised * upper).astype(act_ref.dtype)
    act_ref[...] = act
    split_columns(act[:, : units // 2], act[:, units // 2 :], core, act_keep_ref, act_give_ref)
    grad = dot(grad_ref[...], w_ref[:, 2 * units : 3 * units])
    dgate = (grad * upper * sig * (1.0 + gate * (1.0 - sig))).astype(dgu_ref.dtype)
    dupper = (grad * raised).astype(dgu_ref.dtype)
    dgu_ref[:, :units] = dgate
    dgu_ref[:, units:] = dupper
    split_columns(dgate, dupper, core, keep_ref, give_ref)
    split_rows(dot_t(dgu_ref[...], w_ref[:, : 2 * units]), tidx, mine_ref, theirs_ref)


def feed_forward_back(where, values, grad, weight, units):
    length, width = values.shape
    low = jnp.bfloat16
    outs = [
        ((length, units), low),
        ((length, 2 * units), low),
        ((length // 2, width), jnp.float32),
        ((length // 2, width), low),
        ((length, units), low),
        ((length, units), low),
        ((length, units // 2), low),
        ((length, units // 2), low),
    ]
    return local_call(feed_kernel, outs, "feed_forward_back", 1)(where, values, grad, weight)


def middle_back(mine, taken, middle, gain, out_grad, *after):
    low = jnp.bfloat16

    def kernel(mine_ref, taken_ref, middle_ref, gain_ref, out_ref, *refs):
        grad_ref, low_ref, gain_grad_ref = refs[len(after) :]
        grad = mine_ref[...] + taken_ref[...].astype(jnp.float32)
        values = middle_ref[...]
        total = out_ref[...] + norm_back(values, gain_ref[...], grad)
        grad_ref[...] = total
        low_ref[...] = total.astype(low)
        gain_grad_ref[...] = jnp.sum(grad * values * norm_scale(values), axis=0, keepdims=True)

    shape = middle.shape
    outs = [(shape, jnp.float32), (shape, low), ((1, shape[1]), jnp.float32)]
    return local_call(kernel, outs, "middle_back", 0, len(after))(
        mine, taken, middle, gain[None, :], out_grad, *after
    )


def first_back(where, grad_proj, weight, resid, *after):
    def kernel(where_ref, dp_ref, w_ref, resid_ref, *refs):
        mine_ref, theirs_ref, gain_grad_ref = refs[len(after) :]
        grad = dot_t(dp_ref[...], w_ref[:, : dp_ref.shape[1]])
        values = resid_ref[...]
        gain_grad_ref[...] = jnp.sum(grad * values * norm_scale(values), axis=0, keepdims=True)
        split_rows(grad, where_ref[0], mine_ref, theirs_ref)

    rows, width = resid.shape
    outs = [
        ((rows // 2, width), jnp.float32),
        ((rows // 2, width), jnp.bfloat16),
        ((1, width), jnp.float32),
    ]
    return local_call(kernel, outs, "first_back", 1, len(after))(
        where, grad_proj, weight, resid, *after
    )


def feed_out(where, act, weight, *after):
    def kernel(where_ref, act_ref, w_ref, *refs):
        units = act_ref.shape[1]
        out = dot_t(act_ref[...], w_ref[:, 2 * units :])
        split_rows(out, where_ref[0], *refs[len(after) :])

    rows, width = act.shape[0] // 2, weight.shape[0]
    outs = [((rows, width), jnp.float32), ((rows, width), jnp.bfloat16)]
    return local_call(kernel, outs, "feed_out", 1, len(after))(where, act, weight, *after)


def weight_grads(sides, dtype):
    width = sum(side[1].shape[1] for side in sides)
    model = sides[0][0].shape[1]
    block = 256

    def kernel(*refs):
        out_ref, a = refs[-1], 0
        for i in range(len(sides)):
            x, y, other_x, other_y = refs[4 * i : 4 * i + 4]
            b = a + y.shape[1]
            for r in range(0, model, block):
                part = cross(x[:, r : r + block], y[...])
                part = part + cross(other_x[:, r : r + block], other_y[...])
                out_ref[r : r + block, a:b] = part.astype(out_ref.dtype)
            a = b

    flat = [value for side in sides for value in side]
    return local_call(kernel, [((model, width), dtype)], "weight_grads")(*flat)[0]


def cross(left, right):
    return lax.dot_general(
        left, right, (((0,), (0,)), ((), ())), preferred_element_type=jnp.float32
    )


def dot(left, right):
    return jnp.dot(left, right, preferred_element_type=jnp.float32)


def dot_t(left, right):
    return lax.dot_general(
        left, right, (((1,), (1,)), ((), ())), preferred_element_type=jnp.float32
    )


def adamw(weight, first, second, grad, rate, decay):
    first = 0.9 * first + 0.1 * grad
    second = 0.95 * second + 0.05 * grad * grad
    fixed_one = first / (1.0 - 0.9**STEP)
    fixed_two = second / (1.0 - 0.95**STEP)
    weight = weight - rate * (fixed_one / (jnp.sqrt(fixed_two) + 1e-08) + decay * weight)
    return (first, second, weight)


def swap(values, axis, distance):
    count = lax.axis_size(axis)
    return lax.ppermute(values, axis, [(i, i ^ distance) for i in range(count)])


def pair_rows(own, other, tidx):
    return jnp.where(
        tidx == 0,
        jnp.concatenate([own, other], axis=0),
        jnp.concatenate([other, own], axis=0),
    )


def gather_rows(own, tidx):
    return pair_rows(own, swap(own, "tensor", 1), tidx)


RING_CHIPS = 8


def ring_chip(place):
    place = place % RING_CHIPS
    half = RING_CHIPS // 2
    if isinstance(place, int):
        return 2 * place if place < half else 2 * (RING_CHIPS - 1 - place) + 1
    return jnp.where(place < half, 2 * place, 2 * (RING_CHIPS - 1 - place) + 1)


def ring_place(chip):
    return jnp.where(chip % 2 == 0, chip // 2, RING_CHIPS - 1 - chip // 2)


def ring_step(values):
    pairs = []
    for p in range(RING_CHIPS):
        pairs.append((CORES * ring_chip(p), CORES * ring_chip(p + 1)))
        pairs.append((CORES * ring_chip(p + 1) + 1, CORES * ring_chip(p) + 1))
    return lax.ppermute(values, "dp", pairs)


def place_rows(pieces, blocks, values=None, columns=0):
    count = len(pieces)
    height, width = pieces[0].shape
    low = pieces[0].dtype
    extra = [] if values is None else [values]

    def kernel(block_ref, *refs):
        out_ref = refs[count + len(extra)]
        for i in range(count):
            start = pl.multiple_of(block_ref[i] * height, height)
            out_ref[pl.ds(start, height), :] = refs[i][...]
        if extra:
            refs[-1][...] = dot(refs[count][...], out_ref[:, :columns]).astype(low)

    outs = [((count * height, width), low)]
    if extra:
        outs.append(((values.shape[0], columns), low))
    return local_call(kernel, outs, "place_rows", 1)(blocks, *pieces, *extra)


def ring_gather(shard, place, core):
    way = 1 - 2 * core
    own = [shard]
    other = [swap(shard, "dp", 1)]
    for _ in range(1, RING_CHIPS):
        own.append(ring_step(own[-1]))
        other.append(swap(own[-1], "dp", 1))
    blocks = [CORES * ring_chip(place - way * k) + core for k in range(RING_CHIPS)]
    blocks += [CORES * ring_chip(place + way * k) + 1 - core for k in range(RING_CHIPS)]
    return own + other, jnp.stack(blocks).astype(jnp.int32), own


def ring_reduce(chains, place, core, rider, last):
    way = 1 - 2 * core
    sums = [None] * len(chains)
    riders = [rider]
    for step in range(1, RING_CHIPS + 1):
        chip = ring_chip(place - way * step)
        for i, chain in enumerate(chains):
            if step == RING_CHIPS and i == 0:
                sums[0], last = lax.optimization_barrier((sums[0], last))
            parts = []
            for grad, a, b in chain:
                rows = grad.shape[0] // RING_CHIPS
                parts.append(lax.dynamic_slice(grad, (chip * rows, a), (rows, b - a)))
            part = parts[0] if len(parts) == 1 else jnp.concatenate(parts, axis=1)
            if step > 1:
                part = part + sums[i].astype(jnp.float32)
            if step < RING_CHIPS:
                part = part.astype(jnp.bfloat16)
                if i == 1:
                    width = part.shape[1]
                    part = ring_step(jnp.concatenate([part, riders[-1]], axis=1))
                    riders.append(part[:, width:])
                    part = part[:, :width]
                else:
                    part = ring_step(part)
            sums[i] = part
        if step == 1:
            first = sums[0]
    stack = jnp.stack(riders)
    total = 0.0
    for p in range(RING_CHIPS):
        taken = lax.dynamic_index_in_dim(
            stack, (way * (place - p)) % RING_CHIPS, axis=0, keepdims=False
        )
        total = total + taken.astype(jnp.float32)
    return jnp.concatenate(sums, axis=1), total, first, last


def both_cores(model_side, keep, give):
    return model_side, keep, swap(model_side, "dp", 1), swap(give, "dp", 1)


def own_rows(summed, core, extra=None):
    rows = summed.shape[0] // CORES
    upper, lower = summed[:rows], summed[rows:]
    mine = jnp.where(core == 0, upper, lower)
    give = jnp.where(core == 0, lower, upper).astype(jnp.bfloat16)
    if extra is None:
        taken = swap(give, "dp", 1).astype(jnp.float32)
        return jnp.where(core == 0, mine, taken), jnp.where(core == 0, taken, mine)
    width = give.shape[1]
    extra = extra.astype(jnp.bfloat16)
    taken = swap(jnp.concatenate([give, extra], axis=1), "dp", 1)
    extra = extra.astype(jnp.float32) + taken[:, width:].astype(jnp.float32)
    taken = taken[:, :width].astype(jnp.float32)
    return jnp.where(core == 0, mine, taken), jnp.where(core == 0, taken, mine), extra


def join_halves(halves, a, b):
    return jnp.concatenate([halves[0][:, a:b], halves[1][:, a:b]], axis=1)


def sum_all(values, axis):
    distance = 1
    while distance < lax.axis_size(axis):
        values = values + swap(values, axis, distance)
        distance *= 2
    return values


def per_device(
    residual,
    out_grad,
    doc_lengths,
    mixer_weight,
    mixer_first,
    mixer_second,
    scan_weight,
    scan_first,
    scan_second,
    merge_weight,
    merge_first,
    merge_second,
    hidden_weight,
    hidden_first,
    hidden_second,
    down_weight,
    down_first,
    down_second,
    head_params,
    head_first,
    head_second,
    shared_params,
    shared_first,
    shared_second,
):
    low = jnp.bfloat16
    tidx = lax.axis_index("tensor")
    count = lax.axis_size("dp")
    chips = count // CORES
    core = lax.axis_index("dp") % CORES
    place = ring_place(lax.axis_index("dp") // CORES)
    group = residual.shape[0] * lax.axis_size("tensor")
    conv_shared = shared_params[2 * D :].reshape(CONV + 1, 2 * STATE)

    ring = chips == RING_CHIPS
    mix_cols = mixer_weight.shape[1]
    both_cols = mix_cols + scan_weight.shape[1]
    spare = jnp.zeros((mixer_weight.shape[0], -both_cols % 256), low)
    first_cols = both_cols + spare.shape[1]
    units = down_weight.shape[0]
    first_shard = jnp.concatenate(
        [mixer_weight.astype(low), scan_weight.astype(low), spare, merge_weight.astype(low).T],
        axis=1,
    )
    rest_shard = jnp.concatenate(
        [hidden_weight.astype(low), down_weight.astype(low).T], axis=1
    )
    where = jnp.stack([tidx, core]).astype(jnp.int32)
    consts = mixer_consts(head_params, conv_shared, doc_lengths[0], where, group)
    gain_one, gain_two = shared_params[:D], shared_params[D : 2 * D]
    resid_all = gather_rows(residual, tidx)
    first_all = scaled_norm(resid_all, gain_one).astype(low)
    grad_feed = gather_rows(out_grad.astype(low), tidx)
    if ring:
        pieces, blocks, own = ring_gather(first_shard, place, core)
        first_w, projected = place_rows(pieces, blocks, first_all, first_cols)
        rest_shard = lax.optimization_barrier((rest_shard, own[4]))[0]
    else:
        first_w = lax.all_gather(first_shard, "dp", axis=0, tiled=True)
        projected = dot(first_all, first_w[:, :first_cols]).astype(low)
    rest_w = lax.all_gather(rest_shard, "dp", axis=0, tiled=True)
    merge_w = first_w[:, first_cols:]
    joined_low, outputs, mine, theirs, joined_keep, joined_give = mixer_forward(
        projected, consts, first_w
    )
    middle = residual + mine + swap(theirs, "tensor", 1).astype(jnp.float32)
    second_all = gather_rows(scaled_norm(middle, gain_two).astype(low), tidx)
    activ_low, grad_gu, mine, theirs, gu_keep, gu_give, act_keep, act_give = feed_forward_back(
        where, second_all, grad_feed, rest_w, units
    )
    taken = swap(theirs, "tensor", 1)
    waits = []
    if ring:
        rest_grad = weight_grads(
            [
                both_cores(second_all, gu_keep, gu_give),
                both_cores(grad_feed, act_keep, act_give),
            ],
            low,
        )
        rest_sum = lax.psum_scatter(
            rest_grad,
            "dp",
            scatter_dimension=0,
            axis_index_groups=[[i * CORES + c for i in range(chips)] for c in range(CORES)],
            tiled=True,
        )
        waits = [rest_grad]
    grad_middle, grad_low, gain_two_grad = middle_back(
        mine, taken, middle, gain_two, out_grad, *waits
    )
    grad_mixed = gather_rows(grad_low, tidx)
    grad_proj, head_grad, conv_grad, proj_keep, proj_give = mixer_backward(
        projected, consts, outputs, grad_mixed, first_w
    )
    waits = []
    if ring:
        first_grad = weight_grads([both_cores(first_all, proj_keep, proj_give)], jnp.float32)
        waits = [first_grad]
    mine_first, theirs_first, gain_one_grad = first_back(
        where, grad_proj, first_w, resid_all, *waits
    )
    gain_one_grad, gain_two_grad = gain_one_grad.reshape(-1), gain_two_grad.reshape(-1)
    waits = []
    shared_part = jnp.concatenate([gain_one_grad, gain_two_grad, conv_grad.reshape(-1)])
    small = jnp.concatenate([shared_part, head_grad.reshape(-1)])
    if ring:
        rest_halves = own_rows(rest_sum.astype(jnp.float32), core)
        hidden_sum = join_halves(rest_halves, 0, units)
        down_sum = join_halves(rest_halves, units, rest_sum.shape[1]).T
        hidden_new = adamw(hidden_weight, hidden_first, hidden_second, hidden_sum, 0.02, 0.1)
        down_new = adamw(down_weight, down_first, down_second, down_sum, 0.02, 0.1)
        merge_grad = weight_grads([both_cores(grad_mixed, joined_keep, joined_give)], jnp.float32)
        a = first_cols // CORES
        cut = (a + merge_grad.shape[1]) // 2 // 128 * 128
        chains = [
            [(first_grad, 0, cut)],
            [(first_grad, cut, a), (merge_grad, 0, merge_grad.shape[1])],
        ]
        rows = D // RING_CHIPS
        rider = jnp.pad(small.astype(low), (0, rows * LANES - small.shape[0]))
        first_sum, small_sum, mark, (hidden_new, down_new) = ring_reduce(
            chains, place, core, rider.reshape(rows, LANES), (hidden_new, down_new)
        )
        waits = [mark]
        half = rows // CORES
        small_sum = jnp.concatenate([small_sum[:half], small_sum[half:]], axis=1)
        first_halves = own_rows(first_sum, core, small_sum)
        merge_sum = join_halves(first_halves, a, first_sum.shape[1]).T
        first_sum = join_halves(first_halves, 0, a)
    else:
        whole = jnp.concatenate(
            [
                cross(first_all, grad_proj),
                cross(second_all, grad_gu),
                cross(grad_feed, activ_low),
                cross(grad_mixed, joined_low),
            ],
            axis=1,
        ).astype(low)
        whole = lax.psum_scatter(whole, "dp", scatter_dimension=0, tiled=True)
        whole = whole.astype(jnp.float32)
        a = grad_proj.shape[1]
        first_sum = whole[:, :a]
        hidden_sum = whole[:, a : a + 2 * units]
        a = a + 2 * units
        down_sum = whole[:, a : a + units].T
        merge_sum = whole[:, a + units :].T
        hidden_new = adamw(hidden_weight, hidden_first, hidden_second, hidden_sum, 0.02, 0.1)
        down_new = adamw(down_weight, down_first, down_second, down_sum, 0.02, 0.1)
    mixer_sum, scan_sum = first_sum[:, :mix_cols], first_sum[:, mix_cols:both_cols]
    split = shared_part.shape[0]
    if ring:
        both = jnp.concatenate([scan_sum, first_halves[2]], axis=1)
        taken = swap(both, "tensor", 1)
        scan_sum = scan_sum + taken[:, : scan_sum.shape[1]]
        own_sum = jnp.concatenate([first_halves[2][:, :LANES], first_halves[2][:, LANES:]], axis=0)
        taken = taken[:, scan_sum.shape[1] :]
        taken = jnp.concatenate([taken[:, :LANES], taken[:, LANES:]], axis=0)
        shared_sum = (own_sum + taken).reshape(-1)[:split]
        head_sum = own_sum.reshape(-1)[split : small.shape[0]].reshape(head_grad.shape)
    else:
        scan_sum = scan_sum + swap(scan_sum, "tensor", 1)
        small = sum_all(small, "dp")
        shared_sum = sum_all(small[:split], "tensor")
        head_sum = small[split:].reshape(head_grad.shape)
    grad_first = mine_first + swap(theirs_first, "tensor", 1).astype(jnp.float32)
    input_grad = grad_middle + norm_back(residual, gain_one, grad_first)
    mine, theirs = feed_out(where, activ_low, rest_w, *waits)
    block_out = middle + mine + swap(theirs, "tensor", 1).astype(jnp.float32)

    mixer_new = adamw(mixer_weight, mixer_first, mixer_second, mixer_sum, 0.02, 0.1)
    scan_new = adamw(scan_weight, scan_first, scan_second, scan_sum, 0.02, 0.1)
    merge_new = adamw(merge_weight, merge_first, merge_second, merge_sum, 0.02, 0.1)
    head_new = adamw(head_params, head_first, head_second, head_sum, 0.2, 0.0)
    shared_new = adamw(shared_params, shared_first, shared_second, shared_sum, 0.2, 0.0)
    return (
        block_out,
        input_grad,
        *mixer_new,
        *scan_new,
        *merge_new,
        *hidden_new,
        *down_new,
        *head_new,
        *shared_new,
    )


def solution(mesh):
    return jax.shard_map(
        per_device,
        mesh=mesh,
        in_specs=(
            P(("dp", "tensor"), None),
            P(("dp", "tensor"), None),
            P("dp", None),
            P("dp", "tensor"),
            P("dp", "tensor"),
            P("dp", "tensor"),
            P("dp", None),
            P("dp", None),
            P("dp", None),
            P("tensor", "dp"),
            P("tensor", "dp"),
            P("tensor", "dp"),
            P("dp", "tensor"),
            P("dp", "tensor"),
            P("dp", "tensor"),
            P("tensor", "dp"),
            P("tensor", "dp"),
            P("tensor", "dp"),
            P("tensor", None),
            P("tensor", None),
            P("tensor", None),
            P(),
            P(),
            P(),
        ),
        out_specs=(
            P(("dp", "tensor"), None),
            P(("dp", "tensor"), None),
            P("dp", "tensor"),
            P("dp", "tensor"),
            P("dp", "tensor"),
            P("dp", None),
            P("dp", None),
            P("dp", None),
            P("tensor", "dp"),
            P("tensor", "dp"),
            P("tensor", "dp"),
            P("dp", "tensor"),
            P("dp", "tensor"),
            P("dp", "tensor"),
            P("tensor", "dp"),
            P("tensor", "dp"),
            P("tensor", "dp"),
            P("tensor", None),
            P("tensor", None),
            P("tensor", None),
            P(),
            P(),
            P(),
        ),
        check_vma=False,
    )
```

```python
import jax
import jax.numpy as jnp
from jax import lax
from jax.experimental import pallas as pl
from jax.experimental.pallas import tpu as pltpu
from jax.sharding import PartitionSpec as P

D = 1024
HEADS_M = 24
HEAD_M = 64
STATE = 128
CONV = 4
HEADS_Q = 8
HEADS_KV = 2
HEAD_A = 64
STEP = 10
CORES = 2


EPS = 1e-05
THETA = 10000.0
HIGH = lax.Precision.HIGHEST


def scaled_norm(values, gain):
    return values * lax.rsqrt(jnp.mean(values * values, axis=-1, keepdims=True) + EPS) * gain


def norm_scale(values):
    return lax.rsqrt(jnp.mean(values * values, axis=-1, keepdims=True) + EPS)


def norm_back(values, gain, grad):
    scale = norm_scale(values)
    scaled = grad * gain
    inner = jnp.mean(values * scaled, axis=-1, keepdims=True)
    return scale * scaled - values * (scale * scale * scale * inner)


def doc_index(lens, count):
    place = jnp.arange(count, dtype=jnp.int32)
    ends = jnp.cumsum(lens)
    after = place[:, None] >= ends[None, :]
    seg = jnp.sum(after.astype(jnp.int32), axis=1)
    start = jnp.sum(jnp.where(after, lens[None, :], 0), axis=1)
    return (seg, place - start)


HEADS = HEADS_M // 2
WIDTH = HEADS * HEAD_M
QCOLS = HEADS_Q // 2 * HEAD_A
LANES = 128
RATE_COL = (CONV + 1) * HEAD_M
SKIP_COL = RATE_COL + 1
BIAS_COL = RATE_COL + 2


def exact_dot(left, right, dims=((1,), (0,))):
    return lax.dot_general(
        left, right, (dims, ((), ())), precision=HIGH, preferred_element_type=jnp.float32
    )


def low_dot(left, right, dims=((1,), (0,))):
    return lax.dot_general(
        left.astype(jnp.bfloat16),
        right.astype(jnp.bfloat16),
        (dims, ((), ())),
        preferred_element_type=jnp.float32,
    )


ROWS = ((0,), (0,))
COLS = ((1,), (1,))


def lane_of(shape):
    return lax.broadcasted_iota(jnp.int32, shape, 1)


def shifted(values, pos, shift):
    return jnp.where(pos >= shift, pltpu.roll(values, shift, 0), 0.0)


def conv_forward(values, rows, pos):
    total = rows[CONV : CONV + 1] + rows[CONV - 1 : CONV] * values
    for shift in range(1, CONV):
        tap = rows[CONV - 1 - shift : CONV - shift]
        total = total + tap * shifted(values, pos, shift)
    return total


def conv_backward(grad, values, rows, pos):
    length = values.shape[0]
    back = rows[CONV - 1 : CONV] * grad
    taps = [jnp.sum(grad * values, axis=0, keepdims=True)]
    for shift in range(1, CONV):
        tap = rows[CONV - 1 - shift : CONV - shift]
        kept = jnp.where(pos >= shift, grad, 0.0)
        back = back + tap * pltpu.roll(kept, length - shift, 0)
        taps.append(jnp.sum(kept * pltpu.roll(values, shift, 0), axis=0, keepdims=True))
    return back, taps[::-1] + [jnp.sum(grad, axis=0, keepdims=True)]


def swap_pairs(values):
    first = lane_of(values.shape) % HEAD_A < HEAD_A // 2
    half = HEAD_A // 2
    return jnp.where(first, pltpu.roll(values, LANES - half, 1), pltpu.roll(values, half, 1))


def turn(values, cosine, sine):
    return values * cosine + swap_pairs(values) * sine


def turn_back(values, cosine, sine):
    return values * cosine + swap_pairs(values * sine)


def half_lanes(values, which):
    mine = lane_of(values.shape) // HEAD_A == which
    return jnp.where(mine, values, jnp.zeros_like(values))


def column_to_lanes(column):
    shape = (column.shape[0], LANES)
    row = lax.broadcasted_iota(jnp.int32, shape, 0)
    mine = (row == lane_of(shape)) & (row < HEADS)
    return jnp.sum(jnp.where(mine, column, 0.0), axis=0, keepdims=True)


def conv_rows(heads_ref):
    tiles = [heads_ref[:, j * LANES : (j + 1) * LANES] for j in range(3)]
    rolled = [pltpu.roll(tile, HEAD_M, 1) for tile in tiles]
    left = lane_of((1, LANES)) < HEAD_M
    rows = []
    for k in range(CONV + 1):
        kinds = (tiles[k // 2], rolled[k // 2])
        even, odd = kinds[k % 2], kinds[1 - k % 2]
        pieces = [
            jnp.where(left, even[h : h + 1], odd[h + 1 : h + 2]) for h in range(0, HEADS, 2)
        ]
        rows.append(jnp.concatenate(pieces, axis=1))
    skip = heads_ref[:, SKIP_COL : SKIP_COL + 1]
    pieces = [jnp.where(left, skip[h : h + 1], skip[h + 1 : h + 2]) for h in range(0, HEADS, 2)]
    rows.append(jnp.concatenate(pieces, axis=1))
    return jnp.concatenate(rows + [jnp.zeros((2, WIDTH), jnp.float32)], axis=0)


def head_rows(rows, dlog, dbias):
    left = lane_of((1, LANES)) < HEAD_M
    lane = lane_of((1, LANES))
    out = []
    for i in range(HEADS // 2):
        tile = rows[:, i * LANES : (i + 1) * LANES]
        kinds = (tile, pltpu.roll(tile, HEAD_M, 1))
        for which in range(2):
            h = 2 * i + which
            piece = [kinds[(which + k) % 2][k : k + 1] for k in range(CONV + 1)]
            dskip = jnp.sum(
                half_lanes(tile[CONV + 1 : CONV + 2], which), axis=1, keepdims=True
            )
            last = jnp.where(lane == HEAD_M, dlog[:, h : h + 1], 0.0)
            last = jnp.where(lane == HEAD_M + 1, dskip, last)
            last = jnp.where(lane == HEAD_M + 2, dbias[:, h : h + 1], last)
            tiles = [
                jnp.where(left, piece[0], piece[1]),
                jnp.where(left, piece[2], piece[3]),
                jnp.where(left, piece[4], last),
            ]
            out.append(jnp.concatenate(tiles, axis=1))
    out.append(jnp.zeros((16 - HEADS, 3 * LANES), jnp.float32))
    return jnp.concatenate(out, axis=0)


def documents(lens_ref, place):
    seg, start, end = jnp.zeros_like(place), jnp.zeros_like(place), 0
    for k in range(lens_ref.shape[0]):
        end = end + lens_ref[k]
        after = place >= end
        seg = seg + jnp.where(after, 1, 0)
        start = start + jnp.where(after, lens_ref[k], 0)
    return seg, place - start


def split_rows(values, tidx, mine_ref, theirs_ref):
    half = values.shape[0] // 2
    upper, lower = values[:half], values[half:]
    mine_ref[...] = jnp.where(tidx == 0, upper, lower)
    theirs_ref[...] = jnp.where(tidx == 0, lower, upper).astype(theirs_ref.dtype)


def split_columns(left, right, core, keep_ref, give_ref):
    keep_ref[...] = jnp.where(core == 0, left, right)
    give_ref[...] = jnp.where(core == 0, right, left)


def mixer_parts(tidx_ref, lens_ref, p_ref, heads_ref, bc_ref):
    length = p_ref.shape[0]
    base = 2 * WIDTH + QCOLS + 2 * HEAD_A
    conv = conv_rows(heads_ref)
    bc = bc_ref[...]
    row = lax.broadcasted_iota(jnp.int32, (length, length), 0)
    column = lax.broadcasted_iota(jnp.int32, (length, length), 1)
    seg, pos = documents(lens_ref, lax.broadcasted_iota(jnp.int32, (length, 1), 0))
    seg_across, _ = documents(lens_ref, lax.broadcasted_iota(jnp.int32, (1, length), 1))
    same = (seg == seg_across) & (row >= column)
    wide = p_ref[:, WIDTH : 2 * WIDTH].astype(jnp.float32)
    chans_pre = conv_forward(wide, conv, pos)
    chans_sig = jax.nn.sigmoid(chans_pre)
    states = p_ref[:, base : base + 2 * STATE].astype(jnp.float32)
    states_pre = conv_forward(states, bc, pos)
    states_sig = jax.nn.sigmoid(states_pre)
    raw = p_ref[:, base + 2 * STATE : base + 2 * STATE + LANES].astype(jnp.float32)
    i = lax.broadcasted_iota(jnp.int32, (LANES, LANES), 0)
    j = lane_of((LANES, LANES))
    sel = ((i == HEADS * tidx_ref[0] + j) & (j < HEADS)).astype(jnp.float32)
    i = lax.broadcasted_iota(jnp.int32, (LANES, WIDTH), 0)
    spread = (i == lane_of((LANES, WIDTH)) // HEAD_M).astype(jnp.float32)
    rates = column_to_lanes(jnp.exp(heads_ref[:, RATE_COL : RATE_COL + 1]))
    bias = column_to_lanes(heads_ref[:, BIAS_COL : BIAS_COL + 1])
    step_pre = exact_dot(raw, sel) + bias
    steps = jnp.maximum(step_pre, 0.0) + jnp.log1p(jnp.exp(-jnp.abs(step_pre)))
    before = (row >= column).astype(jnp.float32)
    cum = exact_dot(before, -rates * steps)
    steps_wide = exact_dot(steps, spread)
    chans = chans_pre * chans_sig
    states_out = states_pre * states_sig
    in_state, out_state = states_out[:, :STATE], states_out[:, STATE:]
    inner = jnp.where(same, exact_dot(out_state, in_state, COLS), 0.0)
    return dict(
        pos=pos, wide=wide, chans_pre=chans_pre, chans_sig=chans_sig, chans=chans,
        states=states, states_pre=states_pre, states_sig=states_sig, in_state=in_state,
        out_state=out_state, step_pre=step_pre, steps=steps, rates=rates, before=before,
        cum=cum, cum_t=cum.T, same=same, steps_wide=steps_wide, inner=inner, conv=conv, bc=bc,
        sel=sel, spread=spread, weighted=(steps_wide * chans).astype(jnp.bfloat16),
    )


def decay_of(parts, head):
    gap = parts["cum"][:, head : head + 1] - parts["cum_t"][head : head + 1, :]
    return jnp.exp(jnp.minimum(gap, 0.0))


def attention_parts(p_ref, cos_ref, sin_ref):
    cosine, sine = cos_ref[...], sin_ref[...]
    pairs = []
    for i in range(QCOLS // LANES):
        a = 2 * WIDTH + i * LANES
        query = turn(p_ref[:, a : a + LANES].astype(jnp.float32), cosine, sine)
        pairs.append((query * HEAD_A ** (-0.5)).astype(jnp.bfloat16))
    a = 2 * WIDTH + QCOLS
    both = p_ref[:, a : a + LANES].astype(jnp.float32)
    key = half_lanes(turn(both, cosine, sine), 0)
    value = half_lanes(both, 1)
    keys = (key.astype(jnp.bfloat16), pltpu.roll(key, HEAD_A, 1).astype(jnp.bfloat16))
    values = (pltpu.roll(value, HEAD_A, 1).astype(jnp.bfloat16), value.astype(jnp.bfloat16))
    return pairs, keys, values


def attention_probs(query, key, same):
    scores = jnp.where(same, low_dot(query, key, COLS), -1e30)
    top = jnp.max(scores, axis=1, keepdims=True)
    raised = jnp.exp(scores - top)
    return raised / jnp.sum(raised, axis=1, keepdims=True)


def forward_kernel(
    tidx_ref, lens_ref, p_ref, heads_ref, bc_ref, cos_ref, sin_ref, w_ref,
    cat_ref, y_ref, mix_ref, mix_low_ref, keep_ref, give_ref,
):
    parts = mixer_parts(tidx_ref, lens_ref, p_ref, heads_ref, bc_ref)
    for i in range(WIDTH // LANES):
        a = i * LANES
        tile = parts["weighted"][:, a : a + LANES]
        out = jnp.zeros((p_ref.shape[0], LANES), jnp.float32)
        for which in range(2):
            mixed = decay_of(parts, 2 * i + which) * parts["inner"]
            out = out + low_dot(mixed, half_lanes(tile, which))
        y_ref[:, a : a + LANES] = out
        gate = p_ref[:, a : a + LANES].astype(jnp.float32)
        out = out + parts["conv"][CONV + 1 : CONV + 2, a : a + LANES] * parts["chans"][:, a : a + LANES]
        cat_ref[:, a : a + LANES] = (out * gate * jax.nn.sigmoid(gate)).astype(cat_ref.dtype)
    pairs, keys, values = attention_parts(p_ref, cos_ref, sin_ref)
    for i, query in enumerate(pairs):
        out = jnp.zeros((p_ref.shape[0], LANES), jnp.float32)
        for which in range(2):
            probs = attention_probs(query, keys[which], parts["same"])
            out = out + low_dot(probs, values[which])
        a = WIDTH + i * LANES
        cat_ref[:, a : a + LANES] = out.astype(cat_ref.dtype)
    cat = cat_ref[...]
    mix_ref[...] = dot_t(cat, w_ref[:, p_ref.shape[1] :])
    mix_low_ref[...] = mix_ref[...].astype(mix_low_ref.dtype)
    half = cat.shape[1] // 2
    split_columns(cat[:, :half], cat[:, half:], tidx_ref[1], keep_ref, give_ref)


def backward_kernel(
    tidx_ref, lens_ref, p_ref, heads_ref, bc_ref, cos_ref, sin_ref, y_ref, dmix_ref, w_ref,
    dp_ref, dheads_ref, dbc_ref, keep_ref, give_ref,
):
    length = p_ref.shape[0]
    low = dp_ref.dtype
    parts = mixer_parts(tidx_ref, lens_ref, p_ref, heads_ref, bc_ref)
    pos, chans = parts["pos"], parts["chans"]
    gate = p_ref[:, :WIDTH].astype(jnp.float32)
    gate_sig = jax.nn.sigmoid(gate)
    grad_all = dot(dmix_ref[...], w_ref[:, p_ref.shape[1] :])
    grad = grad_all[:, :WIDTH]
    skip = parts["conv"][CONV + 1 : CONV + 2]
    outputs = y_ref[...]
    dgate = grad * (outputs + skip * chans) * gate_sig * (1.0 + gate * (1.0 - gate_sig))
    dp_ref[:, :WIDTH] = dgate.astype(low)
    dy = grad * gate * gate_sig
    dy_low = dy.astype(jnp.bfloat16)
    dweighted = []
    dinner = jnp.zeros((length, length), jnp.float32)
    for i in range(WIDTH // LANES):
        a = i * LANES
        tile = parts["weighted"][:, a : a + LANES]
        out = jnp.zeros((length, LANES), jnp.float32)
        for which in range(2):
            decay = decay_of(parts, 2 * i + which)
            dy_half = half_lanes(dy_low[:, a : a + LANES], which)
            out = out + low_dot(decay * parts["inner"], dy_half, ROWS)
            dinner = dinner + low_dot(dy_half, tile, COLS) * decay
        dweighted.append(out)
    dweighted = jnp.concatenate(dweighted, axis=1)
    spread = parts["spread"]
    weighted = parts["weighted"].astype(jnp.float32)
    dcum = exact_dot(dy_low.astype(jnp.float32) * outputs - weighted * dweighted, spread, COLS)
    dsteps = exact_dot(dweighted * chans, spread, COLS)
    dchans = skip * dy + parts["steps_wide"] * dweighted
    drate = exact_dot(parts["before"], dcum, ROWS)
    dsteps = (dsteps - parts["rates"] * drate) * jax.nn.sigmoid(parts["step_pre"])
    dlog = jnp.sum(-parts["rates"] * parts["steps"] * drate, axis=0, keepdims=True)
    dbias = jnp.sum(dsteps, axis=0, keepdims=True)
    base = 2 * WIDTH + QCOLS + 2 * HEAD_A
    draw = exact_dot(dsteps, parts["sel"], COLS)
    dp_ref[:, base + 2 * STATE :] = draw.astype(low)

    sig, pre = parts["chans_sig"], parts["chans_pre"]
    dpre = dchans * sig * (1.0 + pre * (1.0 - sig))
    back, rows = conv_backward(dpre, parts["wide"], parts["conv"], pos)
    dp_ref[:, WIDTH : 2 * WIDTH] = back.astype(low)
    rows.append(jnp.sum(dy * chans, axis=0, keepdims=True))
    rows = jnp.concatenate(rows + [jnp.zeros((2, WIDTH), jnp.float32)], axis=0)
    dheads_ref[...] = head_rows(rows, dlog, dbias)

    dinner = jnp.where(parts["same"], dinner, 0.0)
    dstates = jnp.concatenate(
        [exact_dot(dinner, parts["out_state"], ROWS), exact_dot(dinner, parts["in_state"])],
        axis=1,
    )
    sig, pre = parts["states_sig"], parts["states_pre"]
    dpre = dstates * sig * (1.0 + pre * (1.0 - sig))
    back, rows = conv_backward(dpre, parts["states"], parts["bc"], pos)
    dp_ref[:, base : base + 2 * STATE] = back.astype(low)
    dbc_ref[...] = jnp.concatenate(rows, axis=0)

    pairs, keys, values = attention_parts(p_ref, cos_ref, sin_ref)
    cosine, sine = cos_ref[...], sin_ref[...]
    dkeys = [jnp.zeros((length, LANES), jnp.float32) for _ in range(2)]
    dvalues = [jnp.zeros((length, LANES), jnp.float32) for _ in range(2)]
    for i, query in enumerate(pairs):
        a = WIDTH + i * LANES
        datt = grad_all[:, a : a + LANES].astype(jnp.bfloat16)
        dquery = jnp.zeros((length, LANES), jnp.float32)
        for which in range(2):
            probs = attention_probs(query, keys[which], parts["same"])
            dprobs = low_dot(datt, values[which], COLS)
            dscores = probs * (dprobs - jnp.sum(probs * dprobs, axis=1, keepdims=True))
            dscores = dscores.astype(jnp.bfloat16)
            dquery = dquery + low_dot(dscores, keys[which])
            dkeys[which] = dkeys[which] + low_dot(dscores, query, ROWS)
            dvalues[which] = dvalues[which] + low_dot(probs, datt, ROWS)
        a = 2 * WIDTH + i * LANES
        dquery = turn_back(dquery * HEAD_A ** (-0.5), cosine, sine)
        dp_ref[:, a : a + LANES] = dquery.astype(low)
    dkey = half_lanes(dkeys[0], 0) + pltpu.roll(half_lanes(dkeys[1], 1), HEAD_A, 1)
    dvalue = pltpu.roll(half_lanes(dvalues[0], 0), HEAD_A, 1) + half_lanes(dvalues[1], 1)
    a = 2 * WIDTH + QCOLS
    dboth = half_lanes(turn_back(dkey, cosine, sine), 0) + dvalue
    dp_ref[:, a : a + LANES] = dboth.astype(low)
    half = dp_ref.shape[1] // 2
    split_columns(dp_ref[:, :half], dp_ref[:, half:], tidx_ref[1], keep_ref, give_ref)


def local_call(kernel, outs, name, scalars=0, after=0):
    space = pl.BlockSpec(memory_space=pltpu.VMEM)
    scalar = pl.BlockSpec(memory_space=pltpu.SMEM)
    return lambda *args: pl.pallas_call(
        kernel,
        out_shape=[jax.ShapeDtypeStruct(shape, dtype) for shape, dtype in outs],
        in_specs=[scalar] * scalars
        + [space] * (len(args) - scalars - after)
        + [pl.BlockSpec(memory_space=pl.ANY)] * after,
        out_specs=[space] * len(outs),
        compiler_params=pltpu.CompilerParams(vmem_limit_bytes=56 * 2**20),
        name=name,
    )(*args)


def mixer_consts(head_params, conv_shared, lens, where, length):
    _, pos = doc_index(lens, length)
    half = HEAD_A // 2
    freq = THETA ** (-jnp.arange(half, dtype=jnp.float32) * 2.0 / HEAD_A)
    angle = pos.astype(jnp.float32)[:, None] * freq[None, :]
    cosine, sine = jnp.cos(angle), jnp.sin(angle)
    heads = jnp.pad(
        head_params, ((0, 16 - HEADS), (0, 3 * LANES - head_params.shape[1]))
    )
    scalars = (where, lens)
    return scalars, (
        heads,
        conv_shared,
        jnp.concatenate([cosine] * 4, axis=1),
        jnp.concatenate([-sine, sine, -sine, sine], axis=1),
    )


def mixer_forward(projected, consts, weight):
    length = projected.shape[0]
    width = WIDTH + QCOLS
    outs = [
        ((length, width), jnp.bfloat16),
        ((length, WIDTH), jnp.float32),
        ((length, weight.shape[0]), jnp.float32),
        ((length, weight.shape[0]), jnp.bfloat16),
        ((length, width // 2), jnp.bfloat16),
        ((length, width // 2), jnp.bfloat16),
    ]
    scalars, arrays = consts
    return local_call(forward_kernel, outs, "mixer_forward", 2)(
        *scalars, projected, *arrays, weight
    )


def mixer_backward(projected, consts, outputs, grad, weight, *after):
    length, width = projected.shape
    outs = [
        ((length, width), jnp.bfloat16),
        ((16, 3 * LANES), jnp.float32),
        ((CONV + 1, 2 * STATE), jnp.float32),
        ((length, width // 2), jnp.bfloat16),
        ((length, width // 2), jnp.bfloat16),
    ]
    scalars, arrays = consts
    kernel = lambda *refs: backward_kernel(*refs[:10], *refs[10 + len(after) :])
    grad_proj, heads, bc, keep, give = local_call(
        kernel, outs, "mixer_backward", 2, len(after)
    )(*scalars, projected, *arrays, outputs, grad, weight, *after)
    return grad_proj, heads[:HEADS, : BIAS_COL + 1], bc, keep, give


def feed_kernel(
    where_ref, x_ref, grad_ref, w_ref,
    act_ref, dgu_ref, dx_ref, dx_low_ref, keep_ref, give_ref, act_keep_ref, act_give_ref,
):
    units = act_ref.shape[1]
    core = where_ref[1]
    gate_up = dot(x_ref[...], w_ref[:, : 2 * units])
    gate, upper = gate_up[:, :units], gate_up[:, units:]
    sig = jax.nn.sigmoid(gate)
    raised = gate * sig
    act = (raised * upper).astype(act_ref.dtype)
    act_ref[...] = act
    split_columns(act[:, : units // 2], act[:, units // 2 :], core, act_keep_ref, act_give_ref)
    grad = dot(grad_ref[...], w_ref[:, 2 * units : 3 * units])
    dgate = (grad * upper * sig * (1.0 + gate * (1.0 - sig))).astype(dgu_ref.dtype)
    dupper = (grad * raised).astype(dgu_ref.dtype)
    dgu_ref[:, :units] = dgate
    dgu_ref[:, units:] = dupper
    split_columns(dgate, dupper, core, keep_ref, give_ref)
    dx_ref[...] = dot_t(dgu_ref[...], w_ref[:, : 2 * units])
    dx_low_ref[...] = dx_ref[...].astype(dx_low_ref.dtype)


def feed_forward_back(where, values, grad, weight, units):
    length, width = values.shape
    low = jnp.bfloat16
    outs = [
        ((length, units), low),
        ((length, 2 * units), low),
        ((length, width), jnp.float32),
        ((length, width), low),
        ((length, units), low),
        ((length, units), low),
        ((length, units // 2), low),
        ((length, units // 2), low),
    ]
    return local_call(feed_kernel, outs, "feed_forward_back", 1)(where, values, grad, weight)


def middle_forward(resid, mix, taken, gain):
    def kernel(resid_ref, mix_ref, taken_ref, gain_ref, middle_ref, normed_ref):
        middle = resid_ref[...] + mix_ref[...] + taken_ref[...].astype(jnp.float32)
        middle_ref[...] = middle
        normed_ref[...] = scaled_norm(middle, gain_ref[...]).astype(normed_ref.dtype)

    outs = [(resid.shape, jnp.float32), (resid.shape, jnp.bfloat16)]
    return local_call(kernel, outs, "middle_forward")(resid, mix, taken, gain[None, :])


def middle_back(where, partial, taken, middle, gain, out_grad, *after):
    low = jnp.bfloat16
    rows, width = middle.shape

    def kernel(where_ref, part_ref, taken_ref, middle_ref, gain_ref, out_ref, *refs):
        grad_ref, low_ref, gain_grad_ref = refs[len(after) :]
        first = where_ref[0] == 0
        grad = part_ref[...] + taken_ref[...].astype(jnp.float32)
        values = middle_ref[...]
        total = out_ref[...] + norm_back(values, gain_ref[...], grad)
        grad_ref[...] = jnp.where(first, total[: rows // 2], total[rows // 2 :])
        low_ref[...] = total.astype(low)
        share = grad * values * norm_scale(values)
        share = jnp.where(first, share[: rows // 2], share[rows // 2 :])
        gain_grad_ref[...] = jnp.sum(share, axis=0, keepdims=True)

    outs = [((rows // 2, width), jnp.float32), ((rows, width), low), ((1, width), jnp.float32)]
    return local_call(kernel, outs, "middle_back", 1, len(after))(
        where, partial, taken, middle, gain[None, :], out_grad, *after
    )


def first_back(where, grad_proj, weight, resid, *after):
    def kernel(where_ref, dp_ref, w_ref, resid_ref, *refs):
        mine_ref, theirs_ref, gain_grad_ref = refs[len(after) :]
        grad = dot_t(dp_ref[...], w_ref[:, : dp_ref.shape[1]])
        values = resid_ref[...]
        gain_grad_ref[...] = jnp.sum(grad * values * norm_scale(values), axis=0, keepdims=True)
        split_rows(grad, where_ref[0], mine_ref, theirs_ref)

    rows, width = resid.shape
    outs = [
        ((rows // 2, width), jnp.float32),
        ((rows // 2, width), jnp.bfloat16),
        ((1, width), jnp.float32),
    ]
    return local_call(kernel, outs, "first_back", 1, len(after))(
        where, grad_proj, weight, resid, *after
    )


def feed_out(where, act, weight, *after):
    def kernel(where_ref, act_ref, w_ref, *refs):
        units = act_ref.shape[1]
        out = dot_t(act_ref[...], w_ref[:, 2 * units :])
        split_rows(out, where_ref[0], *refs[len(after) :])

    rows, width = act.shape[0] // 2, weight.shape[0]
    outs = [((rows, width), jnp.float32), ((rows, width), jnp.bfloat16)]
    return local_call(kernel, outs, "feed_out", 1, len(after))(where, act, weight, *after)


def weight_grads(sides, dtype):
    width = sum(side[1].shape[1] for side in sides)
    model = sides[0][0].shape[1]
    block = 256

    def kernel(*refs):
        out_ref, a = refs[-1], 0
        for i in range(len(sides)):
            x, y, other_x, other_y = refs[4 * i : 4 * i + 4]
            b = a + y.shape[1]
            for r in range(0, model, block):
                part = cross(x[:, r : r + block], y[...])
                part = part + cross(other_x[:, r : r + block], other_y[...])
                out_ref[r : r + block, a:b] = part.astype(out_ref.dtype)
            a = b

    flat = [value for side in sides for value in side]
    return local_call(kernel, [((model, width), dtype)], "weight_grads")(*flat)[0]


def cross(left, right):
    return lax.dot_general(
        left, right, (((0,), (0,)), ((), ())), preferred_element_type=jnp.float32
    )


def dot(left, right):
    return jnp.dot(left, right, preferred_element_type=jnp.float32)


def dot_t(left, right):
    return lax.dot_general(
        left, right, (((1,), (1,)), ((), ())), preferred_element_type=jnp.float32
    )


def adamw(weight, first, second, grad, rate, decay):
    first = 0.9 * first + 0.1 * grad
    second = 0.95 * second + 0.05 * grad * grad
    fixed_one = first / (1.0 - 0.9**STEP)
    fixed_two = second / (1.0 - 0.95**STEP)
    weight = weight - rate * (fixed_one / (jnp.sqrt(fixed_two) + 1e-08) + decay * weight)
    return (first, second, weight)


def swap(values, axis, distance):
    count = lax.axis_size(axis)
    return lax.ppermute(values, axis, [(i, i ^ distance) for i in range(count)])


def pair_rows(own, other, tidx):
    return jnp.where(
        tidx == 0,
        jnp.concatenate([own, other], axis=0),
        jnp.concatenate([other, own], axis=0),
    )


def gather_rows(own, tidx):
    return pair_rows(own, swap(own, "tensor", 1), tidx)


RING_CHIPS = 8


def ring_chip(place):
    place = place % RING_CHIPS
    half = RING_CHIPS // 2
    if isinstance(place, int):
        return 2 * place if place < half else 2 * (RING_CHIPS - 1 - place) + 1
    return jnp.where(place < half, 2 * place, 2 * (RING_CHIPS - 1 - place) + 1)


def ring_place(chip):
    return jnp.where(chip % 2 == 0, chip // 2, RING_CHIPS - 1 - chip // 2)


def ring_step(values):
    pairs = []
    for p in range(RING_CHIPS):
        pairs.append((CORES * ring_chip(p), CORES * ring_chip(p + 1)))
        pairs.append((CORES * ring_chip(p + 1) + 1, CORES * ring_chip(p) + 1))
    return lax.ppermute(values, "dp", pairs)


def place_rows(pieces, blocks, values=None, columns=0):
    count = len(pieces)
    height, width = pieces[0].shape
    low = pieces[0].dtype
    extra = [] if values is None else [values]

    def kernel(block_ref, *refs):
        out_ref = refs[count + len(extra)]
        for i in range(count):
            start = pl.multiple_of(block_ref[i] * height, height)
            out_ref[pl.ds(start, height), :] = refs[i][...]
        if extra:
            refs[-1][...] = dot(refs[count][...], out_ref[:, :columns]).astype(low)

    outs = [((count * height, width), low)]
    if extra:
        outs.append(((values.shape[0], columns), low))
    return local_call(kernel, outs, "place_rows", 1)(blocks, *pieces, *extra)


def ring_gather(shard, place, core):
    way = 1 - 2 * core
    own = [shard]
    other = [swap(shard, "dp", 1)]
    for _ in range(1, RING_CHIPS):
        own.append(ring_step(own[-1]))
        other.append(swap(own[-1], "dp", 1))
    blocks = [CORES * ring_chip(place - way * k) + core for k in range(RING_CHIPS)]
    blocks += [CORES * ring_chip(place + way * k) + 1 - core for k in range(RING_CHIPS)]
    return own + other, jnp.stack(blocks).astype(jnp.int32), own


def chunk_grad(chips, step, chain, came, rider, dtype):
    width = sum(b - a for _, a, b in chain)
    rows = chain[0][0][0].shape[1] // RING_CHIPS
    flat = [value for side, _, _ in chain for value in side]
    flat += [value for value in (came, rider) if value is not None]
    full = width
    if rider is not None:
        full = width + rider.shape[1]
    elif came is not None and dtype == jnp.bfloat16:
        full = came.shape[1]

    def kernel(chips_ref, *refs):
        out_ref = refs[-1]
        start = pl.multiple_of(chips_ref[step - 1] * rows, rows)
        mine = pl.ds(start, rows)
        at, last = 0, 4 * len(chain)
        for i, (_, a, b) in enumerate(chain):
            x, y, other_x, other_y = refs[4 * i : 4 * i + 4]
            part = cross(x[:, mine], y[:, a:b]) + cross(other_x[:, mine], other_y[:, a:b])
            if came is not None:
                part = part + refs[last][:, at : at + b - a].astype(jnp.float32)
            out_ref[:, at : at + b - a] = part.astype(out_ref.dtype)
            at += b - a
        if rider is not None:
            out_ref[:, width:] = refs[last][...]
        elif full > width:
            out_ref[:, width:] = refs[last][:, width:]

    return local_call(kernel, [((rows, full), dtype)], "chunk_grad", 1)(chips, *flat)[0]


def ring_reduce(chains, place, core, rider):
    way = 1 - 2 * core
    chips = jnp.stack([ring_chip(place - way * k) for k in range(1, RING_CHIPS + 1)])
    chips = chips.astype(jnp.int32)
    sums = [None] * len(chains)
    riders = [rider]
    for step in range(1, RING_CHIPS):
        for i, chain in enumerate(chains):
            riding = rider if step == 1 and i == 1 else None
            part = chunk_grad(chips, step, chain, sums[i], riding, jnp.bfloat16)
            sums[i] = ring_step(part)
        riders.append(sums[1][:, -LANES:])
        if step == 1:
            first = sums[0]
    for i, chain in enumerate(chains):
        sums[i] = chunk_grad(chips, RING_CHIPS, chain, sums[i], None, jnp.float32)
    stack = jnp.stack(riders)
    total = 0.0
    for p in range(RING_CHIPS):
        taken = lax.dynamic_index_in_dim(
            stack, (way * (place - p)) % RING_CHIPS, axis=0, keepdims=False
        )
        total = total + taken.astype(jnp.float32)
    return jnp.concatenate(sums, axis=1), total, first


def both_cores(model_side, keep, give):
    return model_side, keep, swap(model_side, "dp", 1), swap(give, "dp", 1)


def own_rows(summed, core, extra=None):
    rows = summed.shape[0] // CORES
    upper, lower = summed[:rows], summed[rows:]
    mine = jnp.where(core == 0, upper, lower)
    give = jnp.where(core == 0, lower, upper).astype(jnp.bfloat16)
    if extra is None:
        taken = swap(give, "dp", 1).astype(jnp.float32)
        return jnp.where(core == 0, mine, taken), jnp.where(core == 0, taken, mine)
    width = give.shape[1]
    extra = extra.astype(jnp.bfloat16)
    taken = swap(jnp.concatenate([give, extra], axis=1), "dp", 1)
    extra = extra.astype(jnp.float32) + taken[:, width:].astype(jnp.float32)
    taken = taken[:, :width].astype(jnp.float32)
    return jnp.where(core == 0, mine, taken), jnp.where(core == 0, taken, mine), extra


def join_halves(halves, a, b):
    return jnp.concatenate([halves[0][:, a:b], halves[1][:, a:b]], axis=1)


def sum_all(values, axis):
    distance = 1
    while distance < lax.axis_size(axis):
        values = values + swap(values, axis, distance)
        distance *= 2
    return values


def per_device(
    residual,
    out_grad,
    doc_lengths,
    mixer_weight,
    mixer_first,
    mixer_second,
    scan_weight,
    scan_first,
    scan_second,
    merge_weight,
    merge_first,
    merge_second,
    hidden_weight,
    hidden_first,
    hidden_second,
    down_weight,
    down_first,
    down_second,
    head_params,
    head_first,
    head_second,
    shared_params,
    shared_first,
    shared_second,
):
    low = jnp.bfloat16
    tidx = lax.axis_index("tensor")
    count = lax.axis_size("dp")
    chips = count // CORES
    core = lax.axis_index("dp") % CORES
    place = ring_place(lax.axis_index("dp") // CORES)
    group = residual.shape[0] * lax.axis_size("tensor")
    conv_shared = shared_params[2 * D :].reshape(CONV + 1, 2 * STATE)

    ring = chips == RING_CHIPS
    mix_cols = mixer_weight.shape[1]
    both_cols = mix_cols + scan_weight.shape[1]
    spare = jnp.zeros((mixer_weight.shape[0], -both_cols % 256), low)
    first_cols = both_cols + spare.shape[1]
    units = down_weight.shape[0]
    first_shard = jnp.concatenate(
        [mixer_weight.astype(low), scan_weight.astype(low), spare, merge_weight.astype(low).T],
        axis=1,
    )
    rest_shard = jnp.concatenate(
        [hidden_weight.astype(low), down_weight.astype(low).T], axis=1
    )
    where = jnp.stack([tidx, core]).astype(jnp.int32)
    consts = mixer_consts(head_params, conv_shared, doc_lengths[0], where, group)
    gain_one, gain_two = shared_params[:D], shared_params[D : 2 * D]
    resid_all = gather_rows(residual, tidx)
    first_all = scaled_norm(resid_all, gain_one).astype(low)
    out_all = gather_rows(out_grad, tidx)
    grad_feed = out_all.astype(low)
    if ring:
        pieces, blocks, own = ring_gather(first_shard, place, core)
        first_w, projected = place_rows(pieces, blocks, first_all, first_cols)
        rest_shard = lax.optimization_barrier((rest_shard, own[4]))[0]
    else:
        first_w = lax.all_gather(first_shard, "dp", axis=0, tiled=True)
        projected = dot(first_all, first_w[:, :first_cols]).astype(low)
    rest_w = lax.all_gather(rest_shard, "dp", axis=0, tiled=True)
    merge_w = first_w[:, first_cols:]
    joined_low, outputs, mix, mix_low, joined_keep, joined_give = mixer_forward(
        projected, consts, first_w
    )
    middle, second_all = middle_forward(resid_all, mix, swap(mix_low, "tensor", 1), gain_two)
    activ_low, grad_gu, dx, dx_low, gu_keep, gu_give, act_keep, act_give = feed_forward_back(
        where, second_all, grad_feed, rest_w, units
    )
    taken = swap(dx_low, "tensor", 1)
    waits = []
    if ring:
        rest_grad = weight_grads(
            [
                both_cores(second_all, gu_keep, gu_give),
                both_cores(grad_feed, act_keep, act_give),
            ],
            low,
        )
        rest_sum = lax.psum_scatter(
            rest_grad,
            "dp",
            scatter_dimension=0,
            axis_index_groups=[[i * CORES + c for i in range(chips)] for c in range(CORES)],
            tiled=True,
        )
        waits = [rest_grad]
    grad_middle, grad_mixed, gain_two_grad = middle_back(
        where, dx, taken, middle, gain_two, out_all, *waits
    )
    waits = []
    if ring:
        other_first, other_joined = swap(first_all, "dp", 1), swap(joined_give, "dp", 1)
        waits = [other_first, other_joined]
    grad_proj, head_grad, conv_grad, proj_keep, proj_give = mixer_backward(
        projected, consts, outputs, grad_mixed, first_w, *waits
    )
    mine_first, theirs_first, gain_one_grad = first_back(where, grad_proj, first_w, resid_all)
    gain_one_grad, gain_two_grad = gain_one_grad.reshape(-1), gain_two_grad.reshape(-1)
    waits = []
    shared_part = jnp.concatenate([gain_one_grad, gain_two_grad, conv_grad.reshape(-1)])
    small = jnp.concatenate([shared_part, head_grad.reshape(-1)])
    if ring:
        rest_halves = own_rows(rest_sum.astype(jnp.float32), core)
        hidden_sum = join_halves(rest_halves, 0, units)
        down_sum = join_halves(rest_halves, units, rest_sum.shape[1]).T
        hidden_new = adamw(hidden_weight, hidden_first, hidden_second, hidden_sum, 0.02, 0.1)
        down_new = adamw(down_weight, down_first, down_second, down_sum, 0.02, 0.1)
        first_sides = (first_all, proj_keep, other_first, swap(proj_give, "dp", 1))
        merge_sides = (grad_mixed, joined_keep, swap(grad_mixed, "dp", 1), other_joined)
        a, b = first_cols // CORES, joined_keep.shape[1]
        cut = (a + b) // 2 // 128 * 128
        chains = [[(first_sides, 0, cut)], [(first_sides, cut, a), (merge_sides, 0, b)]]
        rows = D // RING_CHIPS
        rider = jnp.pad(small.astype(low), (0, rows * LANES - small.shape[0]))
        first_sum, small_sum, mark = ring_reduce(
            chains, place, core, rider.reshape(rows, LANES)
        )
        waits = [mark]
        half = rows // CORES
        small_sum = jnp.concatenate([small_sum[:half], small_sum[half:]], axis=1)
        first_halves = own_rows(first_sum, core, small_sum)
        merge_sum = join_halves(first_halves, a, first_sum.shape[1]).T
        first_sum = join_halves(first_halves, 0, a)
    else:
        whole = jnp.concatenate(
            [
                cross(first_all, grad_proj),
                cross(second_all, grad_gu),
                cross(grad_feed, activ_low),
                cross(grad_mixed, joined_low),
            ],
            axis=1,
        ).astype(low)
        whole = lax.psum_scatter(whole, "dp", scatter_dimension=0, tiled=True)
        whole = whole.astype(jnp.float32)
        a = grad_proj.shape[1]
        first_sum = whole[:, :a]
        hidden_sum = whole[:, a : a + 2 * units]
        a = a + 2 * units
        down_sum = whole[:, a : a + units].T
        merge_sum = whole[:, a + units :].T
        hidden_new = adamw(hidden_weight, hidden_first, hidden_second, hidden_sum, 0.02, 0.1)
        down_new = adamw(down_weight, down_first, down_second, down_sum, 0.02, 0.1)
    mixer_sum, scan_sum = first_sum[:, :mix_cols], first_sum[:, mix_cols:both_cols]
    split = shared_part.shape[0]
    if ring:
        both = jnp.concatenate([scan_sum, first_halves[2]], axis=1)
        taken = swap(both, "tensor", 1)
        scan_sum = scan_sum + taken[:, : scan_sum.shape[1]]
        own_sum = jnp.concatenate([first_halves[2][:, :LANES], first_halves[2][:, LANES:]], axis=0)
        taken = taken[:, scan_sum.shape[1] :]
        taken = jnp.concatenate([taken[:, :LANES], taken[:, LANES:]], axis=0)
        shared_sum = (own_sum + taken).reshape(-1)[:split]
        head_sum = own_sum.reshape(-1)[split : small.shape[0]].reshape(head_grad.shape)
    else:
        scan_sum = scan_sum + swap(scan_sum, "tensor", 1)
        small = sum_all(small, "dp")
        shared_sum = sum_all(small[:split], "tensor")
        head_sum = small[split:].reshape(head_grad.shape)
    grad_first = mine_first + swap(theirs_first, "tensor", 1).astype(jnp.float32)
    input_grad = grad_middle + norm_back(residual, gain_one, grad_first)
    mine, theirs = feed_out(where, activ_low, rest_w, *waits)
    rows = middle.shape[0] // 2
    middle = jnp.where(tidx == 0, middle[:rows], middle[rows:])
    block_out = middle + mine + swap(theirs, "tensor", 1).astype(jnp.float32)

    mixer_new = adamw(mixer_weight, mixer_first, mixer_second, mixer_sum, 0.02, 0.1)
    scan_new = adamw(scan_weight, scan_first, scan_second, scan_sum, 0.02, 0.1)
    merge_new = adamw(merge_weight, merge_first, merge_second, merge_sum, 0.02, 0.1)
    head_new = adamw(head_params, head_first, head_second, head_sum, 0.2, 0.0)
    shared_new = adamw(shared_params, shared_first, shared_second, shared_sum, 0.2, 0.0)
    return (
        block_out,
        input_grad,
        *mixer_new,
        *scan_new,
        *merge_new,
        *hidden_new,
        *down_new,
        *head_new,
        *shared_new,
    )


def solution(mesh):
    return jax.shard_map(
        per_device,
        mesh=mesh,
        in_specs=(
            P(("dp", "tensor"), None),
            P(("dp", "tensor"), None),
            P("dp", None),
            P("dp", "tensor"),
            P("dp", "tensor"),
            P("dp", "tensor"),
            P("dp", None),
            P("dp", None),
            P("dp", None),
            P("tensor", "dp"),
            P("tensor", "dp"),
            P("tensor", "dp"),
            P("dp", "tensor"),
            P("dp", "tensor"),
            P("dp", "tensor"),
            P("tensor", "dp"),
            P("tensor", "dp"),
            P("tensor", "dp"),
            P("tensor", None),
            P("tensor", None),
            P("tensor", None),
            P(),
            P(),
            P(),
        ),
        out_specs=(
            P(("dp", "tensor"), None),
            P(("dp", "tensor"), None),
            P("dp", "tensor"),
            P("dp", "tensor"),
            P("dp", "tensor"),
            P("dp", None),
            P("dp", None),
            P("dp", None),
            P("tensor", "dp"),
            P("tensor", "dp"),
            P("tensor", "dp"),
            P("dp", "tensor"),
            P("dp", "tensor"),
            P("dp", "tensor"),
            P("tensor", "dp"),
            P("tensor", "dp"),
            P("tensor", "dp"),
            P("tensor", None),
            P("tensor", None),
            P("tensor", None),
            P(),
            P(),
            P(),
        ),
        check_vma=False,
    )
```

```python
import jax
import jax.numpy as jnp
from jax import lax
from jax.experimental import pallas as pl
from jax.experimental.pallas import tpu as pltpu
from jax.sharding import PartitionSpec as P

D = 1024
HEADS_M = 24
HEAD_M = 64
STATE = 128
CONV = 4
HEADS_Q = 8
HEADS_KV = 2
HEAD_A = 64
STEP = 10
CORES = 2


EPS = 1e-05
THETA = 10000.0
HIGH = lax.Precision.HIGHEST


def scaled_norm(values, gain):
    return values * lax.rsqrt(jnp.mean(values * values, axis=-1, keepdims=True) + EPS) * gain


def norm_scale(values):
    return lax.rsqrt(jnp.mean(values * values, axis=-1, keepdims=True) + EPS)


def norm_back(values, gain, grad):
    scale = norm_scale(values)
    scaled = grad * gain
    inner = jnp.mean(values * scaled, axis=-1, keepdims=True)
    return scale * scaled - values * (scale * scale * scale * inner)


def doc_index(lens, count):
    place = jnp.arange(count, dtype=jnp.int32)
    ends = jnp.cumsum(lens)
    after = place[:, None] >= ends[None, :]
    seg = jnp.sum(after.astype(jnp.int32), axis=1)
    start = jnp.sum(jnp.where(after, lens[None, :], 0), axis=1)
    return (seg, place - start)


HEADS = HEADS_M // 2
WIDTH = HEADS * HEAD_M
QCOLS = HEADS_Q // 2 * HEAD_A
LANES = 128
RATE_COL = (CONV + 1) * HEAD_M
SKIP_COL = RATE_COL + 1
BIAS_COL = RATE_COL + 2


def exact_dot(left, right, dims=((1,), (0,))):
    return lax.dot_general(
        left, right, (dims, ((), ())), precision=HIGH, preferred_element_type=jnp.float32
    )


def low_dot(left, right, dims=((1,), (0,))):
    return lax.dot_general(
        left.astype(jnp.bfloat16),
        right.astype(jnp.bfloat16),
        (dims, ((), ())),
        preferred_element_type=jnp.float32,
    )


ROWS = ((0,), (0,))
COLS = ((1,), (1,))


def lane_of(shape):
    return lax.broadcasted_iota(jnp.int32, shape, 1)


def shifted(values, pos, shift):
    return jnp.where(pos >= shift, pltpu.roll(values, shift, 0), 0.0)


def conv_forward(values, rows, pos):
    total = rows[CONV : CONV + 1] + rows[CONV - 1 : CONV] * values
    for shift in range(1, CONV):
        tap = rows[CONV - 1 - shift : CONV - shift]
        total = total + tap * shifted(values, pos, shift)
    return total


def conv_backward(grad, values, rows, pos):
    length = values.shape[0]
    back = rows[CONV - 1 : CONV] * grad
    taps = [jnp.sum(grad * values, axis=0, keepdims=True)]
    for shift in range(1, CONV):
        tap = rows[CONV - 1 - shift : CONV - shift]
        kept = jnp.where(pos >= shift, grad, 0.0)
        back = back + tap * pltpu.roll(kept, length - shift, 0)
        taps.append(jnp.sum(kept * pltpu.roll(values, shift, 0), axis=0, keepdims=True))
    return back, taps[::-1] + [jnp.sum(grad, axis=0, keepdims=True)]


def swap_pairs(values):
    first = lane_of(values.shape) % HEAD_A < HEAD_A // 2
    half = HEAD_A // 2
    return jnp.where(first, pltpu.roll(values, LANES - half, 1), pltpu.roll(values, half, 1))


def turn(values, cosine, sine):
    return values * cosine + swap_pairs(values) * sine


def turn_back(values, cosine, sine):
    return values * cosine + swap_pairs(values * sine)


def half_lanes(values, which):
    mine = lane_of(values.shape) // HEAD_A == which
    return jnp.where(mine, values, jnp.zeros_like(values))


def column_to_lanes(column):
    shape = (column.shape[0], LANES)
    row = lax.broadcasted_iota(jnp.int32, shape, 0)
    mine = (row == lane_of(shape)) & (row < HEADS)
    return jnp.sum(jnp.where(mine, column, 0.0), axis=0, keepdims=True)


def conv_rows(heads_ref):
    tiles = [heads_ref[:, j * LANES : (j + 1) * LANES] for j in range(3)]
    rolled = [pltpu.roll(tile, HEAD_M, 1) for tile in tiles]
    left = lane_of((1, LANES)) < HEAD_M
    rows = []
    for k in range(CONV + 1):
        kinds = (tiles[k // 2], rolled[k // 2])
        even, odd = kinds[k % 2], kinds[1 - k % 2]
        pieces = [
            jnp.where(left, even[h : h + 1], odd[h + 1 : h + 2]) for h in range(0, HEADS, 2)
        ]
        rows.append(jnp.concatenate(pieces, axis=1))
    skip = heads_ref[:, SKIP_COL : SKIP_COL + 1]
    pieces = [jnp.where(left, skip[h : h + 1], skip[h + 1 : h + 2]) for h in range(0, HEADS, 2)]
    rows.append(jnp.concatenate(pieces, axis=1))
    return jnp.concatenate(rows + [jnp.zeros((2, WIDTH), jnp.float32)], axis=0)


def head_rows(rows, dlog, dbias):
    left = lane_of((1, LANES)) < HEAD_M
    lane = lane_of((1, LANES))
    out = []
    for i in range(HEADS // 2):
        tile = rows[:, i * LANES : (i + 1) * LANES]
        kinds = (tile, pltpu.roll(tile, HEAD_M, 1))
        for which in range(2):
            h = 2 * i + which
            piece = [kinds[(which + k) % 2][k : k + 1] for k in range(CONV + 1)]
            dskip = jnp.sum(
                half_lanes(tile[CONV + 1 : CONV + 2], which), axis=1, keepdims=True
            )
            last = jnp.where(lane == HEAD_M, dlog[:, h : h + 1], 0.0)
            last = jnp.where(lane == HEAD_M + 1, dskip, last)
            last = jnp.where(lane == HEAD_M + 2, dbias[:, h : h + 1], last)
            tiles = [
                jnp.where(left, piece[0], piece[1]),
                jnp.where(left, piece[2], piece[3]),
                jnp.where(left, piece[4], last),
            ]
            out.append(jnp.concatenate(tiles, axis=1))
    out.append(jnp.zeros((16 - HEADS, 3 * LANES), jnp.float32))
    return jnp.concatenate(out, axis=0)


def documents(lens_ref, place):
    seg, start, end = jnp.zeros_like(place), jnp.zeros_like(place), 0
    for k in range(lens_ref.shape[0]):
        end = end + lens_ref[k]
        after = place >= end
        seg = seg + jnp.where(after, 1, 0)
        start = start + jnp.where(after, lens_ref[k], 0)
    return seg, place - start


def split_rows(values, tidx, mine_ref, theirs_ref):
    half = values.shape[0] // 2
    upper, lower = values[:half], values[half:]
    mine_ref[...] = jnp.where(tidx == 0, upper, lower)
    theirs_ref[...] = jnp.where(tidx == 0, lower, upper).astype(theirs_ref.dtype)


def split_columns(left, right, core, keep_ref, give_ref):
    keep_ref[...] = jnp.where(core == 0, left, right)
    give_ref[...] = jnp.where(core == 0, right, left)


def mixer_parts(tidx_ref, lens_ref, p_ref, heads_ref, bc_ref):
    length = p_ref.shape[0]
    base = 2 * WIDTH + QCOLS + 2 * HEAD_A
    conv = conv_rows(heads_ref)
    bc = bc_ref[...]
    row = lax.broadcasted_iota(jnp.int32, (length, length), 0)
    column = lax.broadcasted_iota(jnp.int32, (length, length), 1)
    seg, pos = documents(lens_ref, lax.broadcasted_iota(jnp.int32, (length, 1), 0))
    seg_across, _ = documents(lens_ref, lax.broadcasted_iota(jnp.int32, (1, length), 1))
    same = (seg == seg_across) & (row >= column)
    wide = p_ref[:, WIDTH : 2 * WIDTH].astype(jnp.float32)
    chans_pre = conv_forward(wide, conv, pos)
    chans_sig = jax.nn.sigmoid(chans_pre)
    states = p_ref[:, base : base + 2 * STATE].astype(jnp.float32)
    states_pre = conv_forward(states, bc, pos)
    states_sig = jax.nn.sigmoid(states_pre)
    raw = p_ref[:, base + 2 * STATE : base + 2 * STATE + LANES].astype(jnp.float32)
    i = lax.broadcasted_iota(jnp.int32, (LANES, LANES), 0)
    j = lane_of((LANES, LANES))
    sel = ((i == HEADS * tidx_ref[0] + j) & (j < HEADS)).astype(jnp.float32)
    i = lax.broadcasted_iota(jnp.int32, (LANES, WIDTH), 0)
    spread = (i == lane_of((LANES, WIDTH)) // HEAD_M).astype(jnp.float32)
    rates = column_to_lanes(jnp.exp(heads_ref[:, RATE_COL : RATE_COL + 1]))
    bias = column_to_lanes(heads_ref[:, BIAS_COL : BIAS_COL + 1])
    step_pre = exact_dot(raw, sel) + bias
    steps = jnp.maximum(step_pre, 0.0) + jnp.log1p(jnp.exp(-jnp.abs(step_pre)))
    before = (row >= column).astype(jnp.float32)
    cum = exact_dot(before, -rates * steps)
    steps_wide = exact_dot(steps, spread)
    chans = chans_pre * chans_sig
    states_out = states_pre * states_sig
    in_state, out_state = states_out[:, :STATE], states_out[:, STATE:]
    inner = jnp.where(same, exact_dot(out_state, in_state, COLS), 0.0)
    return dict(
        pos=pos, wide=wide, chans_pre=chans_pre, chans_sig=chans_sig, chans=chans,
        states=states, states_pre=states_pre, states_sig=states_sig, in_state=in_state,
        out_state=out_state, step_pre=step_pre, steps=steps, rates=rates, before=before,
        cum=cum, cum_t=cum.T, same=same, steps_wide=steps_wide, inner=inner, conv=conv, bc=bc,
        sel=sel, spread=spread, weighted=(steps_wide * chans).astype(jnp.bfloat16),
    )


def decay_of(parts, head):
    gap = parts["cum"][:, head : head + 1] - parts["cum_t"][head : head + 1, :]
    return jnp.exp(jnp.minimum(gap, 0.0))


def attention_parts(p_ref, cos_ref, sin_ref):
    cosine, sine = cos_ref[...], sin_ref[...]
    pairs = []
    for i in range(QCOLS // LANES):
        a = 2 * WIDTH + i * LANES
        query = turn(p_ref[:, a : a + LANES].astype(jnp.float32), cosine, sine)
        pairs.append((query * HEAD_A ** (-0.5)).astype(jnp.bfloat16))
    a = 2 * WIDTH + QCOLS
    both = p_ref[:, a : a + LANES].astype(jnp.float32)
    key = half_lanes(turn(both, cosine, sine), 0)
    value = half_lanes(both, 1)
    keys = (key.astype(jnp.bfloat16), pltpu.roll(key, HEAD_A, 1).astype(jnp.bfloat16))
    values = (pltpu.roll(value, HEAD_A, 1).astype(jnp.bfloat16), value.astype(jnp.bfloat16))
    return pairs, keys, values


def attention_probs(query, key, same):
    scores = jnp.where(same, low_dot(query, key, COLS), -1e30)
    top = jnp.max(scores, axis=1, keepdims=True)
    raised = jnp.exp(scores - top)
    return raised / jnp.sum(raised, axis=1, keepdims=True)


def forward_kernel(
    tidx_ref, lens_ref, p_ref, heads_ref, bc_ref, cos_ref, sin_ref, w_ref,
    cat_ref, y_ref, mix_ref, mix_low_ref, keep_ref, give_ref,
):
    parts = mixer_parts(tidx_ref, lens_ref, p_ref, heads_ref, bc_ref)
    for i in range(WIDTH // LANES):
        a = i * LANES
        tile = parts["weighted"][:, a : a + LANES]
        out = jnp.zeros((p_ref.shape[0], LANES), jnp.float32)
        for which in range(2):
            mixed = decay_of(parts, 2 * i + which) * parts["inner"]
            out = out + low_dot(mixed, half_lanes(tile, which))
        y_ref[:, a : a + LANES] = out
        gate = p_ref[:, a : a + LANES].astype(jnp.float32)
        out = out + parts["conv"][CONV + 1 : CONV + 2, a : a + LANES] * parts["chans"][:, a : a + LANES]
        cat_ref[:, a : a + LANES] = (out * gate * jax.nn.sigmoid(gate)).astype(cat_ref.dtype)
    pairs, keys, values = attention_parts(p_ref, cos_ref, sin_ref)
    for i, query in enumerate(pairs):
        out = jnp.zeros((p_ref.shape[0], LANES), jnp.float32)
        for which in range(2):
            probs = attention_probs(query, keys[which], parts["same"])
            out = out + low_dot(probs, values[which])
        a = WIDTH + i * LANES
        cat_ref[:, a : a + LANES] = out.astype(cat_ref.dtype)
    cat = cat_ref[...]
    mix_ref[...] = dot_t(cat, w_ref[:, p_ref.shape[1] :])
    mix_low_ref[...] = mix_ref[...].astype(mix_low_ref.dtype)
    half = cat.shape[1] // 2
    split_columns(cat[:, :half], cat[:, half:], tidx_ref[1], keep_ref, give_ref)


def backward_kernel(
    tidx_ref, lens_ref, p_ref, heads_ref, bc_ref, cos_ref, sin_ref, y_ref, dmix_ref, w_ref,
    dp_ref, dheads_ref, dbc_ref, keep_ref, give_ref,
):
    length = p_ref.shape[0]
    low = dp_ref.dtype
    parts = mixer_parts(tidx_ref, lens_ref, p_ref, heads_ref, bc_ref)
    pos, chans = parts["pos"], parts["chans"]
    gate = p_ref[:, :WIDTH].astype(jnp.float32)
    gate_sig = jax.nn.sigmoid(gate)
    grad_all = dot(dmix_ref[...], w_ref[:, p_ref.shape[1] :])
    grad = grad_all[:, :WIDTH]
    skip = parts["conv"][CONV + 1 : CONV + 2]
    outputs = y_ref[...]
    dgate = grad * (outputs + skip * chans) * gate_sig * (1.0 + gate * (1.0 - gate_sig))
    dp_ref[:, :WIDTH] = dgate.astype(low)
    dy = grad * gate * gate_sig
    dy_low = dy.astype(jnp.bfloat16)
    dweighted = []
    dinner = jnp.zeros((length, length), jnp.float32)
    for i in range(WIDTH // LANES):
        a = i * LANES
        tile = parts["weighted"][:, a : a + LANES]
        out = jnp.zeros((length, LANES), jnp.float32)
        for which in range(2):
            decay = decay_of(parts, 2 * i + which)
            dy_half = half_lanes(dy_low[:, a : a + LANES], which)
            out = out + low_dot(decay * parts["inner"], dy_half, ROWS)
            dinner = dinner + low_dot(dy_half, tile, COLS) * decay
        dweighted.append(out)
    dweighted = jnp.concatenate(dweighted, axis=1)
    spread = parts["spread"]
    weighted = parts["weighted"].astype(jnp.float32)
    dcum = exact_dot(dy_low.astype(jnp.float32) * outputs - weighted * dweighted, spread, COLS)
    dsteps = exact_dot(dweighted * chans, spread, COLS)
    dchans = skip * dy + parts["steps_wide"] * dweighted
    drate = exact_dot(parts["before"], dcum, ROWS)
    dsteps = (dsteps - parts["rates"] * drate) * jax.nn.sigmoid(parts["step_pre"])
    dlog = jnp.sum(-parts["rates"] * parts["steps"] * drate, axis=0, keepdims=True)
    dbias = jnp.sum(dsteps, axis=0, keepdims=True)
    base = 2 * WIDTH + QCOLS + 2 * HEAD_A
    draw = exact_dot(dsteps, parts["sel"], COLS)
    dp_ref[:, base + 2 * STATE :] = draw.astype(low)

    sig, pre = parts["chans_sig"], parts["chans_pre"]
    dpre = dchans * sig * (1.0 + pre * (1.0 - sig))
    back, rows = conv_backward(dpre, parts["wide"], parts["conv"], pos)
    dp_ref[:, WIDTH : 2 * WIDTH] = back.astype(low)
    rows.append(jnp.sum(dy * chans, axis=0, keepdims=True))
    rows = jnp.concatenate(rows + [jnp.zeros((2, WIDTH), jnp.float32)], axis=0)
    dheads_ref[...] = head_rows(rows, dlog, dbias)

    dinner = jnp.where(parts["same"], dinner, 0.0)
    dstates = jnp.concatenate(
        [exact_dot(dinner, parts["out_state"], ROWS), exact_dot(dinner, parts["in_state"])],
        axis=1,
    )
    sig, pre = parts["states_sig"], parts["states_pre"]
    dpre = dstates * sig * (1.0 + pre * (1.0 - sig))
    back, rows = conv_backward(dpre, parts["states"], parts["bc"], pos)
    dp_ref[:, base : base + 2 * STATE] = back.astype(low)
    dbc_ref[...] = jnp.concatenate(rows, axis=0)

    pairs, keys, values = attention_parts(p_ref, cos_ref, sin_ref)
    cosine, sine = cos_ref[...], sin_ref[...]
    dkeys = [jnp.zeros((length, LANES), jnp.float32) for _ in range(2)]
    dvalues = [jnp.zeros((length, LANES), jnp.float32) for _ in range(2)]
    for i, query in enumerate(pairs):
        a = WIDTH + i * LANES
        datt = grad_all[:, a : a + LANES].astype(jnp.bfloat16)
        dquery = jnp.zeros((length, LANES), jnp.float32)
        for which in range(2):
            probs = attention_probs(query, keys[which], parts["same"])
            dprobs = low_dot(datt, values[which], COLS)
            dscores = probs * (dprobs - jnp.sum(probs * dprobs, axis=1, keepdims=True))
            dscores = dscores.astype(jnp.bfloat16)
            dquery = dquery + low_dot(dscores, keys[which])
            dkeys[which] = dkeys[which] + low_dot(dscores, query, ROWS)
            dvalues[which] = dvalues[which] + low_dot(probs, datt, ROWS)
        a = 2 * WIDTH + i * LANES
        dquery = turn_back(dquery * HEAD_A ** (-0.5), cosine, sine)
        dp_ref[:, a : a + LANES] = dquery.astype(low)
    dkey = half_lanes(dkeys[0], 0) + pltpu.roll(half_lanes(dkeys[1], 1), HEAD_A, 1)
    dvalue = pltpu.roll(half_lanes(dvalues[0], 0), HEAD_A, 1) + half_lanes(dvalues[1], 1)
    a = 2 * WIDTH + QCOLS
    dboth = half_lanes(turn_back(dkey, cosine, sine), 0) + dvalue
    dp_ref[:, a : a + LANES] = dboth.astype(low)
    half = dp_ref.shape[1] // 2
    split_columns(dp_ref[:, :half], dp_ref[:, half:], tidx_ref[1], keep_ref, give_ref)


def local_call(kernel, outs, name, scalars=0, after=0):
    space = pl.BlockSpec(memory_space=pltpu.VMEM)
    scalar = pl.BlockSpec(memory_space=pltpu.SMEM)
    return lambda *args: pl.pallas_call(
        kernel,
        out_shape=[jax.ShapeDtypeStruct(shape, dtype) for shape, dtype in outs],
        in_specs=[scalar] * scalars
        + [space] * (len(args) - scalars - after)
        + [pl.BlockSpec(memory_space=pl.ANY)] * after,
        out_specs=[space] * len(outs),
        compiler_params=pltpu.CompilerParams(vmem_limit_bytes=56 * 2**20),
        name=name,
    )(*args)


def mixer_consts(head_params, conv_shared, lens, where, length):
    _, pos = doc_index(lens, length)
    half = HEAD_A // 2
    freq = THETA ** (-jnp.arange(half, dtype=jnp.float32) * 2.0 / HEAD_A)
    angle = pos.astype(jnp.float32)[:, None] * freq[None, :]
    cosine, sine = jnp.cos(angle), jnp.sin(angle)
    heads = jnp.pad(
        head_params, ((0, 16 - HEADS), (0, 3 * LANES - head_params.shape[1]))
    )
    scalars = (where, lens)
    return scalars, (
        heads,
        conv_shared,
        jnp.concatenate([cosine] * 4, axis=1),
        jnp.concatenate([-sine, sine, -sine, sine], axis=1),
    )


def mixer_forward(projected, consts, weight):
    length = projected.shape[0]
    width = WIDTH + QCOLS
    outs = [
        ((length, width), jnp.bfloat16),
        ((length, WIDTH), jnp.float32),
        ((length, weight.shape[0]), jnp.float32),
        ((length, weight.shape[0]), jnp.bfloat16),
        ((length, width // 2), jnp.bfloat16),
        ((length, width // 2), jnp.bfloat16),
    ]
    scalars, arrays = consts
    return local_call(forward_kernel, outs, "mixer_forward", 2)(
        *scalars, projected, *arrays, weight
    )


def mixer_backward(projected, consts, outputs, grad, weight, *after):
    length, width = projected.shape
    outs = [
        ((length, width), jnp.bfloat16),
        ((16, 3 * LANES), jnp.float32),
        ((CONV + 1, 2 * STATE), jnp.float32),
        ((length, width // 2), jnp.bfloat16),
        ((length, width // 2), jnp.bfloat16),
    ]
    scalars, arrays = consts
    kernel = lambda *refs: backward_kernel(*refs[:10], *refs[10 + len(after) :])
    grad_proj, heads, bc, keep, give = local_call(
        kernel, outs, "mixer_backward", 2, len(after)
    )(*scalars, projected, *arrays, outputs, grad, weight, *after)
    return grad_proj, heads[:HEADS, : BIAS_COL + 1], bc, keep, give


def feed_kernel(
    where_ref, x_ref, grad_ref, w_ref,
    act_ref, dgu_ref, dx_ref, dx_low_ref, keep_ref, give_ref, act_keep_ref, act_give_ref,
):
    units = act_ref.shape[1]
    core = where_ref[1]
    gate_up = dot(x_ref[...], w_ref[:, : 2 * units])
    gate, upper = gate_up[:, :units], gate_up[:, units:]
    sig = jax.nn.sigmoid(gate)
    raised = gate * sig
    act = (raised * upper).astype(act_ref.dtype)
    act_ref[...] = act
    split_columns(act[:, : units // 2], act[:, units // 2 :], core, act_keep_ref, act_give_ref)
    grad = dot(grad_ref[...], w_ref[:, 2 * units : 3 * units])
    dgate = (grad * upper * sig * (1.0 + gate * (1.0 - sig))).astype(dgu_ref.dtype)
    dupper = (grad * raised).astype(dgu_ref.dtype)
    dgu_ref[:, :units] = dgate
    dgu_ref[:, units:] = dupper
    split_columns(dgate, dupper, core, keep_ref, give_ref)
    dx_ref[...] = dot_t(dgu_ref[...], w_ref[:, : 2 * units])
    dx_low_ref[...] = dx_ref[...].astype(dx_low_ref.dtype)


def feed_forward_back(where, values, grad, weight, units):
    length, width = values.shape
    low = jnp.bfloat16
    outs = [
        ((length, units), low),
        ((length, 2 * units), low),
        ((length, width), jnp.float32),
        ((length, width), low),
        ((length, units), low),
        ((length, units), low),
        ((length, units // 2), low),
        ((length, units // 2), low),
    ]
    return local_call(feed_kernel, outs, "feed_forward_back", 1)(where, values, grad, weight)


def middle_forward(resid, mix, taken, gain):
    def kernel(resid_ref, mix_ref, taken_ref, gain_ref, middle_ref, normed_ref):
        middle = resid_ref[...] + mix_ref[...] + taken_ref[...].astype(jnp.float32)
        middle_ref[...] = middle
        normed_ref[...] = scaled_norm(middle, gain_ref[...]).astype(normed_ref.dtype)

    outs = [(resid.shape, jnp.float32), (resid.shape, jnp.bfloat16)]
    return local_call(kernel, outs, "middle_forward")(resid, mix, taken, gain[None, :])


def middle_back(where, partial, taken, middle, gain, out_grad, *after):
    low = jnp.bfloat16
    rows, width = middle.shape

    def kernel(where_ref, part_ref, taken_ref, middle_ref, gain_ref, out_ref, *refs):
        grad_ref, low_ref, gain_grad_ref = refs[len(after) :]
        first = where_ref[0] == 0
        grad = part_ref[...] + taken_ref[...].astype(jnp.float32)
        values = middle_ref[...]
        total = out_ref[...] + norm_back(values, gain_ref[...], grad)
        grad_ref[...] = jnp.where(first, total[: rows // 2], total[rows // 2 :])
        low_ref[...] = total.astype(low)
        share = grad * values * norm_scale(values)
        share = jnp.where(first, share[: rows // 2], share[rows // 2 :])
        gain_grad_ref[...] = jnp.sum(share, axis=0, keepdims=True)

    outs = [((rows // 2, width), jnp.float32), ((rows, width), low), ((1, width), jnp.float32)]
    return local_call(kernel, outs, "middle_back", 1, len(after))(
        where, partial, taken, middle, gain[None, :], out_grad, *after
    )


def first_back(where, grad_proj, weight, resid, *after):
    def kernel(where_ref, dp_ref, w_ref, resid_ref, *refs):
        mine_ref, theirs_ref, gain_grad_ref = refs[len(after) :]
        grad = dot_t(dp_ref[...], w_ref[:, : dp_ref.shape[1]])
        values = resid_ref[...]
        gain_grad_ref[...] = jnp.sum(grad * values * norm_scale(values), axis=0, keepdims=True)
        split_rows(grad, where_ref[0], mine_ref, theirs_ref)

    rows, width = resid.shape
    outs = [
        ((rows // 2, width), jnp.float32),
        ((rows // 2, width), jnp.bfloat16),
        ((1, width), jnp.float32),
    ]
    return local_call(kernel, outs, "first_back", 1, len(after))(
        where, grad_proj, weight, resid, *after
    )


def feed_out(where, act, weight, *after):
    def kernel(where_ref, act_ref, w_ref, *refs):
        units = act_ref.shape[1]
        out = dot_t(act_ref[...], w_ref[:, 2 * units :])
        split_rows(out, where_ref[0], *refs[len(after) :])

    rows, width = act.shape[0] // 2, weight.shape[0]
    outs = [((rows, width), jnp.float32), ((rows, width), jnp.bfloat16)]
    return local_call(kernel, outs, "feed_out", 1, len(after))(where, act, weight, *after)


def weight_grads(sides, dtype, *after):
    width = sum(side[1].shape[1] for side in sides)
    model = sides[0][0].shape[1]
    block = 256

    def kernel(*refs):
        out_ref, a = refs[-1], 0
        for i in range(len(sides)):
            x, y, other_x, other_y = refs[4 * i : 4 * i + 4]
            b = a + y.shape[1]
            for r in range(0, model, block):
                part = cross(x[:, r : r + block], y[...])
                part = part + cross(other_x[:, r : r + block], other_y[...])
                out_ref[r : r + block, a:b] = part.astype(out_ref.dtype)
            a = b

    flat = [value for side in sides for value in side]
    return local_call(kernel, [((model, width), dtype)], "weight_grads", 0, len(after))(
        *flat, *after
    )[0]


def cross(left, right):
    return lax.dot_general(
        left, right, (((0,), (0,)), ((), ())), preferred_element_type=jnp.float32
    )


def dot(left, right):
    return jnp.dot(left, right, preferred_element_type=jnp.float32)


def dot_t(left, right):
    return lax.dot_general(
        left, right, (((1,), (1,)), ((), ())), preferred_element_type=jnp.float32
    )


def adamw(weight, first, second, grad, rate, decay):
    first = 0.9 * first + 0.1 * grad
    second = 0.95 * second + 0.05 * grad * grad
    fixed_one = first / (1.0 - 0.9**STEP)
    fixed_two = second / (1.0 - 0.95**STEP)
    weight = weight - rate * (fixed_one / (jnp.sqrt(fixed_two) + 1e-08) + decay * weight)
    return (first, second, weight)


def swap(values, axis, distance):
    count = lax.axis_size(axis)
    return lax.ppermute(values, axis, [(i, i ^ distance) for i in range(count)])


def pair_rows(own, other, tidx):
    return jnp.where(
        tidx == 0,
        jnp.concatenate([own, other], axis=0),
        jnp.concatenate([other, own], axis=0),
    )


def gather_rows(own, tidx):
    return pair_rows(own, swap(own, "tensor", 1), tidx)


RING_CHIPS = 8


def ring_chip(place):
    place = place % RING_CHIPS
    half = RING_CHIPS // 2
    if isinstance(place, int):
        return 2 * place if place < half else 2 * (RING_CHIPS - 1 - place) + 1
    return jnp.where(place < half, 2 * place, 2 * (RING_CHIPS - 1 - place) + 1)


def ring_place(chip):
    return jnp.where(chip % 2 == 0, chip // 2, RING_CHIPS - 1 - chip // 2)


def ring_step(values):
    pairs = []
    for p in range(RING_CHIPS):
        pairs.append((CORES * ring_chip(p), CORES * ring_chip(p + 1)))
        pairs.append((CORES * ring_chip(p + 1) + 1, CORES * ring_chip(p) + 1))
    return lax.ppermute(values, "dp", pairs)


def place_rows(pieces, blocks, values=None, columns=0):
    count = len(pieces)
    height, width = pieces[0].shape
    low = pieces[0].dtype
    extra = [] if values is None else [values]

    def kernel(block_ref, *refs):
        out_ref = refs[count + len(extra)]
        for i in range(count):
            start = pl.multiple_of(block_ref[i] * height, height)
            out_ref[pl.ds(start, height), :] = refs[i][...]
        if extra:
            refs[-1][...] = dot(refs[count][...], out_ref[:, :columns]).astype(low)

    outs = [((count * height, width), low)]
    if extra:
        outs.append(((values.shape[0], columns), low))
    return local_call(kernel, outs, "place_rows", 1)(blocks, *pieces, *extra)


def ring_gather(shard, place, core):
    way = 1 - 2 * core
    own = [shard]
    other = [swap(shard, "dp", 1)]
    for _ in range(1, RING_CHIPS):
        own.append(ring_step(own[-1]))
        other.append(swap(own[-1], "dp", 1))
    blocks = [CORES * ring_chip(place - way * k) + core for k in range(RING_CHIPS)]
    blocks += [CORES * ring_chip(place + way * k) + 1 - core for k in range(RING_CHIPS)]
    return own + other, jnp.stack(blocks).astype(jnp.int32), own


def ring_reduce(chains, place, core, rider):
    way = 1 - 2 * core
    sums = [None] * len(chains)
    riders = [rider]
    for step in range(1, RING_CHIPS + 1):
        chip = ring_chip(place - way * step)
        for i, chain in enumerate(chains):
            parts = []
            for grad, a, b in chain:
                rows = grad.shape[0] // RING_CHIPS
                parts.append(lax.dynamic_slice(grad, (chip * rows, a), (rows, b - a)))
            part = parts[0] if len(parts) == 1 else jnp.concatenate(parts, axis=1)
            if step > 1:
                part = part.astype(jnp.float32) + sums[i].astype(jnp.float32)
            if step < RING_CHIPS:
                part = part.astype(jnp.bfloat16)
                if i == 1:
                    width = part.shape[1]
                    part = ring_step(jnp.concatenate([part, riders[-1]], axis=1))
                    riders.append(part[:, width:])
                    part = part[:, :width]
                else:
                    part = ring_step(part)
            sums[i] = part
        if step == 1:
            first = sums[0]
    stack = jnp.stack(riders)
    total = 0.0
    for p in range(RING_CHIPS):
        taken = lax.dynamic_index_in_dim(
            stack, (way * (place - p)) % RING_CHIPS, axis=0, keepdims=False
        )
        total = total + taken.astype(jnp.float32)
    return jnp.concatenate(sums, axis=1), total, first


def both_cores(model_side, keep, give):
    return model_side, keep, swap(model_side, "dp", 1), swap(give, "dp", 1)


def own_rows(summed, core, extra=None):
    rows = summed.shape[0] // CORES
    upper, lower = summed[:rows], summed[rows:]
    mine = jnp.where(core == 0, upper, lower)
    give = jnp.where(core == 0, lower, upper).astype(jnp.bfloat16)
    if extra is None:
        taken = swap(give, "dp", 1).astype(jnp.float32)
        return jnp.where(core == 0, mine, taken), jnp.where(core == 0, taken, mine)
    width = give.shape[1]
    extra = extra.astype(jnp.bfloat16)
    taken = swap(jnp.concatenate([give, extra], axis=1), "dp", 1)
    extra = extra.astype(jnp.float32) + taken[:, width:].astype(jnp.float32)
    taken = taken[:, :width].astype(jnp.float32)
    return jnp.where(core == 0, mine, taken), jnp.where(core == 0, taken, mine), extra


def join_halves(halves, a, b):
    return jnp.concatenate([halves[0][:, a:b], halves[1][:, a:b]], axis=1)


def sum_all(values, axis):
    distance = 1
    while distance < lax.axis_size(axis):
        values = values + swap(values, axis, distance)
        distance *= 2
    return values


def per_device(
    residual,
    out_grad,
    doc_lengths,
    mixer_weight,
    mixer_first,
    mixer_second,
    scan_weight,
    scan_first,
    scan_second,
    merge_weight,
    merge_first,
    merge_second,
    hidden_weight,
    hidden_first,
    hidden_second,
    down_weight,
    down_first,
    down_second,
    head_params,
    head_first,
    head_second,
    shared_params,
    shared_first,
    shared_second,
):
    low = jnp.bfloat16
    tidx = lax.axis_index("tensor")
    count = lax.axis_size("dp")
    chips = count // CORES
    core = lax.axis_index("dp") % CORES
    place = ring_place(lax.axis_index("dp") // CORES)
    group = residual.shape[0] * lax.axis_size("tensor")
    conv_shared = shared_params[2 * D :].reshape(CONV + 1, 2 * STATE)

    ring = chips == RING_CHIPS
    mix_cols = mixer_weight.shape[1]
    both_cols = mix_cols + scan_weight.shape[1]
    spare = jnp.zeros((mixer_weight.shape[0], -both_cols % 256), low)
    first_cols = both_cols + spare.shape[1]
    units = down_weight.shape[0]
    first_shard = jnp.concatenate(
        [mixer_weight.astype(low), scan_weight.astype(low), spare, merge_weight.astype(low).T],
        axis=1,
    )
    rest_shard = jnp.concatenate(
        [hidden_weight.astype(low), down_weight.astype(low).T], axis=1
    )
    where = jnp.stack([tidx, core]).astype(jnp.int32)
    consts = mixer_consts(head_params, conv_shared, doc_lengths[0], where, group)
    gain_one, gain_two = shared_params[:D], shared_params[D : 2 * D]
    resid_all = gather_rows(residual, tidx)
    first_all = scaled_norm(resid_all, gain_one).astype(low)
    out_all = gather_rows(out_grad, tidx)
    grad_feed = out_all.astype(low)
    if ring:
        pieces, blocks, own = ring_gather(first_shard, place, core)
        first_w, projected = place_rows(pieces, blocks, first_all, first_cols)
        rest_shard = lax.optimization_barrier((rest_shard, own[4]))[0]
    else:
        first_w = lax.all_gather(first_shard, "dp", axis=0, tiled=True)
        projected = dot(first_all, first_w[:, :first_cols]).astype(low)
    rest_w = lax.all_gather(rest_shard, "dp", axis=0, tiled=True)
    merge_w = first_w[:, first_cols:]
    joined_low, outputs, mix, mix_low, joined_keep, joined_give = mixer_forward(
        projected, consts, first_w
    )
    middle, second_all = middle_forward(resid_all, mix, swap(mix_low, "tensor", 1), gain_two)
    activ_low, grad_gu, dx, dx_low, gu_keep, gu_give, act_keep, act_give = feed_forward_back(
        where, second_all, grad_feed, rest_w, units
    )
    taken = swap(dx_low, "tensor", 1)
    waits = []
    if ring:
        rest_grad = weight_grads(
            [
                both_cores(second_all, gu_keep, gu_give),
                both_cores(grad_feed, act_keep, act_give),
            ],
            low,
        )
        rest_sum = lax.psum_scatter(
            rest_grad,
            "dp",
            scatter_dimension=0,
            axis_index_groups=[[i * CORES + c for i in range(chips)] for c in range(CORES)],
            tiled=True,
        )
        waits = [rest_grad]
    grad_middle, grad_mixed, gain_two_grad = middle_back(
        where, dx, taken, middle, gain_two, out_all, *waits
    )
    waits = []
    if ring:
        other_first, other_joined = swap(first_all, "dp", 1), swap(joined_give, "dp", 1)
        waits = [other_first, other_joined]
    grad_proj, head_grad, conv_grad, proj_keep, proj_give = mixer_backward(
        projected, consts, outputs, grad_mixed, first_w, *waits
    )
    mine_first, theirs_first, gain_one_grad = first_back(where, grad_proj, first_w, resid_all)
    gain_one_grad, gain_two_grad = gain_one_grad.reshape(-1), gain_two_grad.reshape(-1)
    waits = []
    shared_part = jnp.concatenate([gain_one_grad, gain_two_grad, conv_grad.reshape(-1)])
    small = jnp.concatenate([shared_part, head_grad.reshape(-1)])
    if ring:
        rest_halves = own_rows(rest_sum.astype(jnp.float32), core)
        hidden_sum = join_halves(rest_halves, 0, units)
        down_sum = join_halves(rest_halves, units, rest_sum.shape[1]).T
        hidden_new = adamw(hidden_weight, hidden_first, hidden_second, hidden_sum, 0.02, 0.1)
        down_new = adamw(down_weight, down_first, down_second, down_sum, 0.02, 0.1)
        first_sides = (first_all, proj_keep, other_first, swap(proj_give, "dp", 1))
        merge_sides = (grad_mixed, joined_keep, swap(grad_mixed, "dp", 1), other_joined)
        a, b = first_cols // CORES, joined_keep.shape[1]
        cut = (a + b) // 2 // 128 * 128
        first_grad = weight_grads([first_sides], low)
        merge_grad = weight_grads([merge_sides], low, first_grad)
        chains = [[(first_grad, 0, cut)], [(first_grad, cut, a), (merge_grad, 0, b)]]
        rows = D // RING_CHIPS
        rider = jnp.pad(small.astype(low), (0, rows * LANES - small.shape[0]))
        first_sum, small_sum, mark = ring_reduce(
            chains, place, core, rider.reshape(rows, LANES)
        )
        waits = [mark]
        half = rows // CORES
        small_sum = jnp.concatenate([small_sum[:half], small_sum[half:]], axis=1)
        first_halves = own_rows(first_sum, core, small_sum)
        merge_sum = join_halves(first_halves, a, first_sum.shape[1]).T
        first_sum = join_halves(first_halves, 0, a)
    else:
        whole = jnp.concatenate(
            [
                cross(first_all, grad_proj),
                cross(second_all, grad_gu),
                cross(grad_feed, activ_low),
                cross(grad_mixed, joined_low),
            ],
            axis=1,
        ).astype(low)
        whole = lax.psum_scatter(whole, "dp", scatter_dimension=0, tiled=True)
        whole = whole.astype(jnp.float32)
        a = grad_proj.shape[1]
        first_sum = whole[:, :a]
        hidden_sum = whole[:, a : a + 2 * units]
        a = a + 2 * units
        down_sum = whole[:, a : a + units].T
        merge_sum = whole[:, a + units :].T
        hidden_new = adamw(hidden_weight, hidden_first, hidden_second, hidden_sum, 0.02, 0.1)
        down_new = adamw(down_weight, down_first, down_second, down_sum, 0.02, 0.1)
    mixer_sum, scan_sum = first_sum[:, :mix_cols], first_sum[:, mix_cols:both_cols]
    split = shared_part.shape[0]
    if ring:
        both = jnp.concatenate([scan_sum, first_halves[2]], axis=1)
        taken = swap(both, "tensor", 1)
        scan_sum = scan_sum + taken[:, : scan_sum.shape[1]]
        own_sum = jnp.concatenate([first_halves[2][:, :LANES], first_halves[2][:, LANES:]], axis=0)
        taken = taken[:, scan_sum.shape[1] :]
        taken = jnp.concatenate([taken[:, :LANES], taken[:, LANES:]], axis=0)
        shared_sum = (own_sum + taken).reshape(-1)[:split]
        head_sum = own_sum.reshape(-1)[split : small.shape[0]].reshape(head_grad.shape)
    else:
        scan_sum = scan_sum + swap(scan_sum, "tensor", 1)
        small = sum_all(small, "dp")
        shared_sum = sum_all(small[:split], "tensor")
        head_sum = small[split:].reshape(head_grad.shape)
    grad_first = mine_first + swap(theirs_first, "tensor", 1).astype(jnp.float32)
    input_grad = grad_middle + norm_back(residual, gain_one, grad_first)
    mine, theirs = feed_out(where, activ_low, rest_w, *waits)
    rows = middle.shape[0] // 2
    middle = jnp.where(tidx == 0, middle[:rows], middle[rows:])
    block_out = middle + mine + swap(theirs, "tensor", 1).astype(jnp.float32)

    mixer_new = adamw(mixer_weight, mixer_first, mixer_second, mixer_sum, 0.02, 0.1)
    scan_new = adamw(scan_weight, scan_first, scan_second, scan_sum, 0.02, 0.1)
    merge_new = adamw(merge_weight, merge_first, merge_second, merge_sum, 0.02, 0.1)
    head_new = adamw(head_params, head_first, head_second, head_sum, 0.2, 0.0)
    shared_new = adamw(shared_params, shared_first, shared_second, shared_sum, 0.2, 0.0)
    return (
        block_out,
        input_grad,
        *mixer_new,
        *scan_new,
        *merge_new,
        *hidden_new,
        *down_new,
        *head_new,
        *shared_new,
    )


def solution(mesh):
    return jax.shard_map(
        per_device,
        mesh=mesh,
        in_specs=(
            P(("dp", "tensor"), None),
            P(("dp", "tensor"), None),
            P("dp", None),
            P("dp", "tensor"),
            P("dp", "tensor"),
            P("dp", "tensor"),
            P("dp", None),
            P("dp", None),
            P("dp", None),
            P("tensor", "dp"),
            P("tensor", "dp"),
            P("tensor", "dp"),
            P("dp", "tensor"),
            P("dp", "tensor"),
            P("dp", "tensor"),
            P("tensor", "dp"),
            P("tensor", "dp"),
            P("tensor", "dp"),
            P("tensor", None),
            P("tensor", None),
            P("tensor", None),
            P(),
            P(),
            P(),
        ),
        out_specs=(
            P(("dp", "tensor"), None),
            P(("dp", "tensor"), None),
            P("dp", "tensor"),
            P("dp", "tensor"),
            P("dp", "tensor"),
            P("dp", None),
            P("dp", None),
            P("dp", None),
            P("tensor", "dp"),
            P("tensor", "dp"),
            P("tensor", "dp"),
            P("dp", "tensor"),
            P("dp", "tensor"),
            P("dp", "tensor"),
            P("tensor", "dp"),
            P("tensor", "dp"),
            P("tensor", "dp"),
            P("tensor", None),
            P("tensor", None),
            P("tensor", None),
            P(),
            P(),
            P(),
        ),
        check_vma=False,
    )
```
